128 devices in a mesh: row: 16 (over y_lo, x, core), col: 8 (over z, y_hi).
Axes of the slice: x: 4, y: 4 (y_hi: 2, y_lo: 2; y = y_hi * 2 + y_lo), z: 4, core: 2. Of those that a mesh axis runs over, the one named last changes fastest.
Arguments:
- object_field: float32 [4, 2, 2048, 4096], P(None, None, 'row', 'col'), may hold values from -4 to 4
- probe_field: float32 [2, 128, 128], replicated, may hold values from -6 to 6
- propagator_phase: float32 [128, 128], replicated, may hold values from -3.140625 to 3.140625
- position_rows: int32 [16, 8, 4], P('row', 'col'), may hold values from 0 to 128
- position_cols: int32 [16, 8, 4], P('row', 'col'), may hold values from 0 to 512
- tile_counts: int32 [16, 8], P('row', 'col'), may hold values from 0 to 4, as said below
- intensities: float32 [16, 8, 4, 128, 128], P('row', 'col'), may hold values from 0.2 to 8
- conv_weight: float32 [3, 9, 32, 4], replicated, may hold values from -1 to 1
- conv_bias: float32 [3, 32], replicated, may hold values from -3 to 3
- output_weight: float32 [3, 4, 32], replicated, may hold values from -1 to 1
- output_bias: float32 [3, 4], replicated, may hold values from -2 to 2
Outputs:
- denoised: float32 [4, 2, 2048, 4096], P(None, None, 'row', 'col')
The draws below stay inside these ranges and needn't reach their ends.
Inputs may be any that keep to these rules, and one draw needn't show every extreme that they name: For every column of tiles and every r < 8, tiles r and r + 8 hold 4 positions together; a tile uses its first tile_counts slots of position_rows, position_cols and intensities.
All inputs are finite; a program needn't handle non-finite values.
Results may differ from the reference program's by a relative error of at most 0.0003.
Values sent between devices are 32-bit elements; how exact they have to be, the bound alone decides.
No kernel may reach another device: no remote copies, remote signals or barrier semaphores. Data moves between devices by JAX's collectives and lax.ppermute only.
A program may use at most 128 MiB of HBM per device.

```python
import math
import jax
import jax.numpy as jnp
from jax import lax

SLICES = 4
PROBE = 128
MARGIN = 64
TH = 128
TW = 512
P_MAX = 4
CH = 32
LAYERS = 3
TR = 16
TC = 8
NY = 2048
NX = 4096


def draw_tile_counts(key, part):
    half_rows = TR // 2
    key_counts = jax.random.fold_in(key, 11)
    key_row = jax.random.fold_in(key, 12)
    key_col = jax.random.fold_in(key, 13)
    upper_half = jax.random.randint(key_counts, (half_rows, TC), 0, P_MAX + 1)
    chosen_row = jax.random.randint(key_row, (), 0, half_rows)
    chosen_col = jax.random.randint(key_col, (), 0, TC)
    grid_rows = lax.broadcasted_iota(jnp.int32, (half_rows, TC), 0)
    grid_cols = lax.broadcasted_iota(jnp.int32, (half_rows, TC), 1)
    upper_half = jnp.where((grid_rows == chosen_row) & (grid_cols == chosen_col), P_MAX, upper_half)
    return jnp.concatenate([upper_half, P_MAX - upper_half], axis=0).astype(jnp.int32)


def set_ends(array, rng, least, high):
    shape = array.shape
    place = [jax.random.randint(jax.random.fold_in(rng, axis), (), 0, shape[axis]) for axis in range(len(shape))]
    array = array.at[tuple(place)].set(least)
    longest = shape.index(max(shape))
    place[longest] = (place[longest] + 1) % shape[longest]
    return array.at[tuple(place)].set(high)


def levels(own_key, dims, pieces, low, high):
    def one(axis_at, parts):
        draws = jax.random.uniform(jax.random.fold_in(jax.random.fold_in(own_key, 6), axis_at), (parts,), jnp.float32, low / len(pieces), high / len(pieces))
        return jnp.repeat(jnp.exp(draws), dims[axis_at] // parts).reshape((-1,) + (1,) * (len(dims) - axis_at - 1))

    loudness = one(*pieces[0])
    for cut in pieces[1:]:
        loudness = loudness * one(*cut)
    return loudness


def bell_draw(key, shape, spread, reach, shards=(), held_as=jnp.bfloat16):
    array = spread * jax.random.normal(key, shape, jnp.float32)
    if shards:
        array = array * levels(key, shape, shards, -0.22, 0.18)
    return jnp.clip(array, -reach, reach).astype(held_as)


def setup_inputs(seed: int = 0) -> dict:
    key_list = jax.random.split(jax.random.key(seed), 12)
    return {
        "object_field": bell_draw(key_list[0], (SLICES, 2, NY, NX), 0.7, 4.0, ((2, 16), (3, 8)), jnp.float32),
        "probe_field": bell_draw(key_list[1], (2, PROBE, PROBE), 1.0, 6.0, (), jnp.float32),
        "propagator_phase": jnp.clip(jax.random.uniform(key_list[2], (PROBE, PROBE), jnp.float32, -3.140625, 3.140625), -3.140625, 3.140625),
        "position_rows": set_ends(jax.random.randint(key_list[3], (TR, TC, P_MAX), 0, TH + 1), jax.random.fold_in(key_list[3], 1), 0, TH).astype(jnp.int32),
        "position_cols": set_ends(jax.random.randint(key_list[4], (TR, TC, P_MAX), 0, TW + 1), jax.random.fold_in(key_list[4], 1), 0, TW).astype(jnp.int32),
        "tile_counts": draw_tile_counts(jax.random.fold_in(key_list[11], 71), 0),
        "intensities": jnp.clip(jnp.exp(math.log(8.0) - 3.6888794 * jax.random.uniform(key_list[6], (TR, TC, P_MAX, PROBE, PROBE), jnp.float32) ** levels(key_list[6], (TR, TC, P_MAX, PROBE, PROBE), ((0, 16), (1, 8)), -0.2, 0.2)), 0.2, 8.0),
        "conv_weight": bell_draw(key_list[7], (LAYERS, 9, CH, SLICES), (9 * SLICES) ** -0.5, 1.0, (), jnp.float32),
        "conv_bias": bell_draw(key_list[8], (LAYERS, CH), 0.5, 3.0, (), jnp.float32),
        "output_weight": bell_draw(key_list[9], (LAYERS, SLICES, CH), CH ** -0.5, 1.0, (), jnp.float32),
        "output_bias": bell_draw(key_list[10], (LAYERS, SLICES), 0.3, 2.0, (), jnp.float32),
    }


step_size = 0.02

def dft_tables(length):
    index = jnp.arange(length, dtype=jnp.int32)
    product = index[:, None] * index[None, :] % length
    angle = 2.0 * jnp.pi / length * product.astype(jnp.float32)
    scale_factor = 1.0 / jnp.sqrt(jnp.float32(length))
    return (jnp.cos(angle) * scale_factor, jnp.sin(angle) * scale_factor)

def matmul(left, right):
    return jnp.dot(left, right, precision=lax.Precision.HIGHEST)

def transform(real_part, imag_part, cosine, sine, direction):
    left_re = matmul(cosine, real_part) + direction * matmul(sine, imag_part)
    left_im = matmul(cosine, imag_part) - direction * matmul(sine, real_part)
    out_re = matmul(left_re, cosine) + direction * matmul(left_im, sine)
    out_im = matmul(left_im, cosine) - direction * matmul(left_re, sine)
    return (out_re, out_im)

def slot_loss(patch, measured, probe_field, phase_re, phase_im, cosine, sine):
    wave_re = probe_field[0]
    wave_im = probe_field[1]
    slices = patch.shape[0]
    for slice_index in range(slices):
        obj_re = patch[slice_index, 0]
        obj_im = patch[slice_index, 1]
        wave_re, wave_im = (wave_re * obj_re - wave_im * obj_im, wave_re * obj_im + wave_im * obj_re)
        if slice_index + 1 < slices:
            spec_re, spec_im = transform(wave_re, wave_im, cosine, sine, 1.0)
            spec_re, spec_im = (spec_re * phase_re - spec_im * phase_im, spec_re * phase_im + spec_im * phase_re)
            wave_re, wave_im = transform(spec_re, spec_im, cosine, sine, -1.0)
    far_re, far_im = transform(wave_re, wave_im, cosine, sine, 1.0)
    mismatch = far_re * far_re + far_im * far_im - measured
    return 0.5 * jnp.sum(mismatch * mismatch)

def batched_gradient(patches, measured, probe_field, phase_re, phase_im, cosine, sine):
    mapped = jax.vmap(jax.grad(slot_loss), in_axes=(0, 0, None, None, None, None, None))
    return mapped(patches, measured, probe_field, phase_re, phase_im, cosine, sine)

def coupling_term(cond_pad, kernel, hidden_bias, out_map, out_bias):
    extent_rows = cond_pad.shape[1] - 2
    extent_cols = cond_pad.shape[2] - 2
    tap_list = [cond_pad[:, shift_row:shift_row + extent_rows, shift_col:shift_col + extent_cols] for shift_row in range(3) for shift_col in range(3)]
    stacked = jnp.concatenate(tap_list, axis=0)
    flat_kernel = jnp.transpose(kernel, (1, 0, 2)).reshape(kernel.shape[1], -1)
    hidden = jnp.einsum('ok,khw->ohw', flat_kernel, stacked, precision=lax.Precision.HIGHEST) + hidden_bias[:, None, None]
    hidden = jax.nn.silu(hidden)
    return jnp.einsum('co,ohw->chw', out_map, hidden, precision=lax.Precision.HIGHEST) + out_bias[:, None, None]

def reference(object_field, probe_field, propagator_phase, position_rows, position_cols, tile_counts, intensities, conv_weight, conv_bias, output_weight, output_bias):
    cosine, sine = dft_tables(PROBE)
    phase_re = jnp.cos(propagator_phase)
    phase_im = jnp.sin(propagator_phase)
    padded = jnp.pad(object_field, ((0, 0), (0, 0), (MARGIN, MARGIN), (MARGIN, MARGIN)))
    zero_index = jnp.int32(0)

    def tile_step(total, tile_id):
        tile_row = tile_id // TC
        tile_col = tile_id % TC
        rows_here = position_rows[tile_row, tile_col].astype(jnp.int32)
        cols_here = position_cols[tile_row, tile_col].astype(jnp.int32)
        count_here = tile_counts[tile_row, tile_col]
        measured = intensities[tile_row, tile_col]
        base_row = (tile_row * TH).astype(jnp.int32)
        base_col = (tile_col * TW).astype(jnp.int32)

        def cut_patch(row_offset, col_offset):
            return lax.dynamic_slice(padded, (zero_index, zero_index, base_row + row_offset, base_col + col_offset), (SLICES, 2, PROBE, PROBE))
        patches = jax.vmap(cut_patch)(rows_here, cols_here)
        grads = batched_gradient(patches, measured, probe_field, phase_re, phase_im, cosine, sine)
        alive = jnp.arange(P_MAX, dtype=jnp.int32) < count_here
        grads = jnp.where(alive[:, None, None, None, None], grads, 0.0)

        def add_slot(slot, accum):
            start = (zero_index, zero_index, base_row + rows_here[slot], base_col + cols_here[slot])
            current = lax.dynamic_slice(accum, start, (SLICES, 2, PROBE, PROBE))
            return lax.dynamic_update_slice(accum, current + grads[slot], start)
        return (lax.fori_loop(0, P_MAX, add_slot, total), None)
    total, _ = lax.scan(tile_step, jnp.zeros_like(padded), jnp.arange(TR * TC, dtype=jnp.int32))
    gradient = total[:, :, MARGIN:MARGIN + NY, MARGIN:MARGIN + NX]
    updated = object_field - step_size * gradient
    channels = updated.reshape(2 * SLICES, NY, NX)
    lower = channels[:SLICES]
    upper = channels[SLICES:]
    for layer_index in range(LAYERS):
        cond = lower if layer_index % 2 == 0 else upper
        cond_pad = jnp.pad(cond, ((0, 0), (1, 1), (1, 1)))

        def band_term(band_index):
            piece = lax.dynamic_slice(cond_pad, (zero_index, band_index * TH, zero_index), (SLICES, TH + 2, NX + 2))
            return coupling_term(piece, conv_weight[layer_index], conv_bias[layer_index], output_weight[layer_index], output_bias[layer_index])
        term = lax.map(band_term, jnp.arange(TR, dtype=jnp.int32))
        term = jnp.transpose(term, (1, 0, 2, 3)).reshape(SLICES, NY, NX)
        if layer_index % 2 == 0:
            upper = upper + term
        else:
            lower = lower + term
    return jnp.concatenate([lower, upper], axis=0).reshape(SLICES, 2, NY, NX)
```

```python
import functools

import jax
import jax.numpy as jnp
import numpy as np
from jax import lax
from jax.experimental import pallas as pl
from jax.experimental.pallas import tpu as pltpu
from jax.sharding import PartitionSpec as P

step_size = 0.02
LANE = 128
HALF = 64
STRIP = 72
BAND = 144
TILES = 5
ROWS_KEPT = 140
KDX = 48
KTOT = 448

f32 = jnp.float32
bf16 = jnp.bfloat16


def params(mib):
    return pltpu.CompilerParams(vmem_limit_bytes=mib << 20)


def vmem():
    return pl.BlockSpec(memory_space=pltpu.VMEM)


def smem():
    return pl.BlockSpec(memory_space=pltpu.SMEM)


def lanes_of(shape):
    return lax.broadcasted_iota(jnp.int32, shape, len(shape) - 1)


def split(value):
    high = value.astype(bf16)
    low = (value - high.astype(f32)).astype(bf16)
    return high, low


def halves_swapped(value):
    return pltpu.roll(value, HALF, value.ndim - 1)


def pack_kernel(obj_ref, ce_ref, co_ref, ev_ref, od_ref):
    row_odd = lax.axis_index("row") % 2
    col_odd = lax.axis_index("col") % 2
    first = lanes_of((HALF, LANE)) < HALF
    ev_start = pl.multiple_of((1 - row_odd) * HALF, HALF)
    od_start = pl.multiple_of(row_odd * HALF, HALF)
    for c in range(8):
        left = obj_ref[c, :, 0:LANE]
        right = obj_ref[c, :, 3 * LANE : 4 * LANE]
        to_left = jnp.where(first, left[:HALF], halves_swapped(left[HALF:]))
        to_right = jnp.where(first, halves_swapped(right[HALF:]), right[:HALF])
        ce_ref[c] = jnp.where(col_odd == 1, to_left, to_right)
        co_ref[c] = jnp.where(col_odd == 1, to_right, to_left)
        for t in range(4):
            ev_ref[t, c] = obj_ref[c, pl.ds(ev_start, HALF), t * LANE : (t + 1) * LANE]
            od_ref[t, c] = obj_ref[c, pl.ds(od_start, HALF), t * LANE : (t + 1) * LANE]


def comb_kernel(ce_ref, co_ref, comb_ref, ev_ref, od_ref):
    row_odd = lax.axis_index("row") % 2
    col_odd = lax.axis_index("col") % 2
    first = lanes_of((HALF, LANE)) < HALF
    for c in range(8):
        ce = ce_ref[c]
        co = co_ref[c]
        from_right = jnp.where(col_odd == 1, co, ce)
        from_left = jnp.where(col_odd == 1, ce, co)
        top = jnp.where(first, from_right, from_left)
        bottom = halves_swapped(jnp.where(first, from_left, from_right))
        comb_ref[c, :HALF] = top
        comb_ref[c, HALF:] = bottom
        ev_ref[c] = jnp.where(row_odd == 1, top, bottom)
        od_ref[c] = jnp.where(row_odd == 1, bottom, top)


def slots_kernel(
    rows_ref,
    cols_ref,
    count_ref,
    obj_ref,
    comb_ref,
    evm_ref,
    odm_ref,
    evc_ref,
    odc_ref,
    meas_ref,
    probe_ref,
    phase_re_ref,
    phase_im_ref,
    left_f_ref,
    left_b_ref,
    right_f_ref,
    right_b_ref,
    u_ref,
    out_evm,
    out_odm,
    out_evc,
    out_odc,
    own_ref,
    frame,
    accum,
    win,
    waves,
    extra,
    sems,
):
    row_odd = lax.axis_index("row") % 2
    ev_at = pl.multiple_of((1 - row_odd) * 192, HALF)
    od_at = pl.multiple_of(row_odd * 192, HALF)
    copies = []
    for t in range(4):
        copies.append((obj_ref.at[:, :, t * LANE : (t + 1) * LANE], frame.at[t, :, HALF:192, :]))
    copies.append((comb_ref, frame.at[4, :, HALF:192, :]))
    copies.append((evm_ref, frame.at[0:4, :, pl.ds(ev_at, HALF), :]))
    copies.append((odm_ref, frame.at[0:4, :, pl.ds(od_at, HALF), :]))
    copies.append((evc_ref, frame.at[4, :, pl.ds(ev_at, HALF), :]))
    copies.append((odc_ref, frame.at[4, :, pl.ds(od_at, HALF), :]))
    started = [pltpu.make_async_copy(src, dst, sems.at[i]) for i, (src, dst) in enumerate(copies)]
    for item in started:
        item.start()
    accum[...] = jnp.zeros(accum.shape, f32)
    for item in started:
        item.wait()

    lane = lanes_of((LANE, LANE))
    spots = []
    for k in range(4):
        row = rows_ref[k]
        at = lax.rem(cols_ref[k] + (640 - HALF), 640)
        q = at // LANE
        s = at - q * LANE
        nxt = jnp.where(q == 4, 0, q + 1)
        spots.append((row, q, nxt, s))

    for k in range(4):
        row, q, nxt, s = spots[k]
        keep = lane >= s
        turn = jnp.where(s == 0, 0, LANE - s)

        def take(c, carry, k=k, row=row, q=q, nxt=nxt, keep=keep, turn=turn):
            here = frame[q, c, pl.ds(row, LANE), :]
            beyond = frame[nxt, c, pl.ds(row, LANE), :]
            win[c // 2, k, c % 2] = pltpu.roll(jnp.where(keep, here, beyond), turn, 1)
            return carry

        lax.fori_loop(0, 8, take, 0)

    h_re = phase_re_ref[...]
    h_im = phase_im_ref[...]

    def left(xs, mat_ref):
        stack = jnp.concatenate([jnp.concatenate([re, im], axis=0) for re, im in xs], axis=1)
        high, low = split(stack)
        out = jnp.dot(
            mat_ref[...], jnp.concatenate([high, low, high], axis=0), preferred_element_type=f32
        )
        return [
            (out[:LANE, k * LANE : (k + 1) * LANE], out[LANE:, k * LANE : (k + 1) * LANE])
            for k in range(4)
        ]

    def right(xs, mat_ref):
        stack = jnp.concatenate([jnp.concatenate([re, im], axis=1) for re, im in xs], axis=0)
        high, low = split(stack)
        out = jnp.dot(
            jnp.concatenate([high, low, high], axis=1), mat_ref[...], preferred_element_type=f32
        )
        return [
            (out[k * LANE : (k + 1) * LANE, :LANE], out[k * LANE : (k + 1) * LANE, LANE:])
            for k in range(4)
        ]

    def forth(xs):
        return right(left(xs, left_f_ref), right_f_ref)

    def back(xs):
        return left(right(xs, right_b_ref), left_b_ref)

    def times(xs, re, im):
        return [(a * re - b * im, a * im + b * re) for a, b in xs]

    for k in range(4):
        waves[0, k, 0] = probe_ref[0]
        waves[0, k, 1] = probe_ref[1]

    def exit_wave(s):
        xs = []
        for k in range(4):
            p_re, p_im = waves[s, k, 0], waves[s, k, 1]
            o_re, o_im = win[s, k, 0], win[s, k, 1]
            xs.append((p_re * o_re - p_im * o_im, p_re * o_im + p_im * o_re))
        return xs

    def forward(s, carry):
        xs = back(times(forth(exit_wave(s)), h_re, h_im))
        for k in range(4):
            waves[s + 1, k, 0] = xs[k][0]
            waves[s + 1, k, 1] = xs[k][1]
        return carry

    lax.fori_loop(0, 3, forward, 0)
    far = forth(exit_wave(3))
    count = count_ref[0]
    seeds = []
    for k in range(4):
        re, im = far[k]
        factor = (re * re + im * im - meas_ref[k]) * (-2.0 * step_size)
        factor = jnp.where(k < count, factor, 0.0)
        seeds.append((factor * re, factor * im))
    gs = back(seeds)
    grad = waves
    for k in range(4):
        grad[4, k, 0] = gs[k][0]
        grad[4, k, 1] = gs[k][1]

    def through(s):
        xs = []
        for k in range(4):
            g_re, g_im = waves[4, k, 0], waves[4, k, 1]
            p_re, p_im = waves[s, k, 0], waves[s, k, 1]
            o_re, o_im = win[s, k, 0], win[s, k, 1]
            win[s, k, 0] = p_re * g_re + p_im * g_im
            win[s, k, 1] = p_re * g_im - p_im * g_re
            xs.append((o_re * g_re + o_im * g_im, o_re * g_im - o_im * g_re))
        return xs

    def backward(i, carry):
        xs = back(times(forth(through(3 - i)), h_re, -h_im))
        for k in range(4):
            waves[4, k, 0] = xs[k][0]
            waves[4, k, 1] = xs[k][1]
        return carry

    lax.fori_loop(0, 3, backward, 0)
    for k in range(4):
        g_re, g_im = waves[4, k, 0], waves[4, k, 1]
        p_re, p_im = probe_ref[0], probe_ref[1]
        win[0, k, 0] = p_re * g_re + p_im * g_im
        win[0, k, 1] = p_re * g_im - p_im * g_re

    for k in range(4):
        row, q, nxt, s = spots[k]
        keep = lane >= s

        def give(c, carry, k=k, row=row, q=q, nxt=nxt, keep=keep, s=s):
            turned = pltpu.roll(win[c // 2, k, c % 2], s, 1)
            here = accum[q, c, pl.ds(row, LANE), :]
            accum[q, c, pl.ds(row, LANE), :] = here + jnp.where(keep, turned, 0.0)
            beyond = accum[nxt, c, pl.ds(row, LANE), :]
            accum[nxt, c, pl.ds(row, LANE), :] = beyond + jnp.where(keep, 0.0, turned)
            return carry

        lax.fori_loop(0, 8, give, 0)

    wide = lanes_of((256, LANE)) // 8
    gathered = jnp.zeros((256, LANE), f32)
    for c in range(8):
        tail = pltpu.roll(accum[3, c], (8 * c + 8) % LANE, 1)
        head = pltpu.roll(accum[0, c], HALF + 8 * c, 1)
        gathered = jnp.where(wide == c, tail, gathered)
        gathered = jnp.where(wide == 8 + c, head, gathered)
    extra[...] = gathered

    ev_from = pl.multiple_of((1 - row_odd) * 184, 8)
    od_from = pl.multiple_of(row_odd * 184, 8)
    for t in range(4):
        out_evm[t] = accum[t, :, pl.ds(ev_from, STRIP), :]
        out_odm[t] = accum[t, :, pl.ds(od_from, STRIP), :]
    out_evc[0:8] = accum[4, :, pl.ds(ev_from, STRIP), :]
    out_odc[0:8] = accum[4, :, pl.ds(od_from, STRIP), :]
    out_evc[8] = extra[pl.ds(ev_from, STRIP), :]
    out_odc[8] = extra[pl.ds(od_from, STRIP), :]
    own_ref[0:8] = accum[4, :, 56:200, :]
    own_ref[8] = extra[56:200, :]
    for t in range(TILES):
        u_ref[t] = frame[t, :, 56:200, :] + accum[t, :, 56:200, :]


def sides_kernel(own_ref, evc_ref, odc_ref, ce_ref, co_ref):
    row_odd = lax.axis_index("row") % 2
    col_odd = lax.axis_index("col") % 2
    first = lanes_of((STRIP, LANE)) < HALF
    for c in range(9):
        ev = evc_ref[c]
        od = odc_ref[c]
        top = own_ref[c, :STRIP] + jnp.where(row_odd == 1, ev, od)
        bottom = halves_swapped(own_ref[c, STRIP:] + jnp.where(row_odd == 1, od, ev))
        to_right = jnp.where(first, top, bottom)
        to_left = jnp.where(first, bottom, top)
        ce_ref[c] = jnp.where(col_odd == 1, to_left, to_right)
        co_ref[c] = jnp.where(col_odd == 1, to_right, to_left)


def denoise_kernel(
    u_ref,
    evm_ref,
    odm_ref,
    evc_ref,
    odc_ref,
    ce_ref,
    co_ref,
    conv_ref,
    map_ref,
    bias_ref,
    out_ref,
    low_st,
    up_st,
    cond_st,
    conv_sc,
    map_sc,
):
    row_id = lax.axis_index("row")
    col_id = lax.axis_index("col")
    row_odd = row_id % 2
    col_odd = col_id % 2
    lane = lanes_of((STRIP, LANE))
    first = lane < HALF

    for layer in range(3):
        high, low = split(conv_ref[layer])
        place = lanes_of(high.shape)
        use_low = ((place >= 288) & (place < 432)) | (place == 433)
        conv_sc[layer] = jnp.where(use_low, low.astype(f32), high.astype(f32)).astype(bf16)
        high, low = split(map_ref[layer])
        map_sc[layer, 0:32] = high
        map_sc[layer, 32:64] = low

    def combine(t, c):
        top = u_ref[t, c, :STRIP]
        bottom = u_ref[t, c, STRIP:]
        ev = evc_ref[c] if t == 4 else evm_ref[t, c]
        od = odc_ref[c] if t == 4 else odm_ref[t, c]
        top = top + jnp.where(row_odd == 1, ev, od)
        bottom = bottom + jnp.where(row_odd == 1, od, ev)
        if t in (0, 3):
            ce = ce_ref[c]
            co = co_ref[c]
            if t == 0:
                side = jnp.where(col_odd == 1, ce, co)
                top = top + jnp.where(first, side, 0.0)
                bottom = bottom + jnp.where(first, halves_swapped(side), 0.0)
            else:
                side = jnp.where(col_odd == 1, co, ce)
                top = top + jnp.where(first, 0.0, side)
                bottom = bottom + jnp.where(first, 0.0, halves_swapped(side))
        if t == 4:
            ce = ce_ref[8]
            co = co_ref[8]
            from_left = jnp.where(col_odd == 1, ce, co)
            from_right = jnp.where(col_odd == 1, co, ce)
            tail_top = pltpu.roll(from_left, (120 - 8 * c) % LANE, 1)
            tail_bottom = pltpu.roll(from_left, (HALF + 120 - 8 * c) % LANE, 1)
            head_top = pltpu.roll(from_right, (HALF - 8 * c) % LANE, 1)
            head_bottom = pltpu.roll(from_right, (LANE - 8 * c) % LANE, 1)
            at_tail = lane >= 120
            at_head = lane < 8
            top = top + jnp.where(at_tail, tail_top, jnp.where(at_head, head_top, 0.0))
            bottom = bottom + jnp.where(at_tail, tail_bottom, jnp.where(at_head, head_bottom, 0.0))
        return jnp.concatenate([top, bottom], axis=0)

    for t in range(TILES):
        for c in range(4):
            low_st[t, pl.ds(c, ROWS_KEPT, stride=4), :] = combine(t, c)[3:143]
            up_st[t, pl.ds(c, ROWS_KEPT, stride=4), :] = combine(t, 4 + c)[4:144]

    last_row = lax.axis_size("row") - 1
    last_col = lax.axis_size("col") - 1
    col_from = jnp.where(col_id == 0, 128, 640)
    right_off = jnp.where(col_id == last_col, 512, 576)
    left_off = jnp.where(col_id == 0, 640, 576)
    del col_from

    def prepare(store, first_row):
        row_low = jnp.where(row_id == 0, -first_row * 4, 0)
        row_high = jnp.where(row_id == last_row, (128 - first_row) * 4, 4 * ROWS_KEPT)

        def body(i, carry):
            at = pl.multiple_of(i * 16, 16)
            x = jnp.concatenate([store[t, pl.ds(at, 16), :] for t in range(TILES)], axis=1)
            column = lax.broadcasted_iota(jnp.int32, x.shape, 1)
            index = lax.broadcasted_iota(jnp.int32, x.shape, 0) + at
            inside = (index >= row_low) & (index < row_high)
            inside = inside & ((column < right_off) | (column >= left_off))
            x = jnp.where(inside, x, 0.0)
            for dx in range(3):
                y = x if dx == 1 else pltpu.roll(x, 1 if dx == 0 else 639, 1)
                high, low = split(y)
                cond_st[0, dx, pl.ds(at, 16), :] = high
                cond_st[1, dx, pl.ds(at, 16), :] = low
            return carry

        lax.fori_loop(0, 4 * ROWS_KEPT // 16, body, 0)

    ones = {w: jnp.ones((16, w), bf16) for w in (LANE, 2 * LANE)}

    def layer_pass(layer, groups, read_at, store, write_at, chunks):
        weights = conv_sc[layer]
        both = map_sc[layer]
        single = map_sc[layer, 0:32]
        bias = bias_ref[layer]

        def body(g, carry):
            src = pl.multiple_of(read_at + g * 32, 16)
            dst = pl.multiple_of(write_at + g * 32, 8)
            for begin, width in chunks:
                pieces = [cond_st[part, dx, pl.ds(src, KDX), begin : begin + width] for part in (0, 1) for dx in range(3)]
                pieces = pieces + pieces[:3] + [ones[width]]
                half = jnp.dot(weights, jnp.concatenate(pieces, axis=0), preferred_element_type=f32)
                hidden = half + half * jnp.tanh(half)
                high, low = split(hidden)
                out = jnp.dot(both, high, preferred_element_type=f32)
                term = out[:32] + out[32:] + jnp.dot(single, low, preferred_element_type=f32)
                for j in range(width // LANE):
                    t = begin // LANE + j
                    bit = term[:, j * LANE : (j + 1) * LANE]
                    store[t, pl.ds(dst, 32), :] = store[t, pl.ds(dst, 32), :] + (bit + bias)
            return carry

        lax.fori_loop(0, groups, body, 0)

    wide = ((0, 256), (256, 256), (512, 128))
    prepare(low_st, -5)
    layer_pass(0, 17, 0, up_st, 8, wide)
    prepare(up_st, -4)
    layer_pass(1, 17, 0, low_st, 16, wide)
    prepare(low_st, -5)
    layer_pass(2, 16, 16, up_st, 16, wide[:2])
    for t in range(4):
        for c in range(4):
            out_ref[c, :, t * LANE : (t + 1) * LANE] = low_st[t, pl.ds(20 + c, 128, stride=4), :]
            out_ref[4 + c, :, t * LANE : (t + 1) * LANE] = up_st[t, pl.ds(16 + c, 128, stride=4), :]


def dft_matrices():
    index = np.arange(LANE)
    angle = 2.0 * np.pi / LANE * (np.outer(index, index) % LANE)
    c = np.cos(angle) / np.sqrt(LANE)
    s = np.sin(angle) / np.sqrt(LANE)
    a = np.block([[c, s], [-s, c]]).astype(np.float32)
    b = np.block([[c, -s], [s, c]]).astype(np.float32)

    def parts(m):
        high = m.astype(jnp.bfloat16)
        low = (m - high.astype(np.float32)).astype(jnp.bfloat16)
        return high, low

    (ah, al), (bh, bl) = parts(a), parts(b)
    left_f = np.concatenate([ah, ah, al], axis=1)
    left_b = np.concatenate([bh, bh, bl], axis=1)
    right_f = np.concatenate([bh, bh, bl], axis=0)
    right_b = np.concatenate([ah, ah, al], axis=0)
    return left_f, left_b, right_f, right_b


def conv_matrices(conv_weight, conv_bias, output_weight, output_bias):
    layers = conv_weight.shape[0]
    w = conv_weight.reshape(layers, 3, 3, 32, 4) * 0.5
    blocks = []
    for layer, start in zip(range(layers), (2, 2, 0)):
        hot = np.zeros((8, 3, 12), np.float32)
        for j in range(8):
            for dy in range(3):
                hot[j, dy, j + dy + start] = 1.0
        m = sum(hot[:, dy][:, None, None, :, None] * jnp.transpose(w[layer, dy], (1, 0, 2))[None, :, :, None, :] for dy in range(3))
        blocks.append(m.reshape(256, 144))
    main = jnp.stack(blocks)
    bias = jnp.tile(conv_bias * 0.5, (1, 8))[:, :, None]
    packed = jnp.concatenate([main, main, main, bias, bias, jnp.zeros((layers, 256, 14), f32)], axis=2)
    eye = np.eye(8, dtype=np.float32)
    maps = (eye[None, :, None, :, None] * output_weight[:, None, :, None, :]).reshape(layers, 32, 256)
    out_bias = jnp.broadcast_to(jnp.tile(output_bias, (1, 8))[:, :, None], (layers, 32, LANE))
    return packed, maps, out_bias


def sds(*shape):
    return jax.ShapeDtypeStruct(shape, f32)


def per_device(
    object_field,
    probe_field,
    propagator_phase,
    position_rows,
    position_cols,
    tile_counts,
    intensities,
    conv_weight,
    conv_bias,
    output_weight,
    output_bias,
):
    rows = lax.axis_size("row")
    cols = lax.axis_size("col")

    def pairs(count, start):
        found = []
        for i in range(start, count - 1, 2):
            found += [(i, i + 1), (i + 1, i)]
        return found

    def row_ev(x):
        return lax.ppermute(x, "row", pairs(rows, 0))

    def row_od(x):
        return lax.ppermute(x, "row", pairs(rows, 1))

    def col_ev(x):
        return lax.ppermute(x, "col", pairs(cols, 0))

    def col_od(x):
        return lax.ppermute(x, "col", pairs(cols, 1))

    obj = object_field.reshape(8, 128, 512)
    ce, co, evm, odm = pl.pallas_call(
        pack_kernel,
        out_shape=[sds(8, HALF, LANE), sds(8, HALF, LANE), sds(4, 8, HALF, LANE), sds(4, 8, HALF, LANE)],
        in_specs=[vmem()],
        out_specs=[vmem()] * 4,
        compiler_params=params(32),
        name="pack",
    )(obj)
    odm = row_od(odm)
    ce = col_ev(ce)
    co = col_od(co)
    evm = row_ev(evm)
    comb, evc, odc = pl.pallas_call(
        comb_kernel,
        out_shape=[sds(8, 128, LANE), sds(8, HALF, LANE), sds(8, HALF, LANE)],
        in_specs=[vmem()] * 2,
        out_specs=[vmem()] * 3,
        compiler_params=params(32),
        name="comb",
    )(ce, co)
    odc = row_od(odc)
    evc = row_ev(evc)
    phase_re = jnp.cos(propagator_phase)
    phase_im = jnp.sin(propagator_phase)
    tables = [jnp.asarray(m) for m in dft_matrices()]
    anywhere = pl.BlockSpec(memory_space=pl.ANY)
    u, evm, odm, evc, odc, own = pl.pallas_call(
        slots_kernel,
        out_shape=[
            sds(TILES, 8, BAND, LANE),
            sds(4, 8, STRIP, LANE),
            sds(4, 8, STRIP, LANE),
            sds(9, STRIP, LANE),
            sds(9, STRIP, LANE),
            sds(9, BAND, LANE),
        ],
        in_specs=[smem()] * 3 + [anywhere] * 6 + [vmem()] * 8,
        out_specs=[vmem()] * 6,
        scratch_shapes=[
            pltpu.VMEM((TILES, 8, 256, LANE), f32),
            pltpu.VMEM((TILES, 8, 256, LANE), f32),
            pltpu.VMEM((4, 4, 2, LANE, LANE), f32),
            pltpu.VMEM((5, 4, 2, LANE, LANE), f32),
            pltpu.VMEM((256, LANE), f32),
            pltpu.SemaphoreType.DMA((9,)),
        ],
        compiler_params=params(56),
        name="slots",
    )(
        position_rows.reshape(-1),
        position_cols.reshape(-1),
        tile_counts.reshape(-1),
        obj,
        comb,
        evm,
        odm,
        evc,
        odc,
        intensities.reshape(4, LANE, LANE),
        probe_field,
        phase_re,
        phase_im,
        *tables,
    )
    odc = row_od(odc)
    evc = row_ev(evc)
    odm = row_od(odm)
    evm = row_ev(evm)
    ce, co = pl.pallas_call(
        sides_kernel,
        out_shape=[sds(9, STRIP, LANE)] * 2,
        in_specs=[vmem()] * 3,
        out_specs=[vmem()] * 2,
        compiler_params=params(32),
        name="sides",
    )(own, evc, odc)
    ce = col_ev(ce)
    co = col_od(co)
    packed, maps, out_bias = conv_matrices(conv_weight, conv_bias, output_weight, output_bias)
    out = pl.pallas_call(
        denoise_kernel,
        out_shape=sds(8, 128, 512),
        in_specs=[vmem()] * 10,
        out_specs=vmem(),
        scratch_shapes=[
            pltpu.VMEM((TILES, 4 * ROWS_KEPT, LANE), f32),
            pltpu.VMEM((TILES, 4 * ROWS_KEPT, LANE), f32),
            pltpu.VMEM((2, 3, 4 * ROWS_KEPT, 640), bf16),
            pltpu.VMEM((3, 256, KTOT), bf16),
            pltpu.VMEM((3, 64, 256), bf16),
        ],
        compiler_params=params(56),
        name="denoise",
    )(u, evm, odm, evc, odc, ce, co, packed, maps, out_bias)
    return out.reshape(4, 2, 128, 512)


def solution(mesh):
    placed = (
        P(None, None, "row", "col"),
        P(),
        P(),
        P("row", "col", None),
        P("row", "col", None),
        P("row", "col"),
        P("row", "col", None, None, None),
        P(),
        P(),
        P(),
        P(),
    )
    return jax.shard_map(
        per_device,
        mesh=mesh,
        in_specs=placed,
        out_specs=P(None, None, "row", "col"),
        check_vma=False,
    )
```

```python
import functools

import jax
import jax.numpy as jnp
import numpy as np
from jax import lax
from jax.experimental import pallas as pl
from jax.experimental.pallas import tpu as pltpu
from jax.sharding import PartitionSpec as P

step_size = 0.02
LANE = 128
HALF = 64
STRIP = 72
BAND = 144
TILES = 5
ROWS_KEPT = 140
KDX = 48
KTOT = 448

f32 = jnp.float32
bf16 = jnp.bfloat16


def params(mib):
    return pltpu.CompilerParams(vmem_limit_bytes=mib << 20)


def vmem():
    return pl.BlockSpec(memory_space=pltpu.VMEM)


def smem():
    return pl.BlockSpec(memory_space=pltpu.SMEM)


def lanes_of(shape):
    return lax.broadcasted_iota(jnp.int32, shape, len(shape) - 1)


def split(value):
    high = value.astype(bf16)
    low = (value - high.astype(f32)).astype(bf16)
    return high, low


def halves_swapped(value):
    return pltpu.roll(value, HALF, value.ndim - 1)


def pack_kernel(first_ref, last_ref, ce_ref, co_ref):
    col_odd = lax.axis_index("col") % 2
    first = lanes_of((HALF, LANE)) < HALF
    for c in range(8):
        left = first_ref[c]
        right = last_ref[c]
        to_left = jnp.where(first, left[:HALF], halves_swapped(left[HALF:]))
        to_right = jnp.where(first, halves_swapped(right[HALF:]), right[:HALF])
        ce_ref[c] = jnp.where(col_odd == 1, to_left, to_right)
        co_ref[c] = jnp.where(col_odd == 1, to_right, to_left)


def comb_kernel(obj_ref, ce_ref, co_ref, comb_ref, ev_ref, od_ref):
    row_odd = lax.axis_index("row") % 2
    col_odd = lax.axis_index("col") % 2
    first = lanes_of((HALF, LANE)) < HALF
    ev_start = pl.multiple_of((1 - row_odd) * HALF, HALF)
    od_start = pl.multiple_of(row_odd * HALF, HALF)
    for c in range(8):
        ce = ce_ref[c]
        co = co_ref[c]
        from_right = jnp.where(col_odd == 1, co, ce)
        from_left = jnp.where(col_odd == 1, ce, co)
        top = jnp.where(first, from_right, from_left)
        bottom = halves_swapped(jnp.where(first, from_left, from_right))
        comb_ref[c, :HALF] = top
        comb_ref[c, HALF:] = bottom
        ev_ref[4, c] = jnp.where(row_odd == 1, top, bottom)
        od_ref[4, c] = jnp.where(row_odd == 1, bottom, top)
        for t in range(4):
            ev_ref[t, c] = obj_ref[c, pl.ds(ev_start, HALF), t * LANE : (t + 1) * LANE]
            od_ref[t, c] = obj_ref[c, pl.ds(od_start, HALF), t * LANE : (t + 1) * LANE]


def slots_kernel(
    rows_ref,
    cols_ref,
    count_ref,
    obj_ref,
    comb_ref,
    ev_ref,
    od_ref,
    meas_ref,
    probe_ref,
    phase_re_ref,
    phase_im_ref,
    left_f_ref,
    left_b_ref,
    right_f_ref,
    right_b_ref,
    u_ref,
    out_ev,
    out_od,
    own_ref,
    frame,
    accum,
    win,
    waves,
    extra,
    sems,
):
    row_odd = lax.axis_index("row") % 2
    ev_at = pl.multiple_of((1 - row_odd) * 192, HALF)
    od_at = pl.multiple_of(row_odd * 192, HALF)
    copies = []
    for t in range(4):
        copies.append((obj_ref.at[:, :, t * LANE : (t + 1) * LANE], frame.at[t, :, HALF:192, :]))
    copies.append((comb_ref, frame.at[4, :, HALF:192, :]))
    copies.append((ev_ref, frame.at[:, :, pl.ds(ev_at, HALF), :]))
    copies.append((od_ref, frame.at[:, :, pl.ds(od_at, HALF), :]))
    started = [pltpu.make_async_copy(src, dst, sems.at[i]) for i, (src, dst) in enumerate(copies)]
    for item in started:
        item.start()
    accum[...] = jnp.zeros(accum.shape, f32)
    for item in started:
        item.wait()

    lane = lanes_of((LANE, LANE))
    spots = []
    for k in range(4):
        row = rows_ref[k]
        at = lax.rem(cols_ref[k] + (640 - HALF), 640)
        q = at // LANE
        s = at - q * LANE
        nxt = jnp.where(q == 4, 0, q + 1)
        spots.append((row, q, nxt, s))

    for k in range(4):
        row, q, nxt, s = spots[k]
        keep = lane >= s
        turn = jnp.where(s == 0, 0, LANE - s)

        def take(c, carry, k=k, row=row, q=q, nxt=nxt, keep=keep, turn=turn):
            here = frame[q, c, pl.ds(row, LANE), :]
            beyond = frame[nxt, c, pl.ds(row, LANE), :]
            win[c // 2, k, c % 2] = pltpu.roll(jnp.where(keep, here, beyond), turn, 1)
            return carry

        lax.fori_loop(0, 8, take, 0)

    h_re = phase_re_ref[...]
    h_im = phase_im_ref[...]

    def left(xs, mat_ref):
        stack = jnp.concatenate([jnp.concatenate([re, im], axis=0) for re, im in xs], axis=1)
        high, low = split(stack)
        out = jnp.dot(
            mat_ref[...], jnp.concatenate([high, low, high], axis=0), preferred_element_type=f32
        )
        return [
            (out[:LANE, k * LANE : (k + 1) * LANE], out[LANE:, k * LANE : (k + 1) * LANE])
            for k in range(4)
        ]

    def right(xs, mat_ref):
        stack = jnp.concatenate([jnp.concatenate([re, im], axis=1) for re, im in xs], axis=0)
        high, low = split(stack)
        out = jnp.dot(
            jnp.concatenate([high, low, high], axis=1), mat_ref[...], preferred_element_type=f32
        )
        return [
            (out[k * LANE : (k + 1) * LANE, :LANE], out[k * LANE : (k + 1) * LANE, LANE:])
            for k in range(4)
        ]

    def forth(xs):
        return right(left(xs, left_f_ref), right_f_ref)

    def back(xs):
        return left(right(xs, right_b_ref), left_b_ref)

    def times(xs, re, im):
        return [(a * re - b * im, a * im + b * re) for a, b in xs]

    for k in range(4):
        waves[0, k, 0] = probe_ref[0]
        waves[0, k, 1] = probe_ref[1]

    def exit_wave(s):
        xs = []
        for k in range(4):
            p_re, p_im = waves[s, k, 0], waves[s, k, 1]
            o_re, o_im = win[s, k, 0], win[s, k, 1]
            xs.append((p_re * o_re - p_im * o_im, p_re * o_im + p_im * o_re))
        return xs

    def forward(s, carry):
        xs = back(times(forth(exit_wave(s)), h_re, h_im))
        for k in range(4):
            waves[s + 1, k, 0] = xs[k][0]
            waves[s + 1, k, 1] = xs[k][1]
        return carry

    lax.fori_loop(0, 3, forward, 0)
    far = forth(exit_wave(3))
    count = count_ref[0]
    seeds = []
    for k in range(4):
        re, im = far[k]
        factor = (re * re + im * im - meas_ref[k]) * (-2.0 * step_size)
        factor = jnp.where(k < count, factor, 0.0)
        seeds.append((factor * re, factor * im))
    gs = back(seeds)
    grad = waves
    for k in range(4):
        grad[4, k, 0] = gs[k][0]
        grad[4, k, 1] = gs[k][1]

    def through(s):
        xs = []
        for k in range(4):
            g_re, g_im = waves[4, k, 0], waves[4, k, 1]
            p_re, p_im = waves[s, k, 0], waves[s, k, 1]
            o_re, o_im = win[s, k, 0], win[s, k, 1]
            win[s, k, 0] = p_re * g_re + p_im * g_im
            win[s, k, 1] = p_re * g_im - p_im * g_re
            xs.append((o_re * g_re + o_im * g_im, o_re * g_im - o_im * g_re))
        return xs

    def backward(i, carry):
        xs = back(times(forth(through(3 - i)), h_re, -h_im))
        for k in range(4):
            waves[4, k, 0] = xs[k][0]
            waves[4, k, 1] = xs[k][1]
        return carry

    lax.fori_loop(0, 3, backward, 0)
    for k in range(4):
        g_re, g_im = waves[4, k, 0], waves[4, k, 1]
        p_re, p_im = probe_ref[0], probe_ref[1]
        win[0, k, 0] = p_re * g_re + p_im * g_im
        win[0, k, 1] = p_re * g_im - p_im * g_re

    for k in range(4):
        row, q, nxt, s = spots[k]
        keep = lane >= s

        def give(c, carry, k=k, row=row, q=q, nxt=nxt, keep=keep, s=s):
            turned = pltpu.roll(win[c // 2, k, c % 2], s, 1)
            here = accum[q, c, pl.ds(row, LANE), :]
            accum[q, c, pl.ds(row, LANE), :] = here + jnp.where(keep, turned, 0.0)
            beyond = accum[nxt, c, pl.ds(row, LANE), :]
            accum[nxt, c, pl.ds(row, LANE), :] = beyond + jnp.where(keep, 0.0, turned)
            return carry

        lax.fori_loop(0, 8, give, 0)

    wide = lanes_of((256, LANE)) // 8
    gathered = jnp.zeros((256, LANE), f32)
    for c in range(8):
        tail = pltpu.roll(accum[3, c], (8 * c + 8) % LANE, 1)
        head = pltpu.roll(accum[0, c], HALF + 8 * c, 1)
        gathered = jnp.where(wide == c, tail, gathered)
        gathered = jnp.where(wide == 8 + c, head, gathered)
    extra[...] = gathered

    ev_from = pl.multiple_of((1 - row_odd) * 184, 8)
    od_from = pl.multiple_of(row_odd * 184, 8)
    for t in range(4):
        out_ev[9 + 8 * t : 17 + 8 * t] = accum[t, :, pl.ds(ev_from, STRIP), :]
        out_od[9 + 8 * t : 17 + 8 * t] = accum[t, :, pl.ds(od_from, STRIP), :]
    out_ev[0:8] = accum[4, :, pl.ds(ev_from, STRIP), :]
    out_od[0:8] = accum[4, :, pl.ds(od_from, STRIP), :]
    out_ev[8] = extra[pl.ds(ev_from, STRIP), :]
    out_od[8] = extra[pl.ds(od_from, STRIP), :]
    own_ref[0:8] = accum[4, :, 56:200, :]
    own_ref[8] = extra[56:200, :]
    for t in range(TILES):
        u_ref[t] = frame[t, :, 56:200, :] + accum[t, :, 56:200, :]


def sides_kernel(own_ref, evc_ref, odc_ref, ce_ref, co_ref):
    row_odd = lax.axis_index("row") % 2
    col_odd = lax.axis_index("col") % 2
    first = lanes_of((STRIP, LANE)) < HALF
    for c in range(9):
        ev = evc_ref[c]
        od = odc_ref[c]
        top = own_ref[c, :STRIP] + jnp.where(row_odd == 1, ev, od)
        bottom = halves_swapped(own_ref[c, STRIP:] + jnp.where(row_odd == 1, od, ev))
        to_right = jnp.where(first, top, bottom)
        to_left = jnp.where(first, bottom, top)
        ce_ref[c] = jnp.where(col_odd == 1, to_left, to_right)
        co_ref[c] = jnp.where(col_odd == 1, to_right, to_left)


def denoise_kernel(
    u_ref,
    ev_ref,
    od_ref,
    ce_ref,
    co_ref,
    conv_ref,
    map_ref,
    bias_ref,
    out_ref,
    low_st,
    up_st,
    cond_st,
    conv_sc,
    map_sc,
    half_sc,
):
    row_id = lax.axis_index("row")
    col_id = lax.axis_index("col")
    row_odd = row_id % 2
    col_odd = col_id % 2
    lane = lanes_of((STRIP, LANE))
    first = lane < HALF

    for layer in range(3):
        high, low = split(conv_ref[layer])
        place = lanes_of(high.shape)
        use_low = ((place >= 288) & (place < 432)) | (place == 433)
        conv_sc[layer] = jnp.where(use_low, low.astype(f32), high.astype(f32)).astype(bf16)
        high, low = split(map_ref[layer])
        map_sc[layer, 0:32] = high
        map_sc[layer, 32:64] = low

    def combine(t, c):
        top = u_ref[t, c, :STRIP]
        bottom = u_ref[t, c, STRIP:]
        plane = c if t == 4 else 9 + 8 * t + c
        ev = ev_ref[plane]
        od = od_ref[plane]
        top = top + jnp.where(row_odd == 1, ev, od)
        bottom = bottom + jnp.where(row_odd == 1, od, ev)
        if t in (0, 3):
            ce = ce_ref[c]
            co = co_ref[c]
            if t == 0:
                side = jnp.where(col_odd == 1, ce, co)
                top = top + jnp.where(first, side, 0.0)
                bottom = bottom + jnp.where(first, halves_swapped(side), 0.0)
            else:
                side = jnp.where(col_odd == 1, co, ce)
                top = top + jnp.where(first, 0.0, side)
                bottom = bottom + jnp.where(first, 0.0, halves_swapped(side))
        if t == 4:
            ce = ce_ref[8]
            co = co_ref[8]
            from_left = jnp.where(col_odd == 1, ce, co)
            from_right = jnp.where(col_odd == 1, co, ce)
            tail_top = pltpu.roll(from_left, (120 - 8 * c) % LANE, 1)
            tail_bottom = pltpu.roll(from_left, (HALF + 120 - 8 * c) % LANE, 1)
            head_top = pltpu.roll(from_right, (HALF - 8 * c) % LANE, 1)
            head_bottom = pltpu.roll(from_right, (LANE - 8 * c) % LANE, 1)
            at_tail = lane >= 120
            at_head = lane < 8
            top = top + jnp.where(at_tail, tail_top, jnp.where(at_head, head_top, 0.0))
            bottom = bottom + jnp.where(at_tail, tail_bottom, jnp.where(at_head, head_bottom, 0.0))
        return jnp.concatenate([top, bottom], axis=0)

    for t in range(TILES):
        for c in range(4):
            low_st[t, pl.ds(c, ROWS_KEPT, stride=4), :] = combine(t, c)[3:143]
            up_st[t, pl.ds(c, ROWS_KEPT, stride=4), :] = combine(t, 4 + c)[4:144]

    last_row = lax.axis_size("row") - 1
    last_col = lax.axis_size("col") - 1
    col_from = jnp.where(col_id == 0, 128, 640)
    right_off = jnp.where(col_id == last_col, 512, 576)
    left_off = jnp.where(col_id == 0, 640, 576)
    del col_from

    def prepare(store, first_row):
        row_low = jnp.where(row_id == 0, -first_row * 4, 0)
        row_high = jnp.where(row_id == last_row, (128 - first_row) * 4, 4 * ROWS_KEPT)

        def body(i, carry):
            at = pl.multiple_of(i * 16, 16)
            x = jnp.concatenate([store[t, pl.ds(at, 16), :] for t in range(TILES)], axis=1)
            column = lax.broadcasted_iota(jnp.int32, x.shape, 1)
            index = lax.broadcasted_iota(jnp.int32, x.shape, 0) + at
            inside = (index >= row_low) & (index < row_high)
            inside = inside & ((column < right_off) | (column >= left_off))
            x = jnp.where(inside, x, 0.0)
            for dx in range(3):
                y = x if dx == 1 else pltpu.roll(x, 1 if dx == 0 else 639, 1)
                high, low = split(y)
                cond_st[0, dx, pl.ds(at, 16), :] = high
                cond_st[1, dx, pl.ds(at, 16), :] = low
            return carry

        lax.fori_loop(0, 4 * ROWS_KEPT // 16, body, 0, unroll=5)

    ones = jnp.ones((16, 640), bf16)

    def layer_pass(layer, groups, read_at, store, write_at, width):
        bias = bias_ref[layer]

        def first_map(g, slot):
            src = pl.multiple_of(read_at + g * 32, 16)
            pieces = [cond_st[part, dx, pl.ds(src, KDX), :width] for part in (0, 1) for dx in range(3)]
            pieces = pieces + pieces[:3] + [ones[:, :width]]
            half_sc[slot, :, :width] = jnp.dot(
                conv_sc[layer], jnp.concatenate(pieces, axis=0), preferred_element_type=f32
            )

        def second_map(g, slot):
            dst = pl.multiple_of(write_at + g * 32, 8)
            half = half_sc[slot, :, :width]
            hidden = half + half * jnp.tanh(half)
            high, low = split(hidden)
            out = jnp.dot(map_sc[layer], high, preferred_element_type=f32)
            low_out = jnp.dot(map_sc[layer, 0:32], low, preferred_element_type=f32)
            term = out[:32] + out[32:] + low_out
            for t in range(width // LANE):
                bit = term[:, t * LANE : (t + 1) * LANE]
                store[t, pl.ds(dst, 32), :] = store[t, pl.ds(dst, 32), :] + (bit + bias)

        first_map(0, 0)
        pairs_whole = (groups - 1) // 2

        def body(i, carry):
            first_map(2 * i + 1, 1)
            second_map(2 * i, 0)
            first_map(2 * i + 2, 0)
            second_map(2 * i + 1, 1)
            return carry

        lax.fori_loop(0, pairs_whole, body, 0)
        done = 2 * pairs_whole
        if groups - done == 2:
            first_map(done + 1, 1)
            second_map(done, 0)
            second_map(done + 1, 1)
        else:
            second_map(done, 0)

    prepare(low_st, -5)
    layer_pass(0, 17, 0, up_st, 8, 640)
    prepare(up_st, -4)
    layer_pass(1, 17, 0, low_st, 16, 640)
    prepare(low_st, -5)
    layer_pass(2, 16, 16, up_st, 16, 512)
    for t in range(4):
        for c in range(4):
            out_ref[c, :, t * LANE : (t + 1) * LANE] = low_st[t, pl.ds(20 + c, 128, stride=4), :]
            out_ref[4 + c, :, t * LANE : (t + 1) * LANE] = up_st[t, pl.ds(16 + c, 128, stride=4), :]


def dft_matrices():
    index = np.arange(LANE)
    angle = 2.0 * np.pi / LANE * (np.outer(index, index) % LANE)
    c = np.cos(angle) / np.sqrt(LANE)
    s = np.sin(angle) / np.sqrt(LANE)
    a = np.block([[c, s], [-s, c]]).astype(np.float32)
    b = np.block([[c, -s], [s, c]]).astype(np.float32)

    def parts(m):
        high = m.astype(jnp.bfloat16)
        low = (m - high.astype(np.float32)).astype(jnp.bfloat16)
        return high, low

    (ah, al), (bh, bl) = parts(a), parts(b)
    left_f = np.concatenate([ah, ah, al], axis=1)
    left_b = np.concatenate([bh, bh, bl], axis=1)
    right_f = np.concatenate([bh, bh, bl], axis=0)
    right_b = np.concatenate([ah, ah, al], axis=0)
    return left_f, left_b, right_f, right_b


def conv_matrices(conv_weight, conv_bias, output_weight, output_bias):
    layers = conv_weight.shape[0]
    w = conv_weight.reshape(layers, 3, 3, 32, 4) * 0.5
    blocks = []
    for layer, start in zip(range(layers), (2, 2, 0)):
        hot = np.zeros((8, 3, 12), np.float32)
        for j in range(8):
            for dy in range(3):
                hot[j, dy, j + dy + start] = 1.0
        m = sum(hot[:, dy][:, None, None, :, None] * jnp.transpose(w[layer, dy], (1, 0, 2))[None, :, :, None, :] for dy in range(3))
        blocks.append(m.reshape(256, 144))
    main = jnp.stack(blocks)
    bias = jnp.tile(conv_bias * 0.5, (1, 8))[:, :, None]
    packed = jnp.concatenate([main, main, main, bias, bias, jnp.zeros((layers, 256, 14), f32)], axis=2)
    eye = np.eye(8, dtype=np.float32)
    maps = (eye[None, :, None, :, None] * output_weight[:, None, :, None, :]).reshape(layers, 32, 256)
    out_bias = jnp.broadcast_to(jnp.tile(output_bias, (1, 8))[:, :, None], (layers, 32, LANE))
    return packed, maps, out_bias


def sds(*shape):
    return jax.ShapeDtypeStruct(shape, f32)


def denoise_call(*operands):
    return pl.pallas_call(
        denoise_kernel,
        out_shape=sds(8, 128, 512),
        in_specs=[vmem()] * 8,
        out_specs=vmem(),
        scratch_shapes=[
            pltpu.VMEM((TILES, 4 * ROWS_KEPT, LANE), f32),
            pltpu.VMEM((TILES, 4 * ROWS_KEPT, LANE), f32),
            pltpu.VMEM((2, 3, 4 * ROWS_KEPT, 640), bf16),
            pltpu.VMEM((3, 256, KTOT), bf16),
            pltpu.VMEM((3, 64, 256), bf16),
            pltpu.VMEM((2, 256, 640), f32),
        ],
        compiler_params=params(56),
        name="denoise",
    )(*operands)


def per_device(
    object_field,
    probe_field,
    propagator_phase,
    position_rows,
    position_cols,
    tile_counts,
    intensities,
    conv_weight,
    conv_bias,
    output_weight,
    output_bias,
):
    rows = lax.axis_size("row")
    cols = lax.axis_size("col")

    def pairs(count, start):
        found = []
        for i in range(start, count - 1, 2):
            found += [(i, i + 1), (i + 1, i)]
        return found

    def row_ev(x):
        return lax.ppermute(x, "row", pairs(rows, 0))

    def row_od(x):
        return lax.ppermute(x, "row", pairs(rows, 1))

    def col_ev(x):
        return lax.ppermute(x, "col", pairs(cols, 0))

    def col_od(x):
        return lax.ppermute(x, "col", pairs(cols, 1))

    obj = object_field.reshape(8, 128, 512)
    def edge(index):
        return pl.BlockSpec((8, 128, LANE), lambda i: (0, 0, index))

    def whole(*shape):
        return pl.BlockSpec(shape, lambda i: (0,) * len(shape))

    ce, co = pl.pallas_call(
        pack_kernel,
        out_shape=[sds(8, HALF, LANE)] * 2,
        grid=(1,),
        in_specs=[edge(0), edge(3)],
        out_specs=[whole(8, HALF, LANE)] * 2,
        compiler_params=params(32),
        name="pack",
    )(obj, obj)
    ce = col_ev(ce)
    co = col_od(co)
    comb, ev, od = pl.pallas_call(
        comb_kernel,
        out_shape=[sds(8, 128, LANE), sds(TILES, 8, HALF, LANE), sds(TILES, 8, HALF, LANE)],
        in_specs=[vmem()] * 3,
        out_specs=[vmem()] * 3,
        compiler_params=params(32),
        name="comb",
    )(obj, ce, co)
    od = row_od(od)
    ev = row_ev(ev)
    phase_re = jnp.cos(propagator_phase)
    phase_im = jnp.sin(propagator_phase)
    tables = [jnp.asarray(m) for m in dft_matrices()]
    anywhere = pl.BlockSpec(memory_space=pl.ANY)
    u, ev, od, own = pl.pallas_call(
        slots_kernel,
        out_shape=[
            sds(TILES, 8, BAND, LANE),
            sds(41, STRIP, LANE),
            sds(41, STRIP, LANE),
            sds(9, BAND, LANE),
        ],
        in_specs=[smem()] * 3 + [anywhere] * 4 + [vmem()] * 8,
        out_specs=[vmem()] * 4,
        scratch_shapes=[
            pltpu.VMEM((TILES, 8, 256, LANE), f32),
            pltpu.VMEM((TILES, 8, 256, LANE), f32),
            pltpu.VMEM((4, 4, 2, LANE, LANE), f32),
            pltpu.VMEM((5, 4, 2, LANE, LANE), f32),
            pltpu.VMEM((256, LANE), f32),
            pltpu.SemaphoreType.DMA((7,)),
        ],
        compiler_params=params(56),
        name="slots",
    )(
        position_rows.reshape(-1),
        position_cols.reshape(-1),
        tile_counts.reshape(-1),
        obj,
        comb,
        ev,
        od,
        intensities.reshape(4, LANE, LANE),
        probe_field,
        phase_re,
        phase_im,
        *tables,
    )
    od = row_od(od)
    ev = row_ev(ev)
    ce, co = pl.pallas_call(
        sides_kernel,
        out_shape=[sds(9, STRIP, LANE)] * 2,
        grid=(1,),
        in_specs=[whole(9, BAND, LANE), whole(9, STRIP, LANE), whole(9, STRIP, LANE)],
        out_specs=[whole(9, STRIP, LANE)] * 2,
        compiler_params=params(32),
        name="sides",
    )(own, ev, od)
    ce = col_ev(ce)
    co = col_od(co)
    packed, maps, out_bias = conv_matrices(conv_weight, conv_bias, output_weight, output_bias)
    out = denoise_call(u, ev, od, ce, co, packed, maps, out_bias)
    return out.reshape(4, 2, 128, 512)


def solution(mesh):
    placed = (
        P(None, None, "row", "col"),
        P(),
        P(),
        P("row", "col", None),
        P("row", "col", None),
        P("row", "col"),
        P("row", "col", None, None, None),
        P(),
        P(),
        P(),
        P(),
    )
    return jax.shard_map(
        per_device,
        mesh=mesh,
        in_specs=placed,
        out_specs=P(None, None, "row", "col"),
        check_vma=False,
    )
```

```python
import functools

import jax
import jax.numpy as jnp
import numpy as np
from jax import lax
from jax.experimental import pallas as pl
from jax.experimental.pallas import tpu as pltpu
from jax.sharding import PartitionSpec as P

step_size = 0.02
LANE = 128
HALF = 64
STRIP = 72
BAND = 144
TILES = 5
ROWS_KEPT = 140
KDX = 48
KTOT = 448

f32 = jnp.float32
bf16 = jnp.bfloat16


def params(mib):
    return pltpu.CompilerParams(vmem_limit_bytes=mib << 20)


def vmem():
    return pl.BlockSpec(memory_space=pltpu.VMEM)


def smem():
    return pl.BlockSpec(memory_space=pltpu.SMEM)


def lanes_of(shape):
    return lax.broadcasted_iota(jnp.int32, shape, len(shape) - 1)


def split(value):
    high = value.astype(bf16)
    low = (value - high.astype(f32)).astype(bf16)
    return high, low


def halves_swapped(value):
    return pltpu.roll(value, HALF, value.ndim - 1)


def pack_kernel(first_ref, last_ref, ce_ref, co_ref):
    col_odd = lax.axis_index("col") % 2
    first = lanes_of((HALF, LANE)) < HALF
    for c in range(8):
        left = first_ref[c]
        right = last_ref[c]
        to_left = jnp.where(first, left[:HALF], halves_swapped(left[HALF:]))
        to_right = jnp.where(first, halves_swapped(right[HALF:]), right[:HALF])
        ce_ref[c] = jnp.where(col_odd == 1, to_left, to_right)
        co_ref[c] = jnp.where(col_odd == 1, to_right, to_left)


def strips_kernel(obj_ref, ev_ref, od_ref):
    row_odd = lax.axis_index("row") % 2
    ev_start = pl.multiple_of((1 - row_odd) * HALF, HALF)
    od_start = pl.multiple_of(row_odd * HALF, HALF)
    for c in range(8):
        for t in range(4):
            ev_ref[t, c] = obj_ref[c, pl.ds(ev_start, HALF), t * LANE : (t + 1) * LANE]
            od_ref[t, c] = obj_ref[c, pl.ds(od_start, HALF), t * LANE : (t + 1) * LANE]


def comb_kernel(ce_ref, co_ref, ev_in, od_in, comb_ref, ev_ref, od_ref, comb_sc, sems):
    del ev_in, od_in
    row_odd = lax.axis_index("row") % 2
    col_odd = lax.axis_index("col") % 2
    first = lanes_of((HALF, LANE)) < HALF
    for c in range(8):
        ce = ce_ref[c]
        co = co_ref[c]
        from_right = jnp.where(col_odd == 1, co, ce)
        from_left = jnp.where(col_odd == 1, ce, co)
        comb_sc[c, :HALF] = jnp.where(first, from_right, from_left)
        comb_sc[c, HALF:] = halves_swapped(jnp.where(first, from_left, from_right))
    ev_start = pl.multiple_of((1 - row_odd) * HALF, HALF)
    od_start = pl.multiple_of(row_odd * HALF, HALF)
    started = [
        pltpu.make_async_copy(comb_sc.at[:, pl.ds(od_start, HALF), :], od_ref.at[4], sems.at[0]),
        pltpu.make_async_copy(comb_sc.at[:, pl.ds(ev_start, HALF), :], ev_ref.at[4], sems.at[1]),
        pltpu.make_async_copy(comb_sc, comb_ref, sems.at[2]),
    ]
    for item in started:
        item.start()
    for item in started:
        item.wait()


def slots_kernel(
    rows_ref,
    cols_ref,
    count_ref,
    obj_ref,
    comb_ref,
    ev_ref,
    od_ref,
    meas_any,
    probe_ref,
    phase_re_ref,
    phase_im_ref,
    left_f_any,
    left_b_any,
    right_f_any,
    right_b_any,
    u_ref,
    out_ev,
    out_od,
    own_ref,
    frame,
    accum,
    win,
    waves,
    extra,
    left_f_ref,
    left_b_ref,
    right_f_ref,
    right_b_ref,
    meas_ref,
    sems,
):
    row_odd = lax.axis_index("row") % 2
    ev_at = pl.multiple_of((1 - row_odd) * 192, HALF)
    od_at = pl.multiple_of(row_odd * 192, HALF)
    copies = []
    for t in range(4):
        copies.append((obj_ref.at[:, :, t * LANE : (t + 1) * LANE], frame.at[t, :, HALF:192, :]))
    copies.append((comb_ref, frame.at[4, :, HALF:192, :]))
    copies.append((ev_ref, frame.at[:, :, pl.ds(ev_at, HALF), :]))
    copies.append((od_ref, frame.at[:, :, pl.ds(od_at, HALF), :]))
    started = [pltpu.make_async_copy(src, dst, sems.at[i]) for i, (src, dst) in enumerate(copies)]
    late = [
        (left_f_any, left_f_ref),
        (right_f_any, right_f_ref),
        (right_b_any, right_b_ref),
        (left_b_any, left_b_ref),
        (meas_any, meas_ref),
    ]
    later = [pltpu.make_async_copy(src, dst, sems.at[7 + i]) for i, (src, dst) in enumerate(late)]
    for item in started + later:
        item.start()
    accum[...] = jnp.zeros(accum.shape, f32)
    for item in started:
        item.wait()

    lane = lanes_of((LANE, LANE))
    spots = []
    for k in range(4):
        row = rows_ref[k]
        at = lax.rem(cols_ref[k] + (640 - HALF), 640)
        q = at // LANE
        s = at - q * LANE
        nxt = jnp.where(q == 4, 0, q + 1)
        spots.append((row, q, nxt, s))

    for k in range(4):
        row, q, nxt, s = spots[k]
        keep = lane >= s
        turn = jnp.where(s == 0, 0, LANE - s)

        def take(c, carry, k=k, row=row, q=q, nxt=nxt, keep=keep, turn=turn):
            here = frame[q, c, pl.ds(row, LANE), :]
            beyond = frame[nxt, c, pl.ds(row, LANE), :]
            win[c // 2, k, c % 2] = pltpu.roll(jnp.where(keep, here, beyond), turn, 1)
            return carry

        lax.fori_loop(0, 8, take, 0, unroll=8)

    h_re = phase_re_ref[...]
    h_im = phase_im_ref[...]

    def left(xs, mat_ref):
        outs = []
        for g in range(0, 4, 2):
            stack = jnp.concatenate([jnp.concatenate(xs[k], axis=0) for k in (g, g + 1)], axis=1)
            high, low = split(stack)
            out = jnp.dot(
                mat_ref[...], jnp.concatenate([high, low, high], axis=0), preferred_element_type=f32
            )
            outs += [(out[:LANE, at : at + LANE], out[LANE:, at : at + LANE]) for at in (0, LANE)]
        return outs

    def right(xs, mat_ref):
        outs = []
        for g in range(0, 4, 2):
            stack = jnp.concatenate([jnp.concatenate(xs[k], axis=1) for k in (g, g + 1)], axis=0)
            high, low = split(stack)
            out = jnp.dot(
                jnp.concatenate([high, low, high], axis=1), mat_ref[...], preferred_element_type=f32
            )
            outs += [(out[at : at + LANE, :LANE], out[at : at + LANE, LANE:]) for at in (0, LANE)]
        return outs

    def forth(xs):
        return right(left(xs, left_f_ref), right_f_ref)

    def back(xs):
        return left(right(xs, right_b_ref), left_b_ref)

    def times(xs, re, im):
        return [(a * re - b * im, a * im + b * re) for a, b in xs]

    for k in range(4):
        waves[0, k, 0] = probe_ref[0]
        waves[0, k, 1] = probe_ref[1]

    def exit_wave(s):
        xs = []
        for k in range(4):
            p_re, p_im = waves[s, k, 0], waves[s, k, 1]
            o_re, o_im = win[s, k, 0], win[s, k, 1]
            xs.append((p_re * o_re - p_im * o_im, p_re * o_im + p_im * o_re))
        return xs

    def forward(s, carry):
        xs = back(times(forth(exit_wave(s)), h_re, h_im))
        for k in range(4):
            waves[s + 1, k, 0] = xs[k][0]
            waves[s + 1, k, 1] = xs[k][1]
        return carry

    for item in later:
        item.wait()
    lax.fori_loop(0, 3, forward, 0)
    far = forth(exit_wave(3))
    count = count_ref[0]
    seeds = []
    for k in range(4):
        re, im = far[k]
        factor = (re * re + im * im - meas_ref[k]) * (-2.0 * step_size)
        factor = jnp.where(k < count, factor, 0.0)
        seeds.append((factor * re, factor * im))
    gs = back(seeds)
    grad = waves
    for k in range(4):
        grad[4, k, 0] = gs[k][0]
        grad[4, k, 1] = gs[k][1]

    def through(s):
        xs = []
        for k in range(4):
            g_re, g_im = waves[4, k, 0], waves[4, k, 1]
            p_re, p_im = waves[s, k, 0], waves[s, k, 1]
            o_re, o_im = win[s, k, 0], win[s, k, 1]
            win[s, k, 0] = p_re * g_re + p_im * g_im
            win[s, k, 1] = p_re * g_im - p_im * g_re
            xs.append((o_re * g_re + o_im * g_im, o_re * g_im - o_im * g_re))
        return xs

    def backward(i, carry):
        xs = back(times(forth(through(3 - i)), h_re, -h_im))
        for k in range(4):
            waves[4, k, 0] = xs[k][0]
            waves[4, k, 1] = xs[k][1]
        return carry

    lax.fori_loop(0, 3, backward, 0)
    for k in range(4):
        g_re, g_im = waves[4, k, 0], waves[4, k, 1]
        p_re, p_im = probe_ref[0], probe_ref[1]
        win[0, k, 0] = p_re * g_re + p_im * g_im
        win[0, k, 1] = p_re * g_im - p_im * g_re

    for k in range(4):
        row, q, nxt, s = spots[k]
        keep = lane >= s

        def give(c, carry, k=k, row=row, q=q, nxt=nxt, keep=keep, s=s):
            turned = pltpu.roll(win[c // 2, k, c % 2], s, 1)
            here = accum[q, c, pl.ds(row, LANE), :]
            accum[q, c, pl.ds(row, LANE), :] = here + jnp.where(keep, turned, 0.0)
            beyond = accum[nxt, c, pl.ds(row, LANE), :]
            accum[nxt, c, pl.ds(row, LANE), :] = beyond + jnp.where(keep, 0.0, turned)
            return carry

        lax.fori_loop(0, 8, give, 0, unroll=8)

    wide = lanes_of((256, LANE)) // 8
    gathered = jnp.zeros((256, LANE), f32)
    for c in range(8):
        tail = pltpu.roll(accum[3, c], (8 * c + 8) % LANE, 1)
        head = pltpu.roll(accum[0, c], HALF + 8 * c, 1)
        gathered = jnp.where(wide == c, tail, gathered)
        gathered = jnp.where(wide == 8 + c, head, gathered)
    extra[...] = gathered

    ev_from = pl.multiple_of((1 - row_odd) * 184, 8)
    od_from = pl.multiple_of(row_odd * 184, 8)
    moves = [
        (accum.at[4, :, pl.ds(od_from, STRIP), :], out_od.at[0:8]),
        (extra.at[pl.ds(od_from, STRIP), :], out_od.at[8]),
    ]
    for t in range(4):
        moves.append((accum.at[t, :, pl.ds(od_from, STRIP), :], out_od.at[9 + 8 * t : 17 + 8 * t]))
    moves.append((accum.at[4, :, pl.ds(ev_from, STRIP), :], out_ev.at[0:8]))
    moves.append((extra.at[pl.ds(ev_from, STRIP), :], out_ev.at[8]))
    for t in range(4):
        moves.append((accum.at[t, :, pl.ds(ev_from, STRIP), :], out_ev.at[9 + 8 * t : 17 + 8 * t]))
    moves.append((accum.at[4, :, 56:200, :], own_ref.at[0:8]))
    moves.append((extra.at[56:200, :], own_ref.at[8]))
    sent = [pltpu.make_async_copy(src, dst, sems.at[12 + i]) for i, (src, dst) in enumerate(moves)]
    for item in sent:
        item.start()
    for t in range(TILES):
        frame[t, :, 56:200, :] = frame[t, :, 56:200, :] + accum[t, :, 56:200, :]
        item = pltpu.make_async_copy(frame.at[t, :, 56:200, :], u_ref.at[t], sems.at[26 + t])
        item.start()
        sent.append(item)
    for item in sent:
        item.wait()


def sides_kernel(own_any, ev_any, od_any, ce_ref, co_ref, own_ref, evc_ref, odc_ref, sems):
    started = [
        pltpu.make_async_copy(own_any, own_ref, sems.at[0]),
        pltpu.make_async_copy(ev_any.at[0:9], evc_ref, sems.at[1]),
        pltpu.make_async_copy(od_any.at[0:9], odc_ref, sems.at[2]),
    ]
    for item in started:
        item.start()
    for item in started:
        item.wait()
    row_odd = lax.axis_index("row") % 2
    col_odd = lax.axis_index("col") % 2
    first = lanes_of((STRIP, LANE)) < HALF
    for c in range(9):
        ev = evc_ref[c]
        od = odc_ref[c]
        top = own_ref[c, :STRIP] + jnp.where(row_odd == 1, ev, od)
        bottom = halves_swapped(own_ref[c, STRIP:] + jnp.where(row_odd == 1, od, ev))
        to_right = jnp.where(first, top, bottom)
        to_left = jnp.where(first, bottom, top)
        ce_ref[c] = jnp.where(col_odd == 1, to_left, to_right)
        co_ref[c] = jnp.where(col_odd == 1, to_right, to_left)


def weights_kernel(taps_ref, bias_ref, map_ref, map_bias_ref, conv_out, map_out, bias_out):
    def hot(rows, cols, test):
        a = lax.broadcasted_iota(jnp.int32, (rows, cols), 0)
        b = lax.broadcasted_iota(jnp.int32, (rows, cols), 1)
        return jnp.where(test(a, b), 1.0, 0.0).astype(f32)

    def exact(a, b):
        return jnp.dot(a, b, precision=lax.Precision.HIGHEST, preferred_element_type=f32)

    place = hot(12, KTOT, lambda a, b: (b < 432) & (a == (b % 144) // 48 * 4 + b % 4))
    row = lax.broadcasted_iota(jnp.int32, (256, KTOT), 0)
    col = lax.broadcasted_iota(jnp.int32, (256, KTOT), 1)
    shift = (col % 48) // 4 - row // 32
    is_bias = (col == 432) | (col == 433)
    use_low = ((col >= 288) & (col < 432)) | (col == 433)
    hidden_hot = hot(256, 32, lambda a, b: a % 32 == b)
    channel_hot = hot(32, 4, lambda a, b: a % 4 == b)
    spread = hot(32, 256, lambda a, b: a == b % 32)
    same_row = hot(32, 256, lambda a, b: a // 4 == b // 32)
    for layer, start in zip(range(3), (2, 2, 0)):
        bias = jnp.sum(hidden_hot * bias_ref[layer : layer + 1, :], axis=1, keepdims=True)
        total = jnp.where(is_bias, bias, 0.0)
        for dy in range(3):
            part = exact(taps_ref[layer, dy], place)
            whole = jnp.concatenate([part] * 8, axis=0)
            total = total + jnp.where((shift == dy + start) & (col < 432), whole, 0.0)
        high, low = split(total * 0.5)
        conv_out[layer] = jnp.where(use_low, low.astype(f32), high.astype(f32)).astype(bf16)
        wide = exact(exact(channel_hot, map_ref[layer]), spread) * same_row
        high, low = split(wide)
        map_out[layer, 0:32] = high
        map_out[layer, 32:64] = low
        out_bias = jnp.sum(channel_hot * map_bias_ref[layer : layer + 1, :], axis=1, keepdims=True)
        bias_out[layer] = jnp.broadcast_to(out_bias, (32, LANE))


def merge_kernel(u_any, ev_any, od_any, low_st, up_st, u_ref, ev_ref, od_ref, sems):
    pairs = ((u_any, u_ref), (ev_any, ev_ref), (od_any, od_ref))
    started = [pltpu.make_async_copy(a, b, sems.at[i]) for i, (a, b) in enumerate(pairs)]
    for item in started:
        item.start()
    for item in started:
        item.wait()
    row_odd = lax.axis_index("row") % 2

    def combine(t, c):
        plane = c if t == 4 else 9 + 8 * t + c
        ev = ev_ref[plane]
        od = od_ref[plane]
        top = u_ref[t, c, :STRIP] + jnp.where(row_odd == 1, ev, od)
        bottom = u_ref[t, c, STRIP:] + jnp.where(row_odd == 1, od, ev)
        return jnp.concatenate([top, bottom], axis=0)

    for t in range(TILES):
        for c in range(4):
            low_st[t, pl.ds(c, ROWS_KEPT, stride=4), :] = combine(t, c)[3:143]
            up_st[t, pl.ds(c, ROWS_KEPT, stride=4), :] = combine(t, 4 + c)[4:144]


def denoise_kernel(
    low_any,
    up_any,
    ce_ref,
    co_ref,
    conv_sc,
    map_sc,
    bias_ref,
    out_ref,
    low_st,
    up_st,
    cond_st,
    half_sc,
    sems,
):
    row_id = lax.axis_index("row")
    col_id = lax.axis_index("col")
    col_odd = col_id % 2
    lane = lanes_of((STRIP, LANE))
    first = lane < HALF
    low_copy = pltpu.make_async_copy(low_any, low_st, sems.at[0])
    up_copy = pltpu.make_async_copy(up_any, up_st, sems.at[1])
    low_copy.start()
    up_copy.start()

    def add_sides(c):
        store = low_st if c < 4 else up_st
        skip = 3 if c < 4 else 4
        ce = ce_ref[c]
        co = co_ref[c]
        from_left = jnp.where(col_odd == 1, ce, co)
        from_right = jnp.where(col_odd == 1, co, ce)
        swapped_left = halves_swapped(from_left)
        swapped_right = halves_swapped(from_right)
        ce = ce_ref[8]
        co = co_ref[8]
        tail = jnp.where(col_odd == 1, ce, co)
        head = jnp.where(col_odd == 1, co, ce)
        tail_top = pltpu.roll(tail, (120 - 8 * c) % LANE, 1)
        tail_bottom = pltpu.roll(tail, (HALF + 120 - 8 * c) % LANE, 1)
        head_top = pltpu.roll(head, (HALF - 8 * c) % LANE, 1)
        head_bottom = pltpu.roll(head, (LANE - 8 * c) % LANE, 1)
        at_tail = lane >= 120
        at_head = lane < 8
        pieces = {
            0: (jnp.where(first, from_left, 0.0), jnp.where(first, swapped_left, 0.0)),
            3: (jnp.where(first, 0.0, from_right), jnp.where(first, 0.0, swapped_right)),
            4: (
                jnp.where(at_tail, tail_top, jnp.where(at_head, head_top, 0.0)),
                jnp.where(at_tail, tail_bottom, jnp.where(at_head, head_bottom, 0.0)),
            ),
        }
        for t, both in pieces.items():
            at = pl.ds(c % 4, ROWS_KEPT, stride=4)
            whole = jnp.concatenate(both, axis=0)[skip : skip + ROWS_KEPT]
            store[t, at, :] = store[t, at, :] + whole

    low_copy.wait()
    for c in range(4):
        add_sides(c)
    up_copy.wait()
    for c in range(4, 8):
        add_sides(c)

    last_row = lax.axis_size("row") - 1
    last_col = lax.axis_size("col") - 1
    right_off = jnp.where(col_id == last_col, 512, 576)
    left_off = jnp.where(col_id == 0, 640, 576)

    def prepare(store, first_row):
        row_low = jnp.where(row_id == 0, -first_row * 4, 0)
        row_high = jnp.where(row_id == last_row, (128 - first_row) * 4, 4 * ROWS_KEPT)

        def body(i, carry):
            at = pl.multiple_of(i * 16, 16)
            x = jnp.concatenate([store[t, pl.ds(at, 16), :] for t in range(TILES)], axis=1)
            column = lax.broadcasted_iota(jnp.int32, x.shape, 1)
            index = lax.broadcasted_iota(jnp.int32, x.shape, 0) + at
            inside = (index >= row_low) & (index < row_high)
            inside = inside & ((column < right_off) | (column >= left_off))
            x = jnp.where(inside, x, 0.0)
            for dx in range(3):
                y = x if dx == 1 else pltpu.roll(x, 1 if dx == 0 else 639, 1)
                high, low = split(y)
                cond_st[0, dx, pl.ds(at, 16), :] = high
                cond_st[1, dx, pl.ds(at, 16), :] = low
            return carry

        lax.fori_loop(0, 4 * ROWS_KEPT // 16, body, 0, unroll=5)

    ones = jnp.ones((16, 640), bf16)

    def layer_pass(layer, groups, read_at, store, write_at, width):
        bias = bias_ref[layer]

        def first_map(g, slot):
            src = pl.multiple_of(read_at + g * 32, 16)
            pieces = [cond_st[part, dx, pl.ds(src, KDX), :width] for part in (0, 1) for dx in range(3)]
            pieces = pieces + pieces[:3] + [ones[:, :width]]
            half_sc[slot, :, :width] = jnp.dot(
                conv_sc[layer], jnp.concatenate(pieces, axis=0), preferred_element_type=f32
            )

        def second_map(g, slot):
            dst = pl.multiple_of(write_at + g * 32, 8)
            half = half_sc[slot, :, :width]
            hidden = half + half * jnp.tanh(half)
            high, low = split(hidden)
            out = jnp.dot(map_sc[layer], high, preferred_element_type=f32)
            low_out = jnp.dot(map_sc[layer, 0:32], low, preferred_element_type=f32)
            term = out[:32] + out[32:] + low_out
            for t in range(width // LANE):
                bit = term[:, t * LANE : (t + 1) * LANE]
                store[t, pl.ds(dst, 32), :] = store[t, pl.ds(dst, 32), :] + (bit + bias)

        first_map(0, 0)
        pairs_whole = (groups - 1) // 2

        def body(i, carry):
            first_map(2 * i + 1, 1)
            second_map(2 * i, 0)
            first_map(2 * i + 2, 0)
            second_map(2 * i + 1, 1)
            return carry

        lax.fori_loop(0, pairs_whole, body, 0)
        done = 2 * pairs_whole
        if groups - done == 2:
            first_map(done + 1, 1)
            second_map(done, 0)
            second_map(done + 1, 1)
        else:
            second_map(done, 0)

    prepare(low_st, -5)
    layer_pass(0, 17, 0, up_st, 8, 640)
    prepare(up_st, -4)
    layer_pass(1, 17, 0, low_st, 16, 640)
    prepare(low_st, -5)
    layer_pass(2, 16, 16, up_st, 16, 512)
    for t in range(4):
        for c in range(4):
            out_ref[c, :, t * LANE : (t + 1) * LANE] = low_st[t, pl.ds(20 + c, 128, stride=4), :]
            out_ref[4 + c, :, t * LANE : (t + 1) * LANE] = up_st[t, pl.ds(16 + c, 128, stride=4), :]


def dft_matrices():
    index = np.arange(LANE)
    angle = 2.0 * np.pi / LANE * (np.outer(index, index) % LANE)
    c = np.cos(angle) / np.sqrt(LANE)
    s = np.sin(angle) / np.sqrt(LANE)
    a = np.block([[c, s], [-s, c]]).astype(np.float32)
    b = np.block([[c, -s], [s, c]]).astype(np.float32)

    def parts(m):
        high = m.astype(jnp.bfloat16)
        low = (m - high.astype(np.float32)).astype(jnp.bfloat16)
        return high, low

    (ah, al), (bh, bl) = parts(a), parts(b)
    left_f = np.concatenate([ah, ah, al], axis=1)
    left_b = np.concatenate([bh, bh, bl], axis=1)
    right_f = np.concatenate([bh, bh, bl], axis=0)
    right_b = np.concatenate([ah, ah, al], axis=0)
    return left_f, left_b, right_f, right_b


def sds(*shape):
    return jax.ShapeDtypeStruct(shape, f32)


def slots_call(*operands):
    anywhere = pl.BlockSpec(memory_space=pl.ANY)
    return pl.pallas_call(
        slots_kernel,
        out_shape=[
            sds(TILES, 8, BAND, LANE),
            sds(41, STRIP, LANE),
            sds(41, STRIP, LANE),
            sds(9, BAND, LANE),
        ],
        in_specs=[smem()] * 3 + [anywhere] * 5 + [vmem()] * 3 + [anywhere] * 4,
        out_specs=[anywhere] * 4,
        scratch_shapes=[
            pltpu.VMEM((TILES, 8, 256, LANE), f32),
            pltpu.VMEM((TILES, 8, 256, LANE), f32),
            pltpu.VMEM((4, 4, 2, LANE, LANE), f32),
            pltpu.VMEM((5, 4, 2, LANE, LANE), f32),
            pltpu.VMEM((256, LANE), f32),
            pltpu.VMEM((256, 768), bf16),
            pltpu.VMEM((256, 768), bf16),
            pltpu.VMEM((768, 256), bf16),
            pltpu.VMEM((768, 256), bf16),
            pltpu.VMEM((4, LANE, LANE), f32),
            pltpu.SemaphoreType.DMA((31,)),
        ],
        compiler_params=params(62),
        name="slots",
    )(*operands)


def denoise_call(u, ev, od, ce, co, taps, conv_bias, output_weight, output_bias):
    anywhere = pl.BlockSpec(memory_space=pl.ANY)
    lines = sds(TILES, 4 * ROWS_KEPT, LANE)
    conv_parts, map_parts, out_bias = pl.pallas_call(
        weights_kernel,
        out_shape=[
            jax.ShapeDtypeStruct((3, 256, KTOT), bf16),
            jax.ShapeDtypeStruct((3, 64, 256), bf16),
            sds(3, 32, LANE),
        ],
        in_specs=[vmem()] * 4,
        out_specs=[vmem()] * 3,
        compiler_params=params(62),
        cost_estimate=pl.CostEstimate(flops=1 << 20, bytes_accessed=3 << 20, transcendentals=0),
        name="weights",
    )(taps, conv_bias, output_weight, output_bias)
    low, up = pl.pallas_call(
        merge_kernel,
        out_shape=[lines] * 2,
        in_specs=[anywhere] * 3,
        out_specs=[vmem()] * 2,
        scratch_shapes=[
            pltpu.VMEM((TILES, 8, BAND, LANE), f32),
            pltpu.VMEM((41, STRIP, LANE), f32),
            pltpu.VMEM((41, STRIP, LANE), f32),
            pltpu.SemaphoreType.DMA((3,)),
        ],
        compiler_params=params(62),
        cost_estimate=pl.CostEstimate(flops=1 << 20, bytes_accessed=9 << 20, transcendentals=0),
        name="merge",
    )(u, ev, od)
    return pl.pallas_call(
        denoise_kernel,
        out_shape=sds(8, 128, 512),
        in_specs=[anywhere] * 2 + [vmem()] * 5,
        out_specs=vmem(),
        scratch_shapes=[
            pltpu.VMEM((TILES, 4 * ROWS_KEPT, LANE), f32),
            pltpu.VMEM((TILES, 4 * ROWS_KEPT, LANE), f32),
            pltpu.VMEM((2, 3, 4 * ROWS_KEPT, 640), bf16),
            pltpu.VMEM((2, 256, 640), f32),
            pltpu.SemaphoreType.DMA((2,)),
        ],
        compiler_params=params(62),
        name="denoise",
    )(low, up, ce, co, conv_parts, map_parts, out_bias)


def per_device(
    object_field,
    probe_field,
    propagator_phase,
    position_rows,
    position_cols,
    tile_counts,
    intensities,
    conv_weight,
    conv_bias,
    output_weight,
    output_bias,
):
    rows = lax.axis_size("row")
    cols = lax.axis_size("col")

    def pairs(count, start):
        found = []
        for i in range(start, count - 1, 2):
            found += [(i, i + 1), (i + 1, i)]
        return found

    def row_ev(x):
        return lax.ppermute(x, "row", pairs(rows, 0))

    def row_od(x):
        return lax.ppermute(x, "row", pairs(rows, 1))

    def col_ev(x):
        return lax.ppermute(x, "col", pairs(cols, 0))

    def col_od(x):
        return lax.ppermute(x, "col", pairs(cols, 1))

    obj = object_field.reshape(8, 128, 512)
    def edge(index):
        return pl.BlockSpec((8, 128, LANE), lambda i: (0, 0, index))

    def whole(*shape):
        return pl.BlockSpec(shape, lambda i: (0,) * len(shape))

    ce, co = pl.pallas_call(
        pack_kernel,
        out_shape=[sds(8, HALF, LANE)] * 2,
        grid=(1,),
        in_specs=[edge(0), edge(3)],
        out_specs=[whole(8, HALF, LANE)] * 2,
        compiler_params=params(62),
        name="pack",
    )(obj, obj)
    ce = col_ev(ce)
    co = col_od(co)
    anywhere = pl.BlockSpec(memory_space=pl.ANY)
    strip = sds(TILES, 8, HALF, LANE)
    ev, od = pl.pallas_call(
        strips_kernel,
        out_shape=[strip] * 2,
        in_specs=[vmem()],
        out_specs=[vmem()] * 2,
        compiler_params=params(62),
        cost_estimate=pl.CostEstimate(flops=0, bytes_accessed=4 << 20, transcendentals=0),
        name="strips",
    )(obj)
    comb, ev, od = pl.pallas_call(
        comb_kernel,
        out_shape=[sds(8, 128, LANE), strip, strip],
        in_specs=[vmem()] * 2 + [anywhere] * 2,
        out_specs=[anywhere] * 3,
        scratch_shapes=[pltpu.VMEM((8, 128, LANE), f32), pltpu.SemaphoreType.DMA((3,))],
        input_output_aliases={2: 1, 3: 2},
        compiler_params=params(62),
        name="comb",
    )(ce, co, ev, od)
    od = row_od(od)
    ev = row_ev(ev)
    phase_re = jnp.cos(propagator_phase)
    phase_im = jnp.sin(propagator_phase)
    tables = [jnp.asarray(m) for m in dft_matrices()]
    u, ev, od, own = slots_call(
        position_rows.reshape(-1),
        position_cols.reshape(-1),
        tile_counts.reshape(-1),
        obj,
        comb,
        ev,
        od,
        intensities.reshape(4, LANE, LANE),
        probe_field,
        phase_re,
        phase_im,
        *tables,
    )
    od = row_od(od)
    ev = row_ev(ev)
    ce, co = pl.pallas_call(
        sides_kernel,
        out_shape=[sds(9, STRIP, LANE)] * 2,
        in_specs=[anywhere] * 3,
        out_specs=[vmem()] * 2,
        scratch_shapes=[
            pltpu.VMEM((9, BAND, LANE), f32),
            pltpu.VMEM((9, STRIP, LANE), f32),
            pltpu.VMEM((9, STRIP, LANE), f32),
            pltpu.SemaphoreType.DMA((3,)),
        ],
        compiler_params=params(62),
        name="sides",
    )(own, ev, od)
    ce = col_ev(ce)
    co = col_od(co)
    taps = conv_weight.reshape(3, 3, 3, 32, 4).transpose(0, 1, 3, 2, 4).reshape(3, 3, 32, 12)
    out = denoise_call(u, ev, od, ce, co, taps, conv_bias, output_weight, output_bias)
    return out.reshape(4, 2, 128, 512)


def solution(mesh):
    placed = (
        P(None, None, "row", "col"),
        P(),
        P(),
        P("row", "col", None),
        P("row", "col", None),
        P("row", "col"),
        P("row", "col", None, None, None),
        P(),
        P(),
        P(),
        P(),
    )
    return jax.shard_map(
        per_device,
        mesh=mesh,
        in_specs=placed,
        out_specs=P(None, None, "row", "col"),
        check_vma=False,
    )
```

```python
import functools

import jax
import jax.numpy as jnp
import numpy as np
from jax import lax
from jax.experimental import pallas as pl
from jax.experimental.pallas import tpu as pltpu
from jax.sharding import PartitionSpec as P

step_size = 0.02
LANE = 128
HALF = 64
STRIP = 72
BAND = 144
TILES = 5
ROWS_KEPT = 140
ROWS_SET = 138
KTOT = 240

f32 = jnp.float32
bf16 = jnp.bfloat16


def params(mib):
    return pltpu.CompilerParams(vmem_limit_bytes=mib << 20)


def vmem():
    return pl.BlockSpec(memory_space=pltpu.VMEM)


def smem():
    return pl.BlockSpec(memory_space=pltpu.SMEM)


def lanes_of(shape):
    return lax.broadcasted_iota(jnp.int32, shape, len(shape) - 1)


def split(value):
    high = value.astype(bf16)
    low = (value - high.astype(f32)).astype(bf16)
    return high, low


def halves_swapped(value):
    return pltpu.roll(value, HALF, value.ndim - 1)


def pack_kernel(first_ref, last_ref, ce_ref, co_ref):
    col_odd = lax.axis_index("col") % 2
    first = lanes_of((HALF, LANE)) < HALF
    for c in range(8):
        left = first_ref[c]
        right = last_ref[c]
        to_left = jnp.where(first, left[:HALF], halves_swapped(left[HALF:]))
        to_right = jnp.where(first, halves_swapped(right[HALF:]), right[:HALF])
        ce_ref[c] = jnp.where(col_odd == 1, to_left, to_right)
        co_ref[c] = jnp.where(col_odd == 1, to_right, to_left)


def strips_kernel(obj_ref, ev_ref, od_ref):
    row_odd = lax.axis_index("row") % 2
    ev_start = pl.multiple_of((1 - row_odd) * HALF, HALF)
    od_start = pl.multiple_of(row_odd * HALF, HALF)
    for c in range(8):
        for t in range(4):
            ev_ref[t, c] = obj_ref[c, pl.ds(ev_start, HALF), t * LANE : (t + 1) * LANE]
            od_ref[t, c] = obj_ref[c, pl.ds(od_start, HALF), t * LANE : (t + 1) * LANE]


def comb_kernel(ce_ref, co_ref, ev_in, od_in, comb_ref, ev_ref, od_ref, comb_sc, sems):
    del ev_in, od_in
    row_odd = lax.axis_index("row") % 2
    col_odd = lax.axis_index("col") % 2
    first = lanes_of((HALF, LANE)) < HALF
    for c in range(8):
        ce = ce_ref[c]
        co = co_ref[c]
        from_right = jnp.where(col_odd == 1, co, ce)
        from_left = jnp.where(col_odd == 1, ce, co)
        comb_sc[c, :HALF] = jnp.where(first, from_right, from_left)
        comb_sc[c, HALF:] = halves_swapped(jnp.where(first, from_left, from_right))
    ev_start = pl.multiple_of((1 - row_odd) * HALF, HALF)
    od_start = pl.multiple_of(row_odd * HALF, HALF)
    started = [
        pltpu.make_async_copy(comb_sc.at[:, pl.ds(od_start, HALF), :], od_ref.at[4], sems.at[0]),
        pltpu.make_async_copy(comb_sc.at[:, pl.ds(ev_start, HALF), :], ev_ref.at[4], sems.at[1]),
        pltpu.make_async_copy(comb_sc, comb_ref, sems.at[2]),
    ]
    for item in started:
        item.start()
    for item in started:
        item.wait()


def slots_kernel(
    rows_ref,
    cols_ref,
    count_ref,
    obj_ref,
    comb_ref,
    ev_ref,
    od_ref,
    meas_any,
    probe_ref,
    phase_re_ref,
    phase_im_ref,
    left_f_any,
    left_b_any,
    right_f_any,
    right_b_any,
    u_ref,
    out_ev,
    out_od,
    own_ref,
    frame,
    accum,
    win,
    waves,
    extra,
    left_f_ref,
    left_b_ref,
    right_f_ref,
    right_b_ref,
    meas_ref,
    sems,
):
    row_odd = lax.axis_index("row") % 2
    ev_at = pl.multiple_of((1 - row_odd) * 192, HALF)
    od_at = pl.multiple_of(row_odd * 192, HALF)
    copies = []
    for t in range(4):
        copies.append((obj_ref.at[:, :, t * LANE : (t + 1) * LANE], frame.at[t, :, HALF:192, :]))
    copies.append((comb_ref, frame.at[4, :, HALF:192, :]))
    copies.append((ev_ref, frame.at[:, :, pl.ds(ev_at, HALF), :]))
    copies.append((od_ref, frame.at[:, :, pl.ds(od_at, HALF), :]))
    started = [pltpu.make_async_copy(src, dst, sems.at[i]) for i, (src, dst) in enumerate(copies)]
    late = [
        (left_f_any, left_f_ref),
        (right_f_any, right_f_ref),
        (right_b_any, right_b_ref),
        (left_b_any, left_b_ref),
        (meas_any, meas_ref),
    ]
    later = [pltpu.make_async_copy(src, dst, sems.at[7 + i]) for i, (src, dst) in enumerate(late)]
    for item in started + later:
        item.start()
    accum[...] = jnp.zeros(accum.shape, f32)
    for item in started:
        item.wait()

    lane = lanes_of((LANE, LANE))
    spots = []
    for k in range(4):
        row = rows_ref[k]
        at = lax.rem(cols_ref[k] + (640 - HALF), 640)
        q = at // LANE
        s = at - q * LANE
        nxt = jnp.where(q == 4, 0, q + 1)
        spots.append((row, q, nxt, s))

    for k in range(4):
        row, q, nxt, s = spots[k]
        keep = lane >= s
        turn = jnp.where(s == 0, 0, LANE - s)

        def take(c, carry, k=k, row=row, q=q, nxt=nxt, keep=keep, turn=turn):
            here = frame[q, c, pl.ds(row, LANE), :]
            beyond = frame[nxt, c, pl.ds(row, LANE), :]
            win[c // 2, k, c % 2] = pltpu.roll(jnp.where(keep, here, beyond), turn, 1)
            return carry

        lax.fori_loop(0, 8, take, 0, unroll=8)

    h_re = phase_re_ref[...]
    h_im = phase_im_ref[...]

    def left(xs, mat_ref):
        outs = []
        for g in range(0, 4, 2):
            stack = jnp.concatenate([jnp.concatenate(xs[k], axis=0) for k in (g, g + 1)], axis=1)
            high, low = split(stack)
            out = jnp.dot(
                mat_ref[...], jnp.concatenate([high, low, high], axis=0), preferred_element_type=f32
            )
            outs += [(out[:LANE, at : at + LANE], out[LANE:, at : at + LANE]) for at in (0, LANE)]
        return outs

    def right(xs, mat_ref):
        outs = []
        for g in range(0, 4, 2):
            stack = jnp.concatenate([jnp.concatenate(xs[k], axis=1) for k in (g, g + 1)], axis=0)
            high, low = split(stack)
            out = jnp.dot(
                jnp.concatenate([high, low, high], axis=1), mat_ref[...], preferred_element_type=f32
            )
            outs += [(out[at : at + LANE, :LANE], out[at : at + LANE, LANE:]) for at in (0, LANE)]
        return outs

    def forth(xs):
        return right(left(xs, left_f_ref), right_f_ref)

    def back(xs):
        return left(right(xs, right_b_ref), left_b_ref)

    def times(xs, re, im):
        return [(a * re - b * im, a * im + b * re) for a, b in xs]

    for k in range(4):
        waves[0, k, 0] = probe_ref[0]
        waves[0, k, 1] = probe_ref[1]

    def exit_wave(s):
        xs = []
        for k in range(4):
            p_re, p_im = waves[s, k, 0], waves[s, k, 1]
            o_re, o_im = win[s, k, 0], win[s, k, 1]
            xs.append((p_re * o_re - p_im * o_im, p_re * o_im + p_im * o_re))
        return xs

    def forward(s, carry):
        xs = back(times(forth(exit_wave(s)), h_re, h_im))
        for k in range(4):
            waves[s + 1, k, 0] = xs[k][0]
            waves[s + 1, k, 1] = xs[k][1]
        return carry

    for item in later:
        item.wait()
    lax.fori_loop(0, 3, forward, 0)
    far = forth(exit_wave(3))
    count = count_ref[0]
    seeds = []
    for k in range(4):
        re, im = far[k]
        factor = (re * re + im * im - meas_ref[k]) * (-2.0 * step_size)
        factor = jnp.where(k < count, factor, 0.0)
        seeds.append((factor * re, factor * im))
    gs = back(seeds)
    grad = waves
    for k in range(4):
        grad[4, k, 0] = gs[k][0]
        grad[4, k, 1] = gs[k][1]

    def through(s):
        xs = []
        for k in range(4):
            g_re, g_im = waves[4, k, 0], waves[4, k, 1]
            p_re, p_im = waves[s, k, 0], waves[s, k, 1]
            o_re, o_im = win[s, k, 0], win[s, k, 1]
            win[s, k, 0] = p_re * g_re + p_im * g_im
            win[s, k, 1] = p_re * g_im - p_im * g_re
            xs.append((o_re * g_re + o_im * g_im, o_re * g_im - o_im * g_re))
        return xs

    def backward(i, carry):
        xs = back(times(forth(through(3 - i)), h_re, -h_im))
        for k in range(4):
            waves[4, k, 0] = xs[k][0]
            waves[4, k, 1] = xs[k][1]
        return carry

    lax.fori_loop(0, 3, backward, 0)
    for k in range(4):
        g_re, g_im = waves[4, k, 0], waves[4, k, 1]
        p_re, p_im = probe_ref[0], probe_ref[1]
        win[0, k, 0] = p_re * g_re + p_im * g_im
        win[0, k, 1] = p_re * g_im - p_im * g_re

    for k in range(4):
        row, q, nxt, s = spots[k]
        keep = lane >= s

        def give(c, carry, k=k, row=row, q=q, nxt=nxt, keep=keep, s=s):
            turned = pltpu.roll(win[c // 2, k, c % 2], s, 1)
            here = accum[q, c, pl.ds(row, LANE), :]
            accum[q, c, pl.ds(row, LANE), :] = here + jnp.where(keep, turned, 0.0)
            beyond = accum[nxt, c, pl.ds(row, LANE), :]
            accum[nxt, c, pl.ds(row, LANE), :] = beyond + jnp.where(keep, 0.0, turned)
            return carry

        lax.fori_loop(0, 8, give, 0, unroll=8)

    wide = lanes_of((256, LANE)) // 8
    gathered = jnp.zeros((256, LANE), f32)
    for c in range(8):
        tail = pltpu.roll(accum[3, c], (8 * c + 8) % LANE, 1)
        head = pltpu.roll(accum[0, c], HALF + 8 * c, 1)
        gathered = jnp.where(wide == c, tail, gathered)
        gathered = jnp.where(wide == 8 + c, head, gathered)
    extra[...] = gathered

    ev_from = pl.multiple_of((1 - row_odd) * 184, 8)
    od_from = pl.multiple_of(row_odd * 184, 8)
    moves = [
        (accum.at[4, :, pl.ds(od_from, STRIP), :], out_od.at[0:8]),
        (extra.at[pl.ds(od_from, STRIP), :], out_od.at[8]),
    ]
    for t in range(4):
        moves.append((accum.at[t, :, pl.ds(od_from, STRIP), :], out_od.at[9 + 8 * t : 17 + 8 * t]))
    moves.append((accum.at[4, :, pl.ds(ev_from, STRIP), :], out_ev.at[0:8]))
    moves.append((extra.at[pl.ds(ev_from, STRIP), :], out_ev.at[8]))
    for t in range(4):
        moves.append((accum.at[t, :, pl.ds(ev_from, STRIP), :], out_ev.at[9 + 8 * t : 17 + 8 * t]))
    moves.append((accum.at[4, :, 56:200, :], own_ref.at[0:8]))
    moves.append((extra.at[56:200, :], own_ref.at[8]))
    sent = [pltpu.make_async_copy(src, dst, sems.at[12 + i]) for i, (src, dst) in enumerate(moves)]
    for item in sent:
        item.start()
    for t in range(TILES):
        frame[t, :, 56:200, :] = frame[t, :, 56:200, :] + accum[t, :, 56:200, :]
        item = pltpu.make_async_copy(frame.at[t, :, 56:200, :], u_ref.at[t], sems.at[26 + t])
        item.start()
        sent.append(item)
    for item in sent:
        item.wait()


def sides_kernel(own_any, ev_any, od_any, ce_ref, co_ref, own_ref, evc_ref, odc_ref, sems):
    started = [
        pltpu.make_async_copy(own_any, own_ref, sems.at[0]),
        pltpu.make_async_copy(ev_any.at[0:9], evc_ref, sems.at[1]),
        pltpu.make_async_copy(od_any.at[0:9], odc_ref, sems.at[2]),
    ]
    for item in started:
        item.start()
    for item in started:
        item.wait()
    row_odd = lax.axis_index("row") % 2
    col_odd = lax.axis_index("col") % 2
    first = lanes_of((STRIP, LANE)) < HALF
    for c in range(9):
        ev = evc_ref[c]
        od = odc_ref[c]
        top = own_ref[c, :STRIP] + jnp.where(row_odd == 1, ev, od)
        bottom = halves_swapped(own_ref[c, STRIP:] + jnp.where(row_odd == 1, od, ev))
        to_right = jnp.where(first, top, bottom)
        to_left = jnp.where(first, bottom, top)
        ce_ref[c] = jnp.where(col_odd == 1, to_left, to_right)
        co_ref[c] = jnp.where(col_odd == 1, to_right, to_left)


def weights_kernel(taps_ref, bias_ref, map_ref, map_bias_ref, conv_out, map_out, bias_out):
    def hot(rows, cols, test):
        a = lax.broadcasted_iota(jnp.int32, (rows, cols), 0)
        b = lax.broadcasted_iota(jnp.int32, (rows, cols), 1)
        return jnp.where(test(a, b), 1.0, 0.0).astype(f32)

    def exact(a, b):
        return jnp.dot(a, b, precision=lax.Precision.HIGHEST, preferred_element_type=f32)

    def column(b):
        half = ((b >= 96) & (b < 144)) | ((b >= 192) & (b < 224))
        line = jnp.where(half, b % 8, b % 16)
        dx = jnp.where(half, (b - jnp.where(b < 144, 96, 192)) // 8 % 3, b // 16 % 3)
        k = line // 4 + jnp.where(half, 4, 0)
        return dx * 4 + line % 4, k, b < 216

    def placed(a, b):
        source, _, valid = column(b)
        return valid & (a == source)

    place = hot(12, KTOT, placed)
    row = lax.broadcasted_iota(jnp.int32, (LANE, KTOT), 0)
    col = lax.broadcasted_iota(jnp.int32, (LANE, KTOT), 1)
    _, window_row, is_tap = column(col)
    shift = window_row - row // 32
    is_bias = (col == 224) | (col == 225)
    use_low = ((col >= 144) & (col < 216)) | (col == 225)
    hidden_hot = hot(LANE, 32, lambda a, b: a % 32 == b)
    channel_hot = hot(32, 4, lambda a, b: a % 4 == b)
    spread = hot(32, 256, lambda a, b: a == b % 32)
    same_row = hot(32, 256, lambda a, b: a // 4 == b // 32)
    for layer in range(3):
        bias = jnp.sum(hidden_hot * bias_ref[layer : layer + 1, :], axis=1, keepdims=True)
        total = jnp.where(is_bias, bias, 0.0)
        for dy in range(3):
            part = exact(taps_ref[layer, dy], place)
            whole = jnp.concatenate([part] * 4, axis=0)
            total = total + jnp.where((shift == dy) & is_tap, whole, 0.0)
        high, low = split(total * 0.5)
        conv_out[layer] = jnp.where(use_low, low.astype(f32), high.astype(f32)).astype(bf16)
        wide = exact(exact(channel_hot, map_ref[layer]), spread) * same_row
        high, low = split(wide)
        map_out[layer, 0:32] = high
        map_out[layer, 32:64] = low
        out_bias = jnp.sum(channel_hot * map_bias_ref[layer : layer + 1, :], axis=1, keepdims=True)
        bias_out[layer] = jnp.broadcast_to(out_bias, (32, LANE))


def merge_kernel(u_any, ev_any, od_any, low_st, up_st, u_ref, ev_ref, od_ref, sems):
    pairs = ((u_any, u_ref), (ev_any, ev_ref), (od_any, od_ref))
    started = [pltpu.make_async_copy(a, b, sems.at[i]) for i, (a, b) in enumerate(pairs)]
    for item in started:
        item.start()
    for item in started:
        item.wait()
    row_odd = lax.axis_index("row") % 2

    def combine(t, c):
        plane = c if t == 4 else 9 + 8 * t + c
        ev = ev_ref[plane]
        od = od_ref[plane]
        top = u_ref[t, c, :STRIP] + jnp.where(row_odd == 1, ev, od)
        bottom = u_ref[t, c, STRIP:] + jnp.where(row_odd == 1, od, ev)
        return jnp.concatenate([top, bottom], axis=0)

    for t in range(TILES):
        for c in range(4):
            low_st[t, pl.ds(c, ROWS_SET, stride=4), :] = combine(t, c)[5:143]
            up_st[t, pl.ds(c, ROWS_SET, stride=4), :] = combine(t, 4 + c)[6:144]


def denoise_kernel(
    low_any,
    up_any,
    ce_ref,
    co_ref,
    conv_sc,
    map_sc,
    bias_ref,
    out_ref,
    low_st,
    up_st,
    cond_st,
    half_sc,
    sems,
):
    row_id = lax.axis_index("row")
    col_id = lax.axis_index("col")
    col_odd = col_id % 2
    lane = lanes_of((STRIP, LANE))
    first = lane < HALF
    low_copy = pltpu.make_async_copy(low_any, low_st, sems.at[0])
    up_copy = pltpu.make_async_copy(up_any, up_st, sems.at[1])
    low_copy.start()
    up_copy.start()

    def add_sides(c):
        store = low_st if c < 4 else up_st
        skip = 5 if c < 4 else 6
        ce = ce_ref[c]
        co = co_ref[c]
        from_left = jnp.where(col_odd == 1, ce, co)
        from_right = jnp.where(col_odd == 1, co, ce)
        swapped_left = halves_swapped(from_left)
        swapped_right = halves_swapped(from_right)
        ce = ce_ref[8]
        co = co_ref[8]
        tail = jnp.where(col_odd == 1, ce, co)
        head = jnp.where(col_odd == 1, co, ce)
        tail_top = pltpu.roll(tail, (120 - 8 * c) % LANE, 1)
        tail_bottom = pltpu.roll(tail, (HALF + 120 - 8 * c) % LANE, 1)
        head_top = pltpu.roll(head, (HALF - 8 * c) % LANE, 1)
        head_bottom = pltpu.roll(head, (LANE - 8 * c) % LANE, 1)
        at_tail = lane >= 120
        at_head = lane < 8
        pieces = {
            0: (jnp.where(first, from_left, 0.0), jnp.where(first, swapped_left, 0.0)),
            3: (jnp.where(first, 0.0, from_right), jnp.where(first, 0.0, swapped_right)),
            4: (
                jnp.where(at_tail, tail_top, jnp.where(at_head, head_top, 0.0)),
                jnp.where(at_tail, tail_bottom, jnp.where(at_head, head_bottom, 0.0)),
            ),
        }
        for t, both in pieces.items():
            at = pl.ds(c % 4, ROWS_SET, stride=4)
            whole = jnp.concatenate(both, axis=0)[skip : skip + ROWS_SET]
            store[t, at, :] = store[t, at, :] + whole

    low_copy.wait()
    for c in range(4):
        add_sides(c)
    up_copy.wait()
    for c in range(4, 8):
        add_sides(c)

    last_row = lax.axis_size("row") - 1
    last_col = lax.axis_size("col") - 1
    right_off = jnp.where(col_id == last_col, 512, 576)
    left_off = jnp.where(col_id == 0, 640, 576)

    def prepare(store, first_row):
        row_low = jnp.where(row_id == 0, -first_row * 4, 0)
        row_high = (jnp.where(row_id == last_row, 128, 131) - first_row) * 4

        def body(i, carry):
            at = pl.multiple_of(i * 16, 16)
            x = jnp.concatenate([store[t, pl.ds(at, 16), :] for t in range(TILES)], axis=1)
            column = lax.broadcasted_iota(jnp.int32, x.shape, 1)
            index = lax.broadcasted_iota(jnp.int32, x.shape, 0) + at
            inside = (index >= row_low) & (index < row_high)
            inside = inside & ((column < right_off) | (column >= left_off))
            x = jnp.where(inside, x, 0.0)
            heads = []
            rests = []
            for dx in range(3):
                y = x if dx == 1 else pltpu.roll(x, 1 if dx == 0 else 639, 1)
                high = y.astype(bf16)
                rest = y - high.astype(f32)
                cond_st[0, dx, pl.ds(at, 16), :] = high
                cond_st[1, dx, pl.ds(at, 16), :] = rest.astype(bf16)
                heads.append(y[:8])
                rests.append(rest[:8])
            for i in range(3):
                both = jnp.concatenate((heads + rests)[2 * i : 2 * i + 2], axis=0)
                cond_st[2, i, pl.ds(at, 16), :] = both.astype(bf16)
            return carry

        lax.fori_loop(0, 4 * ROWS_KEPT // 16, body, 0, unroll=7)

    ones = jnp.ones((16, 640), bf16)

    def layer_pass(layer, store, write_at, width):
        groups = 17
        bias = bias_ref[layer]

        def first_map(g, slot):
            for h in range(2):
                here = pl.ds(pl.multiple_of(g * 32 + 16 * h, 16), 16)
                below = pl.ds(pl.multiple_of(g * 32 + 16 * h + 16, 16), 16)
                main = [cond_st[part, dx, here, :width] for part in (0, 1) for dx in range(3)]
                half = [cond_st[2, i, below, :width] for i in range(3)]
                pieces = main + half + main[:3] + half[:2] + [ones[:, :width]]
                half_sc[slot, h * LANE : (h + 1) * LANE, :width] = jnp.dot(
                    conv_sc[layer], jnp.concatenate(pieces, axis=0), preferred_element_type=f32
                )

        def second_map(g, slot):
            dst = pl.multiple_of(write_at + g * 32, 8)
            half = half_sc[slot, :, :width]
            hidden = half + half * jnp.tanh(half)
            high, low = split(hidden)
            out = jnp.dot(map_sc[layer], high, preferred_element_type=f32)
            low_out = jnp.dot(map_sc[layer, 0:32], low, preferred_element_type=f32)
            term = out[:32] + out[32:] + low_out
            for t in range(width // LANE):
                bit = term[:, t * LANE : (t + 1) * LANE]
                store[t, pl.ds(dst, 32), :] = store[t, pl.ds(dst, 32), :] + (bit + bias)

        first_map(0, 0)
        pairs_whole = (groups - 1) // 2

        def body(i, carry):
            first_map(2 * i + 1, 1)
            second_map(2 * i, 0)
            first_map(2 * i + 2, 0)
            second_map(2 * i + 1, 1)
            return carry

        lax.fori_loop(0, pairs_whole, body, 0)
        done = 2 * pairs_whole
        if groups - done == 2:
            first_map(done + 1, 1)
            second_map(done, 0)
            second_map(done + 1, 1)
        else:
            second_map(done, 0)

    prepare(low_st, -3)
    layer_pass(0, up_st, 0, 640)
    prepare(up_st, -2)
    layer_pass(1, low_st, 8, 640)
    prepare(low_st, -3)
    layer_pass(2, up_st, 0, 512)
    for t in range(4):
        for c in range(4):
            out_ref[c, :, t * LANE : (t + 1) * LANE] = low_st[t, pl.ds(12 + c, 128, stride=4), :]
            out_ref[4 + c, :, t * LANE : (t + 1) * LANE] = up_st[t, pl.ds(8 + c, 128, stride=4), :]


def dft_matrices():
    index = np.arange(LANE)
    angle = 2.0 * np.pi / LANE * (np.outer(index, index) % LANE)
    c = np.cos(angle) / np.sqrt(LANE)
    s = np.sin(angle) / np.sqrt(LANE)
    a = np.block([[c, s], [-s, c]]).astype(np.float32)
    b = np.block([[c, -s], [s, c]]).astype(np.float32)

    def parts(m):
        high = m.astype(jnp.bfloat16)
        low = (m - high.astype(np.float32)).astype(jnp.bfloat16)
        return high, low

    (ah, al), (bh, bl) = parts(a), parts(b)
    left_f = np.concatenate([ah, ah, al], axis=1)
    left_b = np.concatenate([bh, bh, bl], axis=1)
    right_f = np.concatenate([bh, bh, bl], axis=0)
    right_b = np.concatenate([ah, ah, al], axis=0)
    return left_f, left_b, right_f, right_b


def sds(*shape):
    return jax.ShapeDtypeStruct(shape, f32)


def slots_call(*operands):
    anywhere = pl.BlockSpec(memory_space=pl.ANY)
    return pl.pallas_call(
        slots_kernel,
        out_shape=[
            sds(TILES, 8, BAND, LANE),
            sds(41, STRIP, LANE),
            sds(41, STRIP, LANE),
            sds(9, BAND, LANE),
        ],
        in_specs=[smem()] * 3 + [anywhere] * 5 + [vmem()] * 3 + [anywhere] * 4,
        out_specs=[anywhere] * 4,
        scratch_shapes=[
            pltpu.VMEM((TILES, 8, 256, LANE), f32),
            pltpu.VMEM((TILES, 8, 256, LANE), f32),
            pltpu.VMEM((4, 4, 2, LANE, LANE), f32),
            pltpu.VMEM((5, 4, 2, LANE, LANE), f32),
            pltpu.VMEM((256, LANE), f32),
            pltpu.VMEM((256, 768), bf16),
            pltpu.VMEM((256, 768), bf16),
            pltpu.VMEM((768, 256), bf16),
            pltpu.VMEM((768, 256), bf16),
            pltpu.VMEM((4, LANE, LANE), f32),
            pltpu.SemaphoreType.DMA((31,)),
        ],
        compiler_params=params(62),
        name="slots",
    )(*operands)


def denoise_call(u, ev, od, ce, co, taps, conv_bias, output_weight, output_bias):
    anywhere = pl.BlockSpec(memory_space=pl.ANY)
    lines = sds(TILES, 4 * ROWS_KEPT, LANE)
    conv_parts, map_parts, out_bias = pl.pallas_call(
        weights_kernel,
        out_shape=[
            jax.ShapeDtypeStruct((3, LANE, KTOT), bf16),
            jax.ShapeDtypeStruct((3, 64, 256), bf16),
            sds(3, 32, LANE),
        ],
        in_specs=[vmem()] * 4,
        out_specs=[vmem()] * 3,
        compiler_params=params(62),
        cost_estimate=pl.CostEstimate(flops=1 << 20, bytes_accessed=3 << 20, transcendentals=0),
        name="weights",
    )(taps, conv_bias, output_weight, output_bias)
    low, up = pl.pallas_call(
        merge_kernel,
        out_shape=[lines] * 2,
        in_specs=[anywhere] * 3,
        out_specs=[vmem()] * 2,
        scratch_shapes=[
            pltpu.VMEM((TILES, 8, BAND, LANE), f32),
            pltpu.VMEM((41, STRIP, LANE), f32),
            pltpu.VMEM((41, STRIP, LANE), f32),
            pltpu.SemaphoreType.DMA((3,)),
        ],
        compiler_params=params(62),
        cost_estimate=pl.CostEstimate(flops=1 << 20, bytes_accessed=9 << 20, transcendentals=0),
        name="merge",
    )(u, ev, od)
    return pl.pallas_call(
        denoise_kernel,
        out_shape=sds(8, 128, 512),
        in_specs=[anywhere] * 2 + [vmem()] * 5,
        out_specs=vmem(),
        scratch_shapes=[
            pltpu.VMEM((TILES, 4 * ROWS_KEPT, LANE), f32),
            pltpu.VMEM((TILES, 4 * ROWS_KEPT, LANE), f32),
            pltpu.VMEM((3, 3, 4 * ROWS_KEPT, 640), bf16),
            pltpu.VMEM((2, 256, 640), f32),
            pltpu.SemaphoreType.DMA((2,)),
        ],
        compiler_params=params(62),
        name="denoise",
    )(low, up, ce, co, conv_parts, map_parts, out_bias)


def per_device(
    object_field,
    probe_field,
    propagator_phase,
    position_rows,
    position_cols,
    tile_counts,
    intensities,
    conv_weight,
    conv_bias,
    output_weight,
    output_bias,
):
    rows = lax.axis_size("row")
    cols = lax.axis_size("col")

    def pairs(count, start):
        found = []
        for i in range(start, count - 1, 2):
            found += [(i, i + 1), (i + 1, i)]
        return found

    def row_ev(x):
        return lax.ppermute(x, "row", pairs(rows, 0))

    def row_od(x):
        return lax.ppermute(x, "row", pairs(rows, 1))

    def col_ev(x):
        return lax.ppermute(x, "col", pairs(cols, 0))

    def col_od(x):
        return lax.ppermute(x, "col", pairs(cols, 1))

    obj = object_field.reshape(8, 128, 512)
    def edge(index):
        return pl.BlockSpec((8, 128, LANE), lambda i: (0, 0, index))

    def whole(*shape):
        return pl.BlockSpec(shape, lambda i: (0,) * len(shape))

    ce, co = pl.pallas_call(
        pack_kernel,
        out_shape=[sds(8, HALF, LANE)] * 2,
        grid=(1,),
        in_specs=[edge(0), edge(3)],
        out_specs=[whole(8, HALF, LANE)] * 2,
        compiler_params=params(62),
        name="pack",
    )(obj, obj)
    ce = col_ev(ce)
    co = col_od(co)
    anywhere = pl.BlockSpec(memory_space=pl.ANY)
    strip = sds(TILES, 8, HALF, LANE)
    ev, od = pl.pallas_call(
        strips_kernel,
        out_shape=[strip] * 2,
        in_specs=[vmem()],
        out_specs=[vmem()] * 2,
        compiler_params=params(62),
        cost_estimate=pl.CostEstimate(flops=0, bytes_accessed=4 << 20, transcendentals=0),
        name="strips",
    )(obj)
    comb, ev, od = pl.pallas_call(
        comb_kernel,
        out_shape=[sds(8, 128, LANE), strip, strip],
        in_specs=[vmem()] * 2 + [anywhere] * 2,
        out_specs=[anywhere] * 3,
        scratch_shapes=[pltpu.VMEM((8, 128, LANE), f32), pltpu.SemaphoreType.DMA((3,))],
        input_output_aliases={2: 1, 3: 2},
        compiler_params=params(62),
        name="comb",
    )(ce, co, ev, od)
    od = row_od(od)
    ev = row_ev(ev)
    phase_re = jnp.cos(propagator_phase)
    phase_im = jnp.sin(propagator_phase)
    tables = [jnp.asarray(m) for m in dft_matrices()]
    u, ev, od, own = slots_call(
        position_rows.reshape(-1),
        position_cols.reshape(-1),
        tile_counts.reshape(-1),
        obj,
        comb,
        ev,
        od,
        intensities.reshape(4, LANE, LANE),
        probe_field,
        phase_re,
        phase_im,
        *tables,
    )
    od = row_od(od)
    ev = row_ev(ev)
    ce, co = pl.pallas_call(
        sides_kernel,
        out_shape=[sds(9, STRIP, LANE)] * 2,
        in_specs=[anywhere] * 3,
        out_specs=[vmem()] * 2,
        scratch_shapes=[
            pltpu.VMEM((9, BAND, LANE), f32),
            pltpu.VMEM((9, STRIP, LANE), f32),
            pltpu.VMEM((9, STRIP, LANE), f32),
            pltpu.SemaphoreType.DMA((3,)),
        ],
        compiler_params=params(62),
        name="sides",
    )(own, ev, od)
    ce = col_ev(ce)
    co = col_od(co)
    taps = conv_weight.reshape(3, 3, 3, 32, 4).transpose(0, 1, 3, 2, 4).reshape(3, 3, 32, 12)
    out = denoise_call(u, ev, od, ce, co, taps, conv_bias, output_weight, output_bias)
    return out.reshape(4, 2, 128, 512)


def solution(mesh):
    placed = (
        P(None, None, "row", "col"),
        P(),
        P(),
        P("row", "col", None),
        P("row", "col", None),
        P("row", "col"),
        P("row", "col", None, None, None),
        P(),
        P(),
        P(),
        P(),
    )
    return jax.shard_map(
        per_device,
        mesh=mesh,
        in_specs=placed,
        out_specs=P(None, None, "row", "col"),
        check_vma=False,
    )
```

```python
import functools

import jax
import jax.numpy as jnp
import numpy as np
from jax import lax
from jax.experimental import pallas as pl
from jax.experimental.pallas import tpu as pltpu
from jax.sharding import PartitionSpec as P

step_size = 0.02
LANE = 128
HALF = 64
STRIP = 72
BAND = 144
TILES = 5
ROWS_KEPT = 140
ROWS_SET = 138
KTOT = 240

f32 = jnp.float32
bf16 = jnp.bfloat16


def params(mib):
    return pltpu.CompilerParams(vmem_limit_bytes=mib << 20)


def vmem():
    return pl.BlockSpec(memory_space=pltpu.VMEM)


def smem():
    return pl.BlockSpec(memory_space=pltpu.SMEM)


def lanes_of(shape):
    return lax.broadcasted_iota(jnp.int32, shape, len(shape) - 1)


def split(value):
    high = value.astype(bf16)
    low = (value - high.astype(f32)).astype(bf16)
    return high, low


def halves_swapped(value):
    return pltpu.roll(value, HALF, value.ndim - 1)


def pack_kernel(first_ref, last_ref, ce_ref, co_ref):
    col_odd = lax.axis_index("col") % 2
    first = lanes_of((HALF, LANE)) < HALF
    for c in range(8):
        left = first_ref[c]
        right = last_ref[c]
        to_left = jnp.where(first, left[:HALF], halves_swapped(left[HALF:]))
        to_right = jnp.where(first, halves_swapped(right[HALF:]), right[:HALF])
        ce_ref[c] = jnp.where(col_odd == 1, to_left, to_right)
        co_ref[c] = jnp.where(col_odd == 1, to_right, to_left)


def strips_kernel(obj_ref, ev_ref, od_ref):
    row_odd = lax.axis_index("row") % 2
    ev_start = pl.multiple_of((1 - row_odd) * HALF, HALF)
    od_start = pl.multiple_of(row_odd * HALF, HALF)
    for c in range(8):
        for t in range(4):
            ev_ref[t, c] = obj_ref[c, pl.ds(ev_start, HALF), t * LANE : (t + 1) * LANE]
            od_ref[t, c] = obj_ref[c, pl.ds(od_start, HALF), t * LANE : (t + 1) * LANE]


def comb_kernel(ce_any, co_any, ev_in, od_in, comb_ref, ev_ref, od_ref, comb_sc, ce_ref, co_ref, sems):
    del ev_in, od_in
    fetched = [
        pltpu.make_async_copy(ce_any, ce_ref, sems.at[3]),
        pltpu.make_async_copy(co_any, co_ref, sems.at[4]),
    ]
    for item in fetched:
        item.start()
    for item in fetched:
        item.wait()
    row_odd = lax.axis_index("row") % 2
    col_odd = lax.axis_index("col") % 2
    first = lanes_of((HALF, LANE)) < HALF
    for c in range(8):
        ce = ce_ref[c]
        co = co_ref[c]
        from_right = jnp.where(col_odd == 1, co, ce)
        from_left = jnp.where(col_odd == 1, ce, co)
        comb_sc[c, :HALF] = jnp.where(first, from_right, from_left)
        comb_sc[c, HALF:] = halves_swapped(jnp.where(first, from_left, from_right))
    ev_start = pl.multiple_of((1 - row_odd) * HALF, HALF)
    od_start = pl.multiple_of(row_odd * HALF, HALF)
    started = [
        pltpu.make_async_copy(comb_sc.at[:, pl.ds(od_start, HALF), :], od_ref.at[4], sems.at[0]),
        pltpu.make_async_copy(comb_sc.at[:, pl.ds(ev_start, HALF), :], ev_ref.at[4], sems.at[1]),
        pltpu.make_async_copy(comb_sc, comb_ref, sems.at[2]),
    ]
    for item in started:
        item.start()
    for item in started:
        item.wait()


def slots_kernel(
    rows_ref,
    cols_ref,
    count_ref,
    obj_ref,
    comb_ref,
    ev_ref,
    od_ref,
    meas_any,
    probe_ref,
    phase_re_ref,
    phase_im_ref,
    left_f_any,
    left_b_any,
    right_f_any,
    right_b_any,
    u_ref,
    out_ev,
    out_od,
    own_ref,
    frame,
    accum,
    win,
    waves,
    extra,
    left_f_ref,
    left_b_ref,
    right_f_ref,
    right_b_ref,
    meas_ref,
    sems,
):
    row_odd = lax.axis_index("row") % 2
    ev_at = pl.multiple_of((1 - row_odd) * 192, HALF)
    od_at = pl.multiple_of(row_odd * 192, HALF)
    copies = []
    for t in range(4):
        copies.append((obj_ref.at[:, :, t * LANE : (t + 1) * LANE], frame.at[t, :, HALF:192, :]))
    copies.append((comb_ref, frame.at[4, :, HALF:192, :]))
    copies.append((ev_ref, frame.at[:, :, pl.ds(ev_at, HALF), :]))
    copies.append((od_ref, frame.at[:, :, pl.ds(od_at, HALF), :]))
    started = [pltpu.make_async_copy(src, dst, sems.at[i]) for i, (src, dst) in enumerate(copies)]
    late = [
        (left_f_any, left_f_ref),
        (right_f_any, right_f_ref),
        (right_b_any, right_b_ref),
        (left_b_any, left_b_ref),
        (meas_any, meas_ref),
    ]
    later = [pltpu.make_async_copy(src, dst, sems.at[7 + i]) for i, (src, dst) in enumerate(late)]
    for item in started + later:
        item.start()
    accum[...] = jnp.zeros(accum.shape, f32)
    for item in started:
        item.wait()

    lane = lanes_of((LANE, LANE))
    spots = []
    for k in range(4):
        row = rows_ref[k]
        at = lax.rem(cols_ref[k] + (640 - HALF), 640)
        q = at // LANE
        s = at - q * LANE
        nxt = jnp.where(q == 4, 0, q + 1)
        spots.append((row, q, nxt, s))

    for k in range(4):
        row, q, nxt, s = spots[k]
        keep = lane >= s
        turn = jnp.where(s == 0, 0, LANE - s)

        def take(c, carry, k=k, row=row, q=q, nxt=nxt, keep=keep, turn=turn):
            here = frame[q, c, pl.ds(row, LANE), :]
            beyond = frame[nxt, c, pl.ds(row, LANE), :]
            win[c // 2, k, c % 2] = pltpu.roll(jnp.where(keep, here, beyond), turn, 1)
            return carry

        lax.fori_loop(0, 8, take, 0, unroll=8)

    h_re = phase_re_ref[...]
    h_im = phase_im_ref[...]

    def left(xs, mat_ref):
        outs = []
        for g in range(0, 4, 2):
            stack = jnp.concatenate([jnp.concatenate(xs[k], axis=0) for k in (g, g + 1)], axis=1)
            high, low = split(stack)
            out = jnp.dot(
                mat_ref[...], jnp.concatenate([high, low, high], axis=0), preferred_element_type=f32
            )
            outs += [(out[:LANE, at : at + LANE], out[LANE:, at : at + LANE]) for at in (0, LANE)]
        return outs

    def right(xs, mat_ref):
        outs = []
        for g in range(0, 4, 2):
            stack = jnp.concatenate([jnp.concatenate(xs[k], axis=1) for k in (g, g + 1)], axis=0)
            high, low = split(stack)
            out = jnp.dot(
                jnp.concatenate([high, low, high], axis=1), mat_ref[...], preferred_element_type=f32
            )
            outs += [(out[at : at + LANE, :LANE], out[at : at + LANE, LANE:]) for at in (0, LANE)]
        return outs

    def forth(xs):
        return right(left(xs, left_f_ref), right_f_ref)

    def back(xs):
        return left(right(xs, right_b_ref), left_b_ref)

    def times(xs, re, im):
        return [(a * re - b * im, a * im + b * re) for a, b in xs]

    for k in range(4):
        waves[0, k, 0] = probe_ref[0]
        waves[0, k, 1] = probe_ref[1]

    def exit_wave(s):
        xs = []
        for k in range(4):
            p_re, p_im = waves[s, k, 0], waves[s, k, 1]
            o_re, o_im = win[s, k, 0], win[s, k, 1]
            xs.append((p_re * o_re - p_im * o_im, p_re * o_im + p_im * o_re))
        return xs

    def forward(s, carry):
        xs = back(times(forth(exit_wave(s)), h_re, h_im))
        for k in range(4):
            waves[s + 1, k, 0] = xs[k][0]
            waves[s + 1, k, 1] = xs[k][1]
        return carry

    for item in later:
        item.wait()
    lax.fori_loop(0, 3, forward, 0)
    far = forth(exit_wave(3))
    count = count_ref[0]
    seeds = []
    for k in range(4):
        re, im = far[k]
        factor = (re * re + im * im - meas_ref[k]) * (-2.0 * step_size)
        factor = jnp.where(k < count, factor, 0.0)
        seeds.append((factor * re, factor * im))
    gs = back(seeds)
    grad = waves
    for k in range(4):
        grad[4, k, 0] = gs[k][0]
        grad[4, k, 1] = gs[k][1]

    def through(s):
        xs = []
        for k in range(4):
            g_re, g_im = waves[4, k, 0], waves[4, k, 1]
            p_re, p_im = waves[s, k, 0], waves[s, k, 1]
            o_re, o_im = win[s, k, 0], win[s, k, 1]
            win[s, k, 0] = p_re * g_re + p_im * g_im
            win[s, k, 1] = p_re * g_im - p_im * g_re
            xs.append((o_re * g_re + o_im * g_im, o_re * g_im - o_im * g_re))
        return xs

    def backward(i, carry):
        xs = back(times(forth(through(3 - i)), h_re, -h_im))
        for k in range(4):
            waves[4, k, 0] = xs[k][0]
            waves[4, k, 1] = xs[k][1]
        return carry

    lax.fori_loop(0, 3, backward, 0)
    for k in range(4):
        g_re, g_im = waves[4, k, 0], waves[4, k, 1]
        p_re, p_im = probe_ref[0], probe_ref[1]
        win[0, k, 0] = p_re * g_re + p_im * g_im
        win[0, k, 1] = p_re * g_im - p_im * g_re

    for k in range(4):
        row, q, nxt, s = spots[k]
        keep = lane >= s

        def give(c, carry, k=k, row=row, q=q, nxt=nxt, keep=keep, s=s):
            turned = pltpu.roll(win[c // 2, k, c % 2], s, 1)
            here = accum[q, c, pl.ds(row, LANE), :]
            accum[q, c, pl.ds(row, LANE), :] = here + jnp.where(keep, turned, 0.0)
            beyond = accum[nxt, c, pl.ds(row, LANE), :]
            accum[nxt, c, pl.ds(row, LANE), :] = beyond + jnp.where(keep, 0.0, turned)
            return carry

        lax.fori_loop(0, 8, give, 0, unroll=8)

    wide = lanes_of((256, LANE)) // 8
    gathered = jnp.zeros((256, LANE), f32)
    for c in range(8):
        tail = pltpu.roll(accum[3, c], (8 * c + 8) % LANE, 1)
        head = pltpu.roll(accum[0, c], HALF + 8 * c, 1)
        gathered = jnp.where(wide == c, tail, gathered)
        gathered = jnp.where(wide == 8 + c, head, gathered)
    extra[...] = gathered

    ev_from = pl.multiple_of((1 - row_odd) * 184, 8)
    od_from = pl.multiple_of(row_odd * 184, 8)
    moves = [
        (accum.at[4, :, pl.ds(od_from, STRIP), :], out_od.at[0:8]),
        (extra.at[pl.ds(od_from, STRIP), :], out_od.at[8]),
    ]
    for t in range(4):
        moves.append((accum.at[t, :, pl.ds(od_from, STRIP), :], out_od.at[9 + 8 * t : 17 + 8 * t]))
    moves.append((accum.at[4, :, pl.ds(ev_from, STRIP), :], out_ev.at[0:8]))
    moves.append((extra.at[pl.ds(ev_from, STRIP), :], out_ev.at[8]))
    for t in range(4):
        moves.append((accum.at[t, :, pl.ds(ev_from, STRIP), :], out_ev.at[9 + 8 * t : 17 + 8 * t]))
    moves.append((accum.at[4, :, 56:200, :], own_ref.at[0:8]))
    moves.append((extra.at[56:200, :], own_ref.at[8]))
    sent = [pltpu.make_async_copy(src, dst, sems.at[12 + i]) for i, (src, dst) in enumerate(moves)]
    for item in sent:
        item.start()
    for t in range(TILES):
        frame[t, :, 56:200, :] = frame[t, :, 56:200, :] + accum[t, :, 56:200, :]
        item = pltpu.make_async_copy(frame.at[t, :, 56:200, :], u_ref.at[t], sems.at[26 + t])
        item.start()
        sent.append(item)
    for item in sent:
        item.wait()


def sides_kernel(own_any, ev_any, od_any, ce_ref, co_ref, own_ref, evc_ref, odc_ref, sems):
    started = [
        pltpu.make_async_copy(own_any, own_ref, sems.at[0]),
        pltpu.make_async_copy(ev_any.at[0:9], evc_ref, sems.at[1]),
        pltpu.make_async_copy(od_any.at[0:9], odc_ref, sems.at[2]),
    ]
    for item in started:
        item.start()
    for item in started:
        item.wait()
    row_odd = lax.axis_index("row") % 2
    col_odd = lax.axis_index("col") % 2
    first = lanes_of((STRIP, LANE)) < HALF
    for c in range(9):
        ev = evc_ref[c]
        od = odc_ref[c]
        top = own_ref[c, :STRIP] + jnp.where(row_odd == 1, ev, od)
        bottom = halves_swapped(own_ref[c, STRIP:] + jnp.where(row_odd == 1, od, ev))
        to_right = jnp.where(first, top, bottom)
        to_left = jnp.where(first, bottom, top)
        ce_ref[c] = jnp.where(col_odd == 1, to_left, to_right)
        co_ref[c] = jnp.where(col_odd == 1, to_right, to_left)


def weights_kernel(taps_ref, bias_ref, map_ref, map_bias_ref, conv_out, map_out, bias_out):
    def hot(rows, cols, test):
        a = lax.broadcasted_iota(jnp.int32, (rows, cols), 0)
        b = lax.broadcasted_iota(jnp.int32, (rows, cols), 1)
        return jnp.where(test(a, b), 1.0, 0.0).astype(f32)

    def exact(a, b):
        return jnp.dot(a, b, precision=lax.Precision.HIGHEST, preferred_element_type=f32)

    def column(b):
        half = ((b >= 96) & (b < 144)) | ((b >= 192) & (b < 224))
        line = jnp.where(half, b % 8, b % 16)
        dx = jnp.where(half, (b - jnp.where(b < 144, 96, 192)) // 8 % 3, b // 16 % 3)
        k = line // 4 + jnp.where(half, 4, 0)
        return dx * 4 + line % 4, k, b < 216

    def placed(a, b):
        source, _, valid = column(b)
        return valid & (a == source)

    place = hot(12, KTOT, placed)
    row = lax.broadcasted_iota(jnp.int32, (LANE, KTOT), 0)
    col = lax.broadcasted_iota(jnp.int32, (LANE, KTOT), 1)
    _, window_row, is_tap = column(col)
    shift = window_row - row // 32
    is_bias = (col == 224) | (col == 225)
    use_low = ((col >= 144) & (col < 216)) | (col == 225)
    hidden_hot = hot(LANE, 32, lambda a, b: a % 32 == b)
    channel_hot = hot(32, 4, lambda a, b: a % 4 == b)
    spread = hot(32, 256, lambda a, b: a == b % 32)
    same_row = hot(32, 256, lambda a, b: a // 4 == b // 32)
    for layer in range(3):
        bias = jnp.sum(hidden_hot * bias_ref[layer : layer + 1, :], axis=1, keepdims=True)
        total = jnp.where(is_bias, bias, 0.0)
        for dy in range(3):
            part = exact(taps_ref[layer, dy], place)
            whole = jnp.concatenate([part] * 4, axis=0)
            total = total + jnp.where((shift == dy) & is_tap, whole, 0.0)
        high, low = split(total * 0.5)
        conv_out[layer] = jnp.where(use_low, low.astype(f32), high.astype(f32)).astype(bf16)
        wide = exact(exact(channel_hot, map_ref[layer]), spread) * same_row
        high, low = split(wide)
        map_out[layer, 0:32] = high
        map_out[layer, 32:64] = low
        out_bias = jnp.sum(channel_hot * map_bias_ref[layer : layer + 1, :], axis=1, keepdims=True)
        bias_out[layer] = jnp.broadcast_to(out_bias, (32, LANE))


def merge_kernel(u_any, ev_any, od_any, low_st, up_st, u_ref, ev_ref, od_ref, sems):
    pairs = ((u_any, u_ref), (ev_any, ev_ref), (od_any, od_ref))
    started = [pltpu.make_async_copy(a, b, sems.at[i]) for i, (a, b) in enumerate(pairs)]
    for item in started:
        item.start()
    for item in started:
        item.wait()
    row_odd = lax.axis_index("row") % 2

    def combine(t, c):
        plane = c if t == 4 else 9 + 8 * t + c
        ev = ev_ref[plane]
        od = od_ref[plane]
        top = u_ref[t, c, :STRIP] + jnp.where(row_odd == 1, ev, od)
        bottom = u_ref[t, c, STRIP:] + jnp.where(row_odd == 1, od, ev)
        return jnp.concatenate([top, bottom], axis=0)

    for t in range(TILES):
        for c in range(4):
            low_st[t, pl.ds(c, ROWS_SET, stride=4), :] = combine(t, c)[5:143]
            up_st[t, pl.ds(c, ROWS_SET, stride=4), :] = combine(t, 4 + c)[6:144]


def denoise_kernel(
    low_any,
    up_any,
    ce_any,
    co_any,
    conv_sc,
    map_sc,
    bias_ref,
    out_any,
    low_st,
    up_st,
    cond_a,
    cond_b,
    half_sc,
    ce_ref,
    co_ref,
    out_ref,
    sems,
):
    row_id = lax.axis_index("row")
    col_id = lax.axis_index("col")
    col_odd = col_id % 2
    lane = lanes_of((STRIP, LANE))
    first = lane < HALF
    low_copy = pltpu.make_async_copy(low_any, low_st, sems.at[0])
    up_copy = pltpu.make_async_copy(up_any, up_st, sems.at[1])
    side_copies = [
        pltpu.make_async_copy(ce_any, ce_ref, sems.at[2]),
        pltpu.make_async_copy(co_any, co_ref, sems.at[3]),
    ]
    side_copies[0].start()
    side_copies[1].start()
    low_copy.start()
    up_copy.start()

    def add_sides(c):
        store = low_st if c < 4 else up_st
        skip = 5 if c < 4 else 6
        ce = ce_ref[c]
        co = co_ref[c]
        from_left = jnp.where(col_odd == 1, ce, co)
        from_right = jnp.where(col_odd == 1, co, ce)
        swapped_left = halves_swapped(from_left)
        swapped_right = halves_swapped(from_right)
        ce = ce_ref[8]
        co = co_ref[8]
        tail = jnp.where(col_odd == 1, ce, co)
        head = jnp.where(col_odd == 1, co, ce)
        tail_top = pltpu.roll(tail, (120 - 8 * c) % LANE, 1)
        tail_bottom = pltpu.roll(tail, (HALF + 120 - 8 * c) % LANE, 1)
        head_top = pltpu.roll(head, (HALF - 8 * c) % LANE, 1)
        head_bottom = pltpu.roll(head, (LANE - 8 * c) % LANE, 1)
        at_tail = lane >= 120
        at_head = lane < 8
        pieces = {
            0: (jnp.where(first, from_left, 0.0), jnp.where(first, swapped_left, 0.0)),
            3: (jnp.where(first, 0.0, from_right), jnp.where(first, 0.0, swapped_right)),
            4: (
                jnp.where(at_tail, tail_top, jnp.where(at_head, head_top, 0.0)),
                jnp.where(at_tail, tail_bottom, jnp.where(at_head, head_bottom, 0.0)),
            ),
        }
        for t, both in pieces.items():
            at = pl.ds(c % 4, ROWS_SET, stride=4)
            whole = jnp.concatenate(both, axis=0)[skip : skip + ROWS_SET]
            store[t, at, :] = store[t, at, :] + whole

    side_copies[0].wait()
    side_copies[1].wait()
    low_copy.wait()
    for c in range(4):
        add_sides(c)
    up_copy.wait()
    for c in range(4, 8):
        add_sides(c)

    last_row = lax.axis_size("row") - 1
    last_col = lax.axis_size("col") - 1
    right_off = jnp.where(col_id == last_col, 512, 576)
    left_off = jnp.where(col_id == 0, 640, 576)

    def prepare(store, first_row, cond_st):
        row_low = jnp.where(row_id == 0, -first_row * 4, 0)
        row_high = (jnp.where(row_id == last_row, 128, 131) - first_row) * 4

        def body(i, carry):
            at = pl.multiple_of(i * 16, 16)
            x = jnp.concatenate([store[t, pl.ds(at, 16), :] for t in range(TILES)], axis=1)
            column = lax.broadcasted_iota(jnp.int32, x.shape, 1)
            index = lax.broadcasted_iota(jnp.int32, x.shape, 0) + at
            inside = (index >= row_low) & (index < row_high)
            inside = inside & ((column < right_off) | (column >= left_off))
            x = jnp.where(inside, x, 0.0)
            heads = []
            rests = []
            for dx in range(3):
                y = x if dx == 1 else pltpu.roll(x, 1 if dx == 0 else 639, 1)
                high = y.astype(bf16)
                rest = y - high.astype(f32)
                cond_st[0, dx, pl.ds(at, 16), :] = high
                cond_st[1, dx, pl.ds(at, 16), :] = rest.astype(bf16)
                heads.append(y[:8])
                rests.append(rest[:8])
            for i in range(3):
                both = jnp.concatenate((heads + rests)[2 * i : 2 * i + 2], axis=0)
                cond_st[2, i, pl.ds(at, 16), :] = both.astype(bf16)
            return carry

        return body

    ones = jnp.ones((16, 640), bf16)

    def layer_pass(layer, cond_st, store, write_at, width, coming=None):
        groups = 17
        bias = bias_ref[layer]

        def first_map(g, slot):
            for h in range(2):
                here = pl.ds(pl.multiple_of(g * 32 + 16 * h, 16), 16)
                below = pl.ds(pl.multiple_of(g * 32 + 16 * h + 16, 16), 16)
                main = [cond_st[part, dx, here, :width] for part in (0, 1) for dx in range(3)]
                half = [cond_st[2, i, below, :width] for i in range(3)]
                pieces = main + half + main[:3] + half[:2] + [ones[:, :width]]
                half_sc[slot, h * LANE : (h + 1) * LANE, :width] = jnp.dot(
                    conv_sc[layer], jnp.concatenate(pieces, axis=0), preferred_element_type=f32
                )

        def second_map(g, slot):
            dst = pl.multiple_of(write_at + g * 32, 8)
            half = half_sc[slot, :, :width]
            hidden = half + half * jnp.tanh(half)
            high, low = split(hidden)
            out = jnp.dot(map_sc[layer], high, preferred_element_type=f32)
            low_out = jnp.dot(map_sc[layer, 0:32], low, preferred_element_type=f32)
            term = out[:32] + out[32:] + low_out
            for t in range(width // LANE):
                bit = term[:, t * LANE : (t + 1) * LANE]
                store[t, pl.ds(dst, 32), :] = store[t, pl.ds(dst, 32), :] + (bit + bias)

        first_map(0, 0)
        pairs_whole = (groups - 1) // 2

        def body(i, carry):
            if coming is not None:
                for j in range(4):
                    coming(jnp.maximum(4 * i - 4, 0) + j, 0)
            first_map(2 * i + 1, 1)
            second_map(2 * i, 0)
            first_map(2 * i + 2, 0)
            second_map(2 * i + 1, 1)
            return carry

        lax.fori_loop(0, pairs_whole, body, 0)
        second_map(2 * pairs_whole, 0)
        if coming is not None:
            for j in range(28, 35):
                coming(j, 0)

    def finish(store, skip, at, sem):
        for t in range(4):
            for c in range(4):
                lines = store[t, pl.ds(skip + c, 128, stride=4), :]
                out_ref[at + c, :, t * LANE : (t + 1) * LANE] = lines
        copy = pltpu.make_async_copy(out_ref.at[at : at + 4], out_any.at[at : at + 4], sem)
        copy.start()
        return copy

    lax.fori_loop(0, 35, prepare(low_st, -3, cond_a), 0, unroll=7)
    layer_pass(0, cond_a, up_st, 0, 640, prepare(up_st, -2, cond_b))
    layer_pass(1, cond_b, low_st, 8, 640, prepare(low_st, -3, cond_a))
    low_out = finish(low_st, 12, 0, sems.at[4])
    layer_pass(2, cond_a, up_st, 0, 512)
    up_out = finish(up_st, 8, 4, sems.at[5])
    low_out.wait()
    up_out.wait()


def dft_matrices():
    index = np.arange(LANE)
    angle = 2.0 * np.pi / LANE * (np.outer(index, index) % LANE)
    c = np.cos(angle) / np.sqrt(LANE)
    s = np.sin(angle) / np.sqrt(LANE)
    a = np.block([[c, s], [-s, c]]).astype(np.float32)
    b = np.block([[c, -s], [s, c]]).astype(np.float32)

    def parts(m):
        high = m.astype(jnp.bfloat16)
        low = (m - high.astype(np.float32)).astype(jnp.bfloat16)
        return high, low

    (ah, al), (bh, bl) = parts(a), parts(b)
    left_f = np.concatenate([ah, ah, al], axis=1)
    left_b = np.concatenate([bh, bh, bl], axis=1)
    right_f = np.concatenate([bh, bh, bl], axis=0)
    right_b = np.concatenate([ah, ah, al], axis=0)
    return left_f, left_b, right_f, right_b


def sds(*shape):
    return jax.ShapeDtypeStruct(shape, f32)


def slots_call(*operands):
    anywhere = pl.BlockSpec(memory_space=pl.ANY)
    return pl.pallas_call(
        slots_kernel,
        out_shape=[
            sds(TILES, 8, BAND, LANE),
            sds(41, STRIP, LANE),
            sds(41, STRIP, LANE),
            sds(9, BAND, LANE),
        ],
        in_specs=[smem()] * 3 + [anywhere] * 5 + [vmem()] * 3 + [anywhere] * 4,
        out_specs=[anywhere] * 4,
        scratch_shapes=[
            pltpu.VMEM((TILES, 8, 256, LANE), f32),
            pltpu.VMEM((TILES, 8, 256, LANE), f32),
            pltpu.VMEM((4, 4, 2, LANE, LANE), f32),
            pltpu.VMEM((5, 4, 2, LANE, LANE), f32),
            pltpu.VMEM((256, LANE), f32),
            pltpu.VMEM((256, 768), bf16),
            pltpu.VMEM((256, 768), bf16),
            pltpu.VMEM((768, 256), bf16),
            pltpu.VMEM((768, 256), bf16),
            pltpu.VMEM((4, LANE, LANE), f32),
            pltpu.SemaphoreType.DMA((31,)),
        ],
        compiler_params=params(62),
        name="slots",
    )(*operands)


def denoise_call(u, ev, od, ce, co, taps, conv_bias, output_weight, output_bias):
    anywhere = pl.BlockSpec(memory_space=pl.ANY)
    lines = sds(TILES, 4 * ROWS_KEPT, LANE)
    conv_parts, map_parts, out_bias = pl.pallas_call(
        weights_kernel,
        out_shape=[
            jax.ShapeDtypeStruct((3, LANE, KTOT), bf16),
            jax.ShapeDtypeStruct((3, 64, 256), bf16),
            sds(3, 32, LANE),
        ],
        in_specs=[vmem()] * 4,
        out_specs=[vmem()] * 3,
        compiler_params=params(62),
        cost_estimate=pl.CostEstimate(flops=1 << 20, bytes_accessed=3 << 20, transcendentals=0),
        name="weights",
    )(taps, conv_bias, output_weight, output_bias)
    low, up = pl.pallas_call(
        merge_kernel,
        out_shape=[lines] * 2,
        in_specs=[anywhere] * 3,
        out_specs=[vmem()] * 2,
        scratch_shapes=[
            pltpu.VMEM((TILES, 8, BAND, LANE), f32),
            pltpu.VMEM((41, STRIP, LANE), f32),
            pltpu.VMEM((41, STRIP, LANE), f32),
            pltpu.SemaphoreType.DMA((3,)),
        ],
        compiler_params=params(62),
        cost_estimate=pl.CostEstimate(flops=1 << 20, bytes_accessed=9 << 20, transcendentals=0),
        name="merge",
    )(u, ev, od)
    return pl.pallas_call(
        denoise_kernel,
        out_shape=sds(8, 128, 512),
        in_specs=[anywhere] * 4 + [vmem()] * 3,
        out_specs=anywhere,
        scratch_shapes=[
            pltpu.VMEM((TILES, 4 * ROWS_KEPT, LANE), f32),
            pltpu.VMEM((TILES, 4 * ROWS_KEPT, LANE), f32),
            pltpu.VMEM((3, 3, 4 * ROWS_KEPT, 640), bf16),
            pltpu.VMEM((3, 3, 4 * ROWS_KEPT, 640), bf16),
            pltpu.VMEM((2, 256, 640), f32),
            pltpu.VMEM((9, STRIP, LANE), f32),
            pltpu.VMEM((9, STRIP, LANE), f32),
            pltpu.VMEM((8, 128, 512), f32),
            pltpu.SemaphoreType.DMA((6,)),
        ],
        compiler_params=params(62),
        name="denoise",
    )(low, up, ce, co, conv_parts, map_parts, out_bias)


def per_device(
    object_field,
    probe_field,
    propagator_phase,
    position_rows,
    position_cols,
    tile_counts,
    intensities,
    conv_weight,
    conv_bias,
    output_weight,
    output_bias,
):
    rows = lax.axis_size("row")
    cols = lax.axis_size("col")

    def pairs(count, start):
        found = []
        for i in range(start, count - 1, 2):
            found += [(i, i + 1), (i + 1, i)]
        return found

    def row_ev(x):
        return lax.ppermute(x, "row", pairs(rows, 0))

    def row_od(x):
        return lax.ppermute(x, "row", pairs(rows, 1))

    def col_ev(x):
        return lax.ppermute(x, "col", pairs(cols, 0))

    def col_od(x):
        return lax.ppermute(x, "col", pairs(cols, 1))

    obj = object_field.reshape(8, 128, 512)
    def edge(index):
        return pl.BlockSpec((8, 128, LANE), lambda i: (0, 0, index))

    def whole(*shape):
        return pl.BlockSpec(shape, lambda i: (0,) * len(shape))

    ce, co = pl.pallas_call(
        pack_kernel,
        out_shape=[sds(8, HALF, LANE)] * 2,
        grid=(1,),
        in_specs=[edge(0), edge(3)],
        out_specs=[whole(8, HALF, LANE)] * 2,
        compiler_params=params(62),
        name="pack",
    )(obj, obj)
    ce = col_ev(ce)
    co = col_od(co)
    anywhere = pl.BlockSpec(memory_space=pl.ANY)
    strip = sds(TILES, 8, HALF, LANE)
    ev, od = pl.pallas_call(
        strips_kernel,
        out_shape=[strip] * 2,
        in_specs=[vmem()],
        out_specs=[vmem()] * 2,
        compiler_params=params(62),
        cost_estimate=pl.CostEstimate(flops=0, bytes_accessed=4 << 20, transcendentals=0),
        name="strips",
    )(obj)
    comb, ev, od = pl.pallas_call(
        comb_kernel,
        out_shape=[sds(8, 128, LANE), strip, strip],
        in_specs=[anywhere] * 4,
        out_specs=[anywhere] * 3,
        scratch_shapes=[
            pltpu.VMEM((8, 128, LANE), f32),
            pltpu.VMEM((8, HALF, LANE), f32),
            pltpu.VMEM((8, HALF, LANE), f32),
            pltpu.SemaphoreType.DMA((5,)),
        ],
        input_output_aliases={2: 1, 3: 2},
        compiler_params=params(62),
        name="comb",
    )(ce, co, ev, od)
    od = row_od(od)
    ev = row_ev(ev)
    phase_re = jnp.cos(propagator_phase)
    phase_im = jnp.sin(propagator_phase)
    tables = [jnp.asarray(m) for m in dft_matrices()]
    u, ev, od, own = slots_call(
        position_rows.reshape(-1),
        position_cols.reshape(-1),
        tile_counts.reshape(-1),
        obj,
        comb,
        ev,
        od,
        intensities.reshape(4, LANE, LANE),
        probe_field,
        phase_re,
        phase_im,
        *tables,
    )
    od = row_od(od)
    ev = row_ev(ev)
    ce, co = pl.pallas_call(
        sides_kernel,
        out_shape=[sds(9, STRIP, LANE)] * 2,
        in_specs=[anywhere] * 3,
        out_specs=[vmem()] * 2,
        scratch_shapes=[
            pltpu.VMEM((9, BAND, LANE), f32),
            pltpu.VMEM((9, STRIP, LANE), f32),
            pltpu.VMEM((9, STRIP, LANE), f32),
            pltpu.SemaphoreType.DMA((3,)),
        ],
        compiler_params=params(62),
        name="sides",
    )(own, ev, od)
    ce = col_ev(ce)
    co = col_od(co)
    taps = conv_weight.reshape(3, 3, 3, 32, 4).transpose(0, 1, 3, 2, 4).reshape(3, 3, 32, 12)
    out = denoise_call(u, ev, od, ce, co, taps, conv_bias, output_weight, output_bias)
    return out.reshape(4, 2, 128, 512)


def solution(mesh):
    placed = (
        P(None, None, "row", "col"),
        P(),
        P(),
        P("row", "col", None),
        P("row", "col", None),
        P("row", "col"),
        P("row", "col", None, None, None),
        P(),
        P(),
        P(),
        P(),
    )
    return jax.shard_map(
        per_device,
        mesh=mesh,
        in_specs=placed,
        out_specs=P(None, None, "row", "col"),
        check_vma=False,
    )
```

```python
import functools

import jax
import jax.numpy as jnp
import numpy as np
from jax import lax
from jax.experimental import pallas as pl
from jax.experimental.pallas import tpu as pltpu
from jax.sharding import PartitionSpec as P

step_size = 0.02
LANE = 128
HALF = 64
STRIP = 72
BAND = 144
TILES = 5
ROWS_KEPT = 140
ROWS_SET = 138
KTOT = 240

f32 = jnp.float32
bf16 = jnp.bfloat16


def params(mib):
    return pltpu.CompilerParams(vmem_limit_bytes=mib << 20)


def vmem():
    return pl.BlockSpec(memory_space=pltpu.VMEM)


def smem():
    return pl.BlockSpec(memory_space=pltpu.SMEM)


def lanes_of(shape):
    return lax.broadcasted_iota(jnp.int32, shape, len(shape) - 1)


def split(value):
    high = value.astype(bf16)
    low = (value - high.astype(f32)).astype(bf16)
    return high, low


def halves_swapped(value):
    return pltpu.roll(value, HALF, value.ndim - 1)


def pack_kernel(first_ref, last_ref, ce_ref, co_ref):
    col_odd = lax.axis_index("col") % 2
    first = lanes_of((HALF, LANE)) < HALF
    for c in range(8):
        left = first_ref[c]
        right = last_ref[c]
        to_left = jnp.where(first, left[:HALF], halves_swapped(left[HALF:]))
        to_right = jnp.where(first, halves_swapped(right[HALF:]), right[:HALF])
        ce_ref[c] = jnp.where(col_odd == 1, to_left, to_right)
        co_ref[c] = jnp.where(col_odd == 1, to_right, to_left)


def strips_kernel(obj_ref, ev_ref, od_ref):
    row_odd = lax.axis_index("row") % 2
    ev_start = pl.multiple_of((1 - row_odd) * HALF, HALF)
    od_start = pl.multiple_of(row_odd * HALF, HALF)
    for c in range(8):
        for t in range(4):
            ev_ref[t, c] = obj_ref[c, pl.ds(ev_start, HALF), t * LANE : (t + 1) * LANE]
            od_ref[t, c] = obj_ref[c, pl.ds(od_start, HALF), t * LANE : (t + 1) * LANE]


def comb_kernel(ce_any, co_any, ev_in, od_in, comb_ref, ev_ref, od_ref, comb_sc, ce_ref, co_ref, sems):
    del ev_in, od_in
    fetched = [
        pltpu.make_async_copy(ce_any, ce_ref, sems.at[3]),
        pltpu.make_async_copy(co_any, co_ref, sems.at[4]),
    ]
    for item in fetched:
        item.start()
    for item in fetched:
        item.wait()
    row_odd = lax.axis_index("row") % 2
    col_odd = lax.axis_index("col") % 2
    first = lanes_of((HALF, LANE)) < HALF
    for c in range(8):
        ce = ce_ref[c]
        co = co_ref[c]
        from_right = jnp.where(col_odd == 1, co, ce)
        from_left = jnp.where(col_odd == 1, ce, co)
        comb_sc[c, :HALF] = jnp.where(first, from_right, from_left)
        comb_sc[c, HALF:] = halves_swapped(jnp.where(first, from_left, from_right))
    ev_start = pl.multiple_of((1 - row_odd) * HALF, HALF)
    od_start = pl.multiple_of(row_odd * HALF, HALF)
    started = [
        pltpu.make_async_copy(comb_sc.at[:, pl.ds(od_start, HALF), :], od_ref.at[4], sems.at[0]),
        pltpu.make_async_copy(comb_sc.at[:, pl.ds(ev_start, HALF), :], ev_ref.at[4], sems.at[1]),
        pltpu.make_async_copy(comb_sc, comb_ref, sems.at[2]),
    ]
    for item in started:
        item.start()
    for item in started:
        item.wait()


def slots_kernel(
    rows_ref,
    cols_ref,
    count_ref,
    obj_ref,
    comb_ref,
    ev_ref,
    od_ref,
    meas_any,
    probe_ref,
    phase_re_ref,
    phase_im_ref,
    left_f_any,
    left_b_any,
    right_f_any,
    right_b_any,
    u_ref,
    out_ev,
    out_odc,
    out_odm,
    own_ref,
    frame,
    accum,
    win,
    waves,
    extra,
    left_f_ref,
    left_b_ref,
    right_f_ref,
    right_b_ref,
    meas_ref,
    sems,
):
    row_odd = lax.axis_index("row") % 2
    ev_at = pl.multiple_of((1 - row_odd) * 192, HALF)
    od_at = pl.multiple_of(row_odd * 192, HALF)
    copies = []
    for t in range(4):
        copies.append((obj_ref.at[:, :, t * LANE : (t + 1) * LANE], frame.at[t, :, HALF:192, :]))
    copies.append((comb_ref, frame.at[4, :, HALF:192, :]))
    copies.append((ev_ref, frame.at[:, :, pl.ds(ev_at, HALF), :]))
    copies.append((od_ref, frame.at[:, :, pl.ds(od_at, HALF), :]))
    started = [pltpu.make_async_copy(src, dst, sems.at[i]) for i, (src, dst) in enumerate(copies)]
    late = [
        (left_f_any, left_f_ref),
        (right_f_any, right_f_ref),
        (right_b_any, right_b_ref),
        (left_b_any, left_b_ref),
        (meas_any, meas_ref),
    ]
    later = [pltpu.make_async_copy(src, dst, sems.at[7 + i]) for i, (src, dst) in enumerate(late)]
    for item in started + later:
        item.start()
    accum[...] = jnp.zeros(accum.shape, f32)
    for item in started:
        item.wait()

    lane = lanes_of((LANE, LANE))
    spots = []
    for k in range(4):
        row = rows_ref[k]
        at = lax.rem(cols_ref[k] + (640 - HALF), 640)
        q = at // LANE
        s = at - q * LANE
        nxt = jnp.where(q == 4, 0, q + 1)
        spots.append((row, q, nxt, s))

    for k in range(4):
        row, q, nxt, s = spots[k]
        keep = lane >= s
        turn = jnp.where(s == 0, 0, LANE - s)

        def take(c, carry, k=k, row=row, q=q, nxt=nxt, keep=keep, turn=turn):
            here = frame[q, c, pl.ds(row, LANE), :]
            beyond = frame[nxt, c, pl.ds(row, LANE), :]
            win[c // 2, k, c % 2] = pltpu.roll(jnp.where(keep, here, beyond), turn, 1)
            return carry

        lax.fori_loop(0, 8, take, 0, unroll=8)

    h_re = phase_re_ref[...]
    h_im = phase_im_ref[...]

    def left(xs, mat_ref):
        outs = []
        for g in range(0, 4, 2):
            stack = jnp.concatenate([jnp.concatenate(xs[k], axis=0) for k in (g, g + 1)], axis=1)
            high, low = split(stack)
            out = jnp.dot(
                mat_ref[...], jnp.concatenate([high, low, high], axis=0), preferred_element_type=f32
            )
            outs += [(out[:LANE, at : at + LANE], out[LANE:, at : at + LANE]) for at in (0, LANE)]
        return outs

    def right(xs, mat_ref):
        outs = []
        for g in range(0, 4, 2):
            stack = jnp.concatenate([jnp.concatenate(xs[k], axis=1) for k in (g, g + 1)], axis=0)
            high, low = split(stack)
            out = jnp.dot(
                jnp.concatenate([high, low, high], axis=1), mat_ref[...], preferred_element_type=f32
            )
            outs += [(out[at : at + LANE, :LANE], out[at : at + LANE, LANE:]) for at in (0, LANE)]
        return outs

    def forth(xs):
        return right(left(xs, left_f_ref), right_f_ref)

    def back(xs):
        return left(right(xs, right_b_ref), left_b_ref)

    def times(xs, re, im):
        return [(a * re - b * im, a * im + b * re) for a, b in xs]

    for k in range(4):
        waves[0, k, 0] = probe_ref[0]
        waves[0, k, 1] = probe_ref[1]

    def exit_wave(s):
        xs = []
        for k in range(4):
            p_re, p_im = waves[s, k, 0], waves[s, k, 1]
            o_re, o_im = win[s, k, 0], win[s, k, 1]
            xs.append((p_re * o_re - p_im * o_im, p_re * o_im + p_im * o_re))
        return xs

    def forward(s, carry):
        xs = back(times(forth(exit_wave(s)), h_re, h_im))
        for k in range(4):
            waves[s + 1, k, 0] = xs[k][0]
            waves[s + 1, k, 1] = xs[k][1]
        return carry

    for item in later:
        item.wait()
    lax.fori_loop(0, 3, forward, 0)
    far = forth(exit_wave(3))
    count = count_ref[0]
    seeds = []
    for k in range(4):
        re, im = far[k]
        factor = (re * re + im * im - meas_ref[k]) * (-2.0 * step_size)
        factor = jnp.where(k < count, factor, 0.0)
        seeds.append((factor * re, factor * im))
    gs = back(seeds)
    grad = waves
    for k in range(4):
        grad[4, k, 0] = gs[k][0]
        grad[4, k, 1] = gs[k][1]

    def through(s):
        xs = []
        for k in range(4):
            g_re, g_im = waves[4, k, 0], waves[4, k, 1]
            p_re, p_im = waves[s, k, 0], waves[s, k, 1]
            o_re, o_im = win[s, k, 0], win[s, k, 1]
            win[s, k, 0] = p_re * g_re + p_im * g_im
            win[s, k, 1] = p_re * g_im - p_im * g_re
            xs.append((o_re * g_re + o_im * g_im, o_re * g_im - o_im * g_re))
        return xs

    def backward(i, carry):
        xs = back(times(forth(through(3 - i)), h_re, -h_im))
        for k in range(4):
            waves[4, k, 0] = xs[k][0]
            waves[4, k, 1] = xs[k][1]
        return carry

    lax.fori_loop(0, 3, backward, 0)
    for k in range(4):
        g_re, g_im = waves[4, k, 0], waves[4, k, 1]
        p_re, p_im = probe_ref[0], probe_ref[1]
        win[0, k, 0] = p_re * g_re + p_im * g_im
        win[0, k, 1] = p_re * g_im - p_im * g_re

    for k in range(4):
        row, q, nxt, s = spots[k]
        keep = lane >= s

        def give(c, carry, k=k, row=row, q=q, nxt=nxt, keep=keep, s=s):
            turned = pltpu.roll(win[c // 2, k, c % 2], s, 1)
            here = accum[q, c, pl.ds(row, LANE), :]
            accum[q, c, pl.ds(row, LANE), :] = here + jnp.where(keep, turned, 0.0)
            beyond = accum[nxt, c, pl.ds(row, LANE), :]
            accum[nxt, c, pl.ds(row, LANE), :] = beyond + jnp.where(keep, 0.0, turned)
            return carry

        lax.fori_loop(0, 8, give, 0, unroll=8)

    wide = lanes_of((256, LANE)) // 8
    gathered = jnp.zeros((256, LANE), f32)
    for c in range(8):
        tail = pltpu.roll(accum[3, c], (8 * c + 8) % LANE, 1)
        head = pltpu.roll(accum[0, c], HALF + 8 * c, 1)
        gathered = jnp.where(wide == c, tail, gathered)
        gathered = jnp.where(wide == 8 + c, head, gathered)
    extra[...] = gathered

    ev_from = pl.multiple_of((1 - row_odd) * 184, 8)
    od_from = pl.multiple_of(row_odd * 184, 8)
    moves = [
        (accum.at[4, :, pl.ds(od_from, STRIP), :], out_odc.at[0:8]),
        (extra.at[pl.ds(od_from, STRIP), :], out_odc.at[8]),
    ]
    for t in range(4):
        moves.append((accum.at[t, :, pl.ds(od_from, STRIP), :], out_odm.at[8 * t : 8 * t + 8]))
    moves.append((accum.at[4, :, pl.ds(ev_from, STRIP), :], out_ev.at[0:8]))
    moves.append((extra.at[pl.ds(ev_from, STRIP), :], out_ev.at[8]))
    for t in range(4):
        moves.append((accum.at[t, :, pl.ds(ev_from, STRIP), :], out_ev.at[9 + 8 * t : 17 + 8 * t]))
    moves.append((accum.at[4, :, 56:200, :], own_ref.at[0:8]))
    moves.append((extra.at[56:200, :], own_ref.at[8]))
    sent = [pltpu.make_async_copy(src, dst, sems.at[12 + i]) for i, (src, dst) in enumerate(moves)]
    for item in sent:
        item.start()
    for t in range(TILES):
        frame[t, :, 56:200, :] = frame[t, :, 56:200, :] + accum[t, :, 56:200, :]
        item = pltpu.make_async_copy(frame.at[t, :, 56:200, :], u_ref.at[t], sems.at[26 + t])
        item.start()
        sent.append(item)
    for item in sent:
        item.wait()


def sides_kernel(own_any, ev_any, odc_any, ce_ref, co_ref, own_ref, evc_ref, odc_ref, sems):
    started = [
        pltpu.make_async_copy(own_any, own_ref, sems.at[0]),
        pltpu.make_async_copy(ev_any.at[0:9], evc_ref, sems.at[1]),
        pltpu.make_async_copy(odc_any, odc_ref, sems.at[2]),
    ]
    for item in started:
        item.start()
    for item in started:
        item.wait()
    row_odd = lax.axis_index("row") % 2
    col_odd = lax.axis_index("col") % 2
    first = lanes_of((STRIP, LANE)) < HALF
    for c in range(9):
        ev = evc_ref[c]
        od = odc_ref[c]
        top = own_ref[c, :STRIP] + jnp.where(row_odd == 1, ev, od)
        bottom = halves_swapped(own_ref[c, STRIP:] + jnp.where(row_odd == 1, od, ev))
        to_right = jnp.where(first, top, bottom)
        to_left = jnp.where(first, bottom, top)
        ce_ref[c] = jnp.where(col_odd == 1, to_left, to_right)
        co_ref[c] = jnp.where(col_odd == 1, to_right, to_left)


def weights_kernel(taps_ref, bias_ref, map_ref, map_bias_ref, conv_out, map_out, bias_out):
    def hot(rows, cols, test):
        a = lax.broadcasted_iota(jnp.int32, (rows, cols), 0)
        b = lax.broadcasted_iota(jnp.int32, (rows, cols), 1)
        return jnp.where(test(a, b), 1.0, 0.0).astype(f32)

    def exact(a, b):
        return jnp.dot(a, b, precision=lax.Precision.HIGHEST, preferred_element_type=f32)

    def column(b):
        half = ((b >= 96) & (b < 144)) | ((b >= 192) & (b < 224))
        line = jnp.where(half, b % 8, b % 16)
        dx = jnp.where(half, (b - jnp.where(b < 144, 96, 192)) // 8 % 3, b // 16 % 3)
        k = line // 4 + jnp.where(half, 4, 0)
        return dx * 4 + line % 4, k, b < 216

    def placed(a, b):
        source, _, valid = column(b)
        return valid & (a == source)

    place = hot(12, KTOT, placed)
    row = lax.broadcasted_iota(jnp.int32, (LANE, KTOT), 0)
    col = lax.broadcasted_iota(jnp.int32, (LANE, KTOT), 1)
    _, window_row, is_tap = column(col)
    shift = window_row - row // 32
    is_bias = (col == 224) | (col == 225)
    use_low = ((col >= 144) & (col < 216)) | (col == 225)
    hidden_hot = hot(LANE, 32, lambda a, b: a % 32 == b)
    channel_hot = hot(32, 4, lambda a, b: a % 4 == b)
    spread = hot(32, 256, lambda a, b: a == b % 32)
    same_row = hot(32, 256, lambda a, b: a // 4 == b // 32)
    for layer in range(3):
        bias = jnp.sum(hidden_hot * bias_ref[layer : layer + 1, :], axis=1, keepdims=True)
        total = jnp.where(is_bias, bias, 0.0)
        for dy in range(3):
            part = exact(taps_ref[layer, dy], place)
            whole = jnp.concatenate([part] * 4, axis=0)
            total = total + jnp.where((shift == dy) & is_tap, whole, 0.0)
        high, low = split(total * 0.5)
        conv_out[layer] = jnp.where(use_low, low.astype(f32), high.astype(f32)).astype(bf16)
        wide = exact(exact(channel_hot, map_ref[layer]), spread) * same_row
        high, low = split(wide)
        map_out[layer, 0:32] = high
        map_out[layer, 32:64] = low
        out_bias = jnp.sum(channel_hot * map_bias_ref[layer : layer + 1, :], axis=1, keepdims=True)
        bias_out[layer] = jnp.broadcast_to(out_bias, (32, LANE))


def merge_kernel(u_any, ev_any, odc_any, odm_any, low_st, up_st, u_ref, ev_ref, od_ref, sems):
    pairs = (
        (u_any, u_ref),
        (ev_any, ev_ref),
        (odc_any, od_ref.at[0:9]),
        (odm_any, od_ref.at[9:41]),
    )
    started = [pltpu.make_async_copy(a, b, sems.at[i]) for i, (a, b) in enumerate(pairs)]
    for item in started:
        item.start()
    for item in started:
        item.wait()
    row_odd = lax.axis_index("row") % 2

    def combine(t, c):
        plane = c if t == 4 else 9 + 8 * t + c
        ev = ev_ref[plane]
        od = od_ref[plane]
        top = u_ref[t, c, :STRIP] + jnp.where(row_odd == 1, ev, od)
        bottom = u_ref[t, c, STRIP:] + jnp.where(row_odd == 1, od, ev)
        return jnp.concatenate([top, bottom], axis=0)

    for t in range(TILES):
        for c in range(4):
            low_st[t, pl.ds(c, ROWS_SET, stride=4), :] = combine(t, c)[5:143]
            up_st[t, pl.ds(c, ROWS_SET, stride=4), :] = combine(t, 4 + c)[6:144]


def denoise_kernel(
    low_any,
    up_any,
    ce_any,
    co_any,
    conv_sc,
    map_sc,
    bias_ref,
    out_any,
    low_st,
    up_st,
    cond_a,
    cond_b,
    half_sc,
    ce_ref,
    co_ref,
    out_ref,
    sems,
):
    row_id = lax.axis_index("row")
    col_id = lax.axis_index("col")
    col_odd = col_id % 2
    lane = lanes_of((STRIP, LANE))
    first = lane < HALF
    low_copy = pltpu.make_async_copy(low_any, low_st, sems.at[0])
    up_copy = pltpu.make_async_copy(up_any, up_st, sems.at[1])
    side_copies = [
        pltpu.make_async_copy(ce_any, ce_ref, sems.at[2]),
        pltpu.make_async_copy(co_any, co_ref, sems.at[3]),
    ]
    side_copies[0].start()
    side_copies[1].start()
    low_copy.start()
    up_copy.start()

    def add_sides(c):
        store = low_st if c < 4 else up_st
        skip = 5 if c < 4 else 6
        ce = ce_ref[c]
        co = co_ref[c]
        from_left = jnp.where(col_odd == 1, ce, co)
        from_right = jnp.where(col_odd == 1, co, ce)
        swapped_left = halves_swapped(from_left)
        swapped_right = halves_swapped(from_right)
        ce = ce_ref[8]
        co = co_ref[8]
        tail = jnp.where(col_odd == 1, ce, co)
        head = jnp.where(col_odd == 1, co, ce)
        tail_top = pltpu.roll(tail, (120 - 8 * c) % LANE, 1)
        tail_bottom = pltpu.roll(tail, (HALF + 120 - 8 * c) % LANE, 1)
        head_top = pltpu.roll(head, (HALF - 8 * c) % LANE, 1)
        head_bottom = pltpu.roll(head, (LANE - 8 * c) % LANE, 1)
        at_tail = lane >= 120
        at_head = lane < 8
        pieces = {
            0: (jnp.where(first, from_left, 0.0), jnp.where(first, swapped_left, 0.0)),
            3: (jnp.where(first, 0.0, from_right), jnp.where(first, 0.0, swapped_right)),
            4: (
                jnp.where(at_tail, tail_top, jnp.where(at_head, head_top, 0.0)),
                jnp.where(at_tail, tail_bottom, jnp.where(at_head, head_bottom, 0.0)),
            ),
        }
        for t, both in pieces.items():
            at = pl.ds(c % 4, ROWS_SET, stride=4)
            whole = jnp.concatenate(both, axis=0)[skip : skip + ROWS_SET]
            store[t, at, :] = store[t, at, :] + whole

    side_copies[0].wait()
    side_copies[1].wait()
    low_copy.wait()
    for c in range(4):
        add_sides(c)
    up_copy.wait()
    for c in range(4, 8):
        add_sides(c)

    last_row = lax.axis_size("row") - 1
    last_col = lax.axis_size("col") - 1
    right_off = jnp.where(col_id == last_col, 512, 576)
    left_off = jnp.where(col_id == 0, 640, 576)

    def prepare(store, first_row, cond_st):
        row_low = jnp.where(row_id == 0, -first_row * 4, 0)
        row_high = (jnp.where(row_id == last_row, 128, 131) - first_row) * 4

        def body(i, carry):
            at = pl.multiple_of(i * 16, 16)
            x = jnp.concatenate([store[t, pl.ds(at, 16), :] for t in range(TILES)], axis=1)
            column = lax.broadcasted_iota(jnp.int32, x.shape, 1)
            index = lax.broadcasted_iota(jnp.int32, x.shape, 0) + at
            inside = (index >= row_low) & (index < row_high)
            inside = inside & ((column < right_off) | (column >= left_off))
            x = jnp.where(inside, x, 0.0)
            heads = []
            rests = []
            for dx in range(3):
                y = x if dx == 1 else pltpu.roll(x, 1 if dx == 0 else 639, 1)
                high = y.astype(bf16)
                rest = y - high.astype(f32)
                cond_st[0, dx, pl.ds(at, 16), :] = high
                cond_st[1, dx, pl.ds(at, 16), :] = rest.astype(bf16)
                heads.append(y[:8])
                rests.append(rest[:8])
            for i in range(3):
                both = jnp.concatenate((heads + rests)[2 * i : 2 * i + 2], axis=0)
                cond_st[2, i, pl.ds(at, 16), :] = both.astype(bf16)
            return carry

        return body

    ones = jnp.ones((16, 640), bf16)

    def layer_pass(layer, cond_st, store, write_at, width, coming=None):
        groups = 17
        bias = bias_ref[layer]

        def first_map(g, slot):
            for h in range(2):
                here = pl.ds(pl.multiple_of(g * 32 + 16 * h, 16), 16)
                below = pl.ds(pl.multiple_of(g * 32 + 16 * h + 16, 16), 16)
                main = [cond_st[part, dx, here, :width] for part in (0, 1) for dx in range(3)]
                half = [cond_st[2, i, below, :width] for i in range(3)]
                pieces = main + half + main[:3] + half[:2] + [ones[:, :width]]
                half_sc[slot, h * LANE : (h + 1) * LANE, :width] = jnp.dot(
                    conv_sc[layer], jnp.concatenate(pieces, axis=0), preferred_element_type=f32
                )

        def second_map(g, slot):
            dst = pl.multiple_of(write_at + g * 32, 8)
            half = half_sc[slot, :, :width]
            hidden = half + half * jnp.tanh(half)
            high, low = split(hidden)
            out = jnp.dot(map_sc[layer], high, preferred_element_type=f32)
            low_out = jnp.dot(map_sc[layer, 0:32], low, preferred_element_type=f32)
            term = out[:32] + out[32:] + low_out
            for t in range(width // LANE):
                bit = term[:, t * LANE : (t + 1) * LANE]
                store[t, pl.ds(dst, 32), :] = store[t, pl.ds(dst, 32), :] + (bit + bias)

        first_map(0, 0)
        pairs_whole = (groups - 1) // 2

        def body(i, carry):
            if coming is not None:
                for j in range(4):
                    coming(jnp.maximum(4 * i - 4, 0) + j, 0)
            first_map(2 * i + 1, 1)
            second_map(2 * i, 0)
            first_map(2 * i + 2, 0)
            second_map(2 * i + 1, 1)
            return carry

        lax.fori_loop(0, pairs_whole, body, 0)
        second_map(2 * pairs_whole, 0)
        if coming is not None:
            for j in range(28, 35):
                coming(j, 0)

    def finish(store, skip, at, sem):
        for t in range(4):
            for c in range(4):
                lines = store[t, pl.ds(skip + c, 128, stride=4), :]
                out_ref[at + c, :, t * LANE : (t + 1) * LANE] = lines
        copy = pltpu.make_async_copy(out_ref.at[at : at + 4], out_any.at[at : at + 4], sem)
        copy.start()
        return copy

    lax.fori_loop(0, 35, prepare(low_st, -3, cond_a), 0, unroll=7)
    layer_pass(0, cond_a, up_st, 0, 640, prepare(up_st, -2, cond_b))
    layer_pass(1, cond_b, low_st, 8, 640, prepare(low_st, -3, cond_a))
    low_out = finish(low_st, 12, 0, sems.at[4])
    layer_pass(2, cond_a, up_st, 0, 512)
    up_out = finish(up_st, 8, 4, sems.at[5])
    low_out.wait()
    up_out.wait()


def dft_matrices():
    index = np.arange(LANE)
    angle = 2.0 * np.pi / LANE * (np.outer(index, index) % LANE)
    c = np.cos(angle) / np.sqrt(LANE)
    s = np.sin(angle) / np.sqrt(LANE)
    a = np.block([[c, s], [-s, c]]).astype(np.float32)
    b = np.block([[c, -s], [s, c]]).astype(np.float32)

    def parts(m):
        high = m.astype(jnp.bfloat16)
        low = (m - high.astype(np.float32)).astype(jnp.bfloat16)
        return high, low

    (ah, al), (bh, bl) = parts(a), parts(b)
    left_f = np.concatenate([ah, ah, al], axis=1)
    left_b = np.concatenate([bh, bh, bl], axis=1)
    right_f = np.concatenate([bh, bh, bl], axis=0)
    right_b = np.concatenate([ah, ah, al], axis=0)
    return left_f, left_b, right_f, right_b


def sds(*shape):
    return jax.ShapeDtypeStruct(shape, f32)


def slots_call(*operands):
    anywhere = pl.BlockSpec(memory_space=pl.ANY)
    return pl.pallas_call(
        slots_kernel,
        out_shape=[
            sds(TILES, 8, BAND, LANE),
            sds(41, STRIP, LANE),
            sds(9, STRIP, LANE),
            sds(32, STRIP, LANE),
            sds(9, BAND, LANE),
        ],
        in_specs=[smem()] * 3 + [anywhere] * 5 + [vmem()] * 3 + [anywhere] * 4,
        out_specs=[anywhere] * 5,
        scratch_shapes=[
            pltpu.VMEM((TILES, 8, 256, LANE), f32),
            pltpu.VMEM((TILES, 8, 256, LANE), f32),
            pltpu.VMEM((4, 4, 2, LANE, LANE), f32),
            pltpu.VMEM((5, 4, 2, LANE, LANE), f32),
            pltpu.VMEM((256, LANE), f32),
            pltpu.VMEM((256, 768), bf16),
            pltpu.VMEM((256, 768), bf16),
            pltpu.VMEM((768, 256), bf16),
            pltpu.VMEM((768, 256), bf16),
            pltpu.VMEM((4, LANE, LANE), f32),
            pltpu.SemaphoreType.DMA((31,)),
        ],
        compiler_params=params(62),
        name="slots",
    )(*operands)


def denoise_call(u, ev, odc, odm, ce, co, taps, conv_bias, output_weight, output_bias):
    anywhere = pl.BlockSpec(memory_space=pl.ANY)
    lines = sds(TILES, 4 * ROWS_KEPT, LANE)
    conv_parts, map_parts, out_bias = pl.pallas_call(
        weights_kernel,
        out_shape=[
            jax.ShapeDtypeStruct((3, LANE, KTOT), bf16),
            jax.ShapeDtypeStruct((3, 64, 256), bf16),
            sds(3, 32, LANE),
        ],
        in_specs=[vmem()] * 4,
        out_specs=[vmem()] * 3,
        compiler_params=params(62),
        cost_estimate=pl.CostEstimate(flops=1 << 20, bytes_accessed=3 << 20, transcendentals=0),
        name="weights",
    )(taps, conv_bias, output_weight, output_bias)
    low, up = pl.pallas_call(
        merge_kernel,
        out_shape=[lines] * 2,
        in_specs=[anywhere] * 4,
        out_specs=[vmem()] * 2,
        scratch_shapes=[
            pltpu.VMEM((TILES, 8, BAND, LANE), f32),
            pltpu.VMEM((41, STRIP, LANE), f32),
            pltpu.VMEM((41, STRIP, LANE), f32),
            pltpu.SemaphoreType.DMA((4,)),
        ],
        compiler_params=params(62),
        cost_estimate=pl.CostEstimate(flops=1 << 20, bytes_accessed=9 << 20, transcendentals=0),
        name="merge",
    )(u, ev, odc, odm)
    return pl.pallas_call(
        denoise_kernel,
        out_shape=sds(8, 128, 512),
        in_specs=[anywhere] * 4 + [vmem()] * 3,
        out_specs=anywhere,
        scratch_shapes=[
            pltpu.VMEM((TILES, 4 * ROWS_KEPT, LANE), f32),
            pltpu.VMEM((TILES, 4 * ROWS_KEPT, LANE), f32),
            pltpu.VMEM((3, 3, 4 * ROWS_KEPT, 640), bf16),
            pltpu.VMEM((3, 3, 4 * ROWS_KEPT, 640), bf16),
            pltpu.VMEM((2, 256, 640), f32),
            pltpu.VMEM((9, STRIP, LANE), f32),
            pltpu.VMEM((9, STRIP, LANE), f32),
            pltpu.VMEM((8, 128, 512), f32),
            pltpu.SemaphoreType.DMA((6,)),
        ],
        compiler_params=params(62),
        name="denoise",
    )(low, up, ce, co, conv_parts, map_parts, out_bias)


def per_device(
    object_field,
    probe_field,
    propagator_phase,
    position_rows,
    position_cols,
    tile_counts,
    intensities,
    conv_weight,
    conv_bias,
    output_weight,
    output_bias,
):
    rows = lax.axis_size("row")
    cols = lax.axis_size("col")

    def pairs(count, start):
        found = []
        for i in range(start, count - 1, 2):
            found += [(i, i + 1), (i + 1, i)]
        return found

    def row_ev(x):
        return lax.ppermute(x, "row", pairs(rows, 0))

    def row_od(x):
        return lax.ppermute(x, "row", pairs(rows, 1))

    def col_ev(x):
        return lax.ppermute(x, "col", pairs(cols, 0))

    def col_od(x):
        return lax.ppermute(x, "col", pairs(cols, 1))

    obj = object_field.reshape(8, 128, 512)
    def edge(index):
        return pl.BlockSpec((8, 128, LANE), lambda i: (0, 0, index))

    def whole(*shape):
        return pl.BlockSpec(shape, lambda i: (0,) * len(shape))

    ce, co = pl.pallas_call(
        pack_kernel,
        out_shape=[sds(8, HALF, LANE)] * 2,
        grid=(1,),
        in_specs=[edge(0), edge(3)],
        out_specs=[whole(8, HALF, LANE)] * 2,
        compiler_params=params(62),
        name="pack",
    )(obj, obj)
    ce = col_ev(ce)
    co = col_od(co)
    anywhere = pl.BlockSpec(memory_space=pl.ANY)
    strip = sds(TILES, 8, HALF, LANE)
    ev, od = pl.pallas_call(
        strips_kernel,
        out_shape=[strip] * 2,
        in_specs=[vmem()],
        out_specs=[vmem()] * 2,
        compiler_params=params(62),
        cost_estimate=pl.CostEstimate(flops=0, bytes_accessed=4 << 20, transcendentals=0),
        name="strips",
    )(obj)
    comb, ev, od = pl.pallas_call(
        comb_kernel,
        out_shape=[sds(8, 128, LANE), strip, strip],
        in_specs=[anywhere] * 4,
        out_specs=[anywhere] * 3,
        scratch_shapes=[
            pltpu.VMEM((8, 128, LANE), f32),
            pltpu.VMEM((8, HALF, LANE), f32),
            pltpu.VMEM((8, HALF, LANE), f32),
            pltpu.SemaphoreType.DMA((5,)),
        ],
        input_output_aliases={2: 1, 3: 2},
        compiler_params=params(62),
        name="comb",
    )(ce, co, ev, od)
    od = row_od(od)
    ev = row_ev(ev)
    phase_re = jnp.cos(propagator_phase)
    phase_im = jnp.sin(propagator_phase)
    tables = [jnp.asarray(m) for m in dft_matrices()]
    u, ev, odc, odm, own = slots_call(
        position_rows.reshape(-1),
        position_cols.reshape(-1),
        tile_counts.reshape(-1),
        obj,
        comb,
        ev,
        od,
        intensities.reshape(4, LANE, LANE),
        probe_field,
        phase_re,
        phase_im,
        *tables,
    )
    odc = row_od(odc)
    odm, odc = lax.optimization_barrier((odm, odc))
    odm = row_od(odm)
    ev = row_ev(ev)
    ce, co = pl.pallas_call(
        sides_kernel,
        out_shape=[sds(9, STRIP, LANE)] * 2,
        in_specs=[anywhere] * 3,
        out_specs=[vmem()] * 2,
        scratch_shapes=[
            pltpu.VMEM((9, BAND, LANE), f32),
            pltpu.VMEM((9, STRIP, LANE), f32),
            pltpu.VMEM((9, STRIP, LANE), f32),
            pltpu.SemaphoreType.DMA((3,)),
        ],
        compiler_params=params(62),
        name="sides",
    )(own, ev, odc)
    ce = col_ev(ce)
    co = col_od(co)
    taps = conv_weight.reshape(3, 3, 3, 32, 4).transpose(0, 1, 3, 2, 4).reshape(3, 3, 32, 12)
    out = denoise_call(u, ev, odc, odm, ce, co, taps, conv_bias, output_weight, output_bias)
    return out.reshape(4, 2, 128, 512)


def solution(mesh):
    placed = (
        P(None, None, "row", "col"),
        P(),
        P(),
        P("row", "col", None),
        P("row", "col", None),
        P("row", "col"),
        P("row", "col", None, None, None),
        P(),
        P(),
        P(),
        P(),
    )
    return jax.shard_map(
        per_device,
        mesh=mesh,
        in_specs=placed,
        out_specs=P(None, None, "row", "col"),
        check_vma=False,
    )
```

```python
import functools

import jax
import jax.numpy as jnp
import numpy as np
from jax import lax
from jax.experimental import pallas as pl
from jax.experimental.pallas import tpu as pltpu
from jax.sharding import PartitionSpec as P

step_size = 0.02
LANE = 128
HALF = 64
STRIP = 72
BAND = 144
TILES = 5
ROWS_KEPT = 140
ROWS_SET = 138
KTOT = 240

f32 = jnp.float32
bf16 = jnp.bfloat16


def params(mib):
    return pltpu.CompilerParams(vmem_limit_bytes=mib << 20)


def vmem():
    return pl.BlockSpec(memory_space=pltpu.VMEM)


def smem():
    return pl.BlockSpec(memory_space=pltpu.SMEM)


def lanes_of(shape):
    return lax.broadcasted_iota(jnp.int32, shape, len(shape) - 1)


def split(value):
    high = value.astype(bf16)
    low = (value - high.astype(f32)).astype(bf16)
    return high, low


def halves_swapped(value):
    return pltpu.roll(value, HALF, value.ndim - 1)


def pack_kernel(first_ref, last_ref, ce_ref, co_ref):
    col_odd = lax.axis_index("col") % 2
    first = lanes_of((HALF, LANE)) < HALF
    for c in range(8):
        left = first_ref[c]
        right = last_ref[c]
        to_left = jnp.where(first, left[:HALF], halves_swapped(left[HALF:]))
        to_right = jnp.where(first, halves_swapped(right[HALF:]), right[:HALF])
        ce_ref[c] = jnp.where(col_odd == 1, to_left, to_right)
        co_ref[c] = jnp.where(col_odd == 1, to_right, to_left)


def strips_kernel(obj_ref, ev_ref, od_ref):
    row_odd = lax.axis_index("row") % 2
    ev_start = pl.multiple_of((1 - row_odd) * HALF, HALF)
    od_start = pl.multiple_of(row_odd * HALF, HALF)
    for c in range(8):
        for t in range(4):
            ev_ref[t, c] = obj_ref[c, pl.ds(ev_start, HALF), t * LANE : (t + 1) * LANE]
            od_ref[t, c] = obj_ref[c, pl.ds(od_start, HALF), t * LANE : (t + 1) * LANE]


def comb_kernel(ce_any, co_any, ev_in, comb_ref, ev_ref, od_ref, comb_sc, ce_ref, co_ref, sems):
    del ev_in
    fetched = [
        pltpu.make_async_copy(ce_any, ce_ref, sems.at[3]),
        pltpu.make_async_copy(co_any, co_ref, sems.at[4]),
    ]
    for item in fetched:
        item.start()
    for item in fetched:
        item.wait()
    row_odd = lax.axis_index("row") % 2
    col_odd = lax.axis_index("col") % 2
    first = lanes_of((HALF, LANE)) < HALF
    for c in range(8):
        ce = ce_ref[c]
        co = co_ref[c]
        from_right = jnp.where(col_odd == 1, co, ce)
        from_left = jnp.where(col_odd == 1, ce, co)
        comb_sc[c, :HALF] = jnp.where(first, from_right, from_left)
        comb_sc[c, HALF:] = halves_swapped(jnp.where(first, from_left, from_right))
    ev_start = pl.multiple_of((1 - row_odd) * HALF, HALF)
    od_start = pl.multiple_of(row_odd * HALF, HALF)
    started = [
        pltpu.make_async_copy(comb_sc.at[:, pl.ds(od_start, HALF), :], od_ref, sems.at[0]),
        pltpu.make_async_copy(comb_sc.at[:, pl.ds(ev_start, HALF), :], ev_ref.at[4], sems.at[1]),
        pltpu.make_async_copy(comb_sc, comb_ref, sems.at[2]),
    ]
    for item in started:
        item.start()
    for item in started:
        item.wait()


def slots_kernel(
    rows_ref,
    cols_ref,
    count_ref,
    obj_ref,
    comb_ref,
    ev_ref,
    odc_ref,
    odm_ref,
    meas_any,
    probe_ref,
    phase_re_ref,
    phase_im_ref,
    left_f_any,
    left_b_any,
    right_f_any,
    right_b_any,
    u_ref,
    out_ev,
    out_odc,
    out_odm,
    own_ref,
    frame,
    accum,
    win,
    waves,
    extra,
    left_f_ref,
    left_b_ref,
    right_f_ref,
    right_b_ref,
    meas_ref,
    sems,
):
    row_odd = lax.axis_index("row") % 2
    ev_at = pl.multiple_of((1 - row_odd) * 192, HALF)
    od_at = pl.multiple_of(row_odd * 192, HALF)
    copies = []
    for t in range(4):
        copies.append((obj_ref.at[:, :, t * LANE : (t + 1) * LANE], frame.at[t, :, HALF:192, :]))
    copies.append((comb_ref, frame.at[4, :, HALF:192, :]))
    copies.append((ev_ref, frame.at[:, :, pl.ds(ev_at, HALF), :]))
    copies.append((odc_ref, frame.at[4, :, pl.ds(od_at, HALF), :]))
    copies.append((odm_ref, frame.at[0:4, :, pl.ds(od_at, HALF), :]))
    started = [pltpu.make_async_copy(src, dst, sems.at[i]) for i, (src, dst) in enumerate(copies)]
    late = [
        (left_f_any, left_f_ref),
        (right_f_any, right_f_ref),
        (right_b_any, right_b_ref),
        (left_b_any, left_b_ref),
        (meas_any, meas_ref),
    ]
    later = [pltpu.make_async_copy(src, dst, sems.at[8 + i]) for i, (src, dst) in enumerate(late)]
    for item in started + later:
        item.start()
    accum[...] = jnp.zeros(accum.shape, f32)
    for item in started:
        item.wait()

    lane = lanes_of((LANE, LANE))
    spots = []
    for k in range(4):
        row = rows_ref[k]
        at = lax.rem(cols_ref[k] + (640 - HALF), 640)
        q = at // LANE
        s = at - q * LANE
        nxt = jnp.where(q == 4, 0, q + 1)
        spots.append((row, q, nxt, s))

    for k in range(4):
        row, q, nxt, s = spots[k]
        keep = lane >= s
        turn = jnp.where(s == 0, 0, LANE - s)

        def take(c, carry, k=k, row=row, q=q, nxt=nxt, keep=keep, turn=turn):
            here = frame[q, c, pl.ds(row, LANE), :]
            beyond = frame[nxt, c, pl.ds(row, LANE), :]
            win[c // 2, k, c % 2] = pltpu.roll(jnp.where(keep, here, beyond), turn, 1)
            return carry

        lax.fori_loop(0, 8, take, 0, unroll=8)

    h_re = phase_re_ref[...]
    h_im = phase_im_ref[...]

    def left(xs, mat_ref):
        outs = []
        for g in range(0, 4, 2):
            stack = jnp.concatenate([jnp.concatenate(xs[k], axis=0) for k in (g, g + 1)], axis=1)
            high, low = split(stack)
            out = jnp.dot(
                mat_ref[...], jnp.concatenate([high, low, high], axis=0), preferred_element_type=f32
            )
            outs += [(out[:LANE, at : at + LANE], out[LANE:, at : at + LANE]) for at in (0, LANE)]
        return outs

    def right(xs, mat_ref):
        outs = []
        for g in range(0, 4, 2):
            stack = jnp.concatenate([jnp.concatenate(xs[k], axis=1) for k in (g, g + 1)], axis=0)
            high, low = split(stack)
            out = jnp.dot(
                jnp.concatenate([high, low, high], axis=1), mat_ref[...], preferred_element_type=f32
            )
            outs += [(out[at : at + LANE, :LANE], out[at : at + LANE, LANE:]) for at in (0, LANE)]
        return outs

    def forth(xs):
        return right(left(xs, left_f_ref), right_f_ref)

    def back(xs):
        return left(right(xs, right_b_ref), left_b_ref)

    def times(xs, re, im):
        return [(a * re - b * im, a * im + b * re) for a, b in xs]

    for k in range(4):
        waves[0, k, 0] = probe_ref[0]
        waves[0, k, 1] = probe_ref[1]

    def exit_wave(s):
        xs = []
        for k in range(4):
            p_re, p_im = waves[s, k, 0], waves[s, k, 1]
            o_re, o_im = win[s, k, 0], win[s, k, 1]
            xs.append((p_re * o_re - p_im * o_im, p_re * o_im + p_im * o_re))
        return xs

    def forward(s, carry):
        xs = back(times(forth(exit_wave(s)), h_re, h_im))
        for k in range(4):
            waves[s + 1, k, 0] = xs[k][0]
            waves[s + 1, k, 1] = xs[k][1]
        return carry

    for item in later:
        item.wait()
    lax.fori_loop(0, 3, forward, 0)
    far = forth(exit_wave(3))
    count = count_ref[0]
    seeds = []
    for k in range(4):
        re, im = far[k]
        factor = (re * re + im * im - meas_ref[k]) * (-2.0 * step_size)
        factor = jnp.where(k < count, factor, 0.0)
        seeds.append((factor * re, factor * im))
    gs = back(seeds)
    grad = waves
    for k in range(4):
        grad[4, k, 0] = gs[k][0]
        grad[4, k, 1] = gs[k][1]

    def through(s):
        xs = []
        for k in range(4):
            g_re, g_im = waves[4, k, 0], waves[4, k, 1]
            p_re, p_im = waves[s, k, 0], waves[s, k, 1]
            o_re, o_im = win[s, k, 0], win[s, k, 1]
            win[s, k, 0] = p_re * g_re + p_im * g_im
            win[s, k, 1] = p_re * g_im - p_im * g_re
            xs.append((o_re * g_re + o_im * g_im, o_re * g_im - o_im * g_re))
        return xs

    def backward(i, carry):
        xs = back(times(forth(through(3 - i)), h_re, -h_im))
        for k in range(4):
            waves[4, k, 0] = xs[k][0]
            waves[4, k, 1] = xs[k][1]
        return carry

    lax.fori_loop(0, 3, backward, 0)
    for k in range(4):
        g_re, g_im = waves[4, k, 0], waves[4, k, 1]
        p_re, p_im = probe_ref[0], probe_ref[1]
        win[0, k, 0] = p_re * g_re + p_im * g_im
        win[0, k, 1] = p_re * g_im - p_im * g_re

    for k in range(4):
        row, q, nxt, s = spots[k]
        keep = lane >= s

        def give(c, carry, k=k, row=row, q=q, nxt=nxt, keep=keep, s=s):
            turned = pltpu.roll(win[c // 2, k, c % 2], s, 1)
            here = accum[q, c, pl.ds(row, LANE), :]
            accum[q, c, pl.ds(row, LANE), :] = here + jnp.where(keep, turned, 0.0)
            beyond = accum[nxt, c, pl.ds(row, LANE), :]
            accum[nxt, c, pl.ds(row, LANE), :] = beyond + jnp.where(keep, 0.0, turned)
            return carry

        lax.fori_loop(0, 8, give, 0, unroll=8)

    wide = lanes_of((256, LANE)) // 8
    gathered = jnp.zeros((256, LANE), f32)
    for c in range(8):
        tail = pltpu.roll(accum[3, c], (8 * c + 8) % LANE, 1)
        head = pltpu.roll(accum[0, c], HALF + 8 * c, 1)
        gathered = jnp.where(wide == c, tail, gathered)
        gathered = jnp.where(wide == 8 + c, head, gathered)
    extra[...] = gathered

    ev_from = pl.multiple_of((1 - row_odd) * 184, 8)
    od_from = pl.multiple_of(row_odd * 184, 8)
    moves = [
        (accum.at[4, :, pl.ds(od_from, STRIP), :], out_odc.at[0:8]),
        (extra.at[pl.ds(od_from, STRIP), :], out_odc.at[8]),
    ]
    for t in range(4):
        moves.append((accum.at[t, :, pl.ds(od_from, STRIP), :], out_odm.at[8 * t : 8 * t + 8]))
    moves.append((accum.at[4, :, pl.ds(ev_from, STRIP), :], out_ev.at[0:8]))
    moves.append((extra.at[pl.ds(ev_from, STRIP), :], out_ev.at[8]))
    for t in range(4):
        moves.append((accum.at[t, :, pl.ds(ev_from, STRIP), :], out_ev.at[9 + 8 * t : 17 + 8 * t]))
    moves.append((accum.at[4, :, 56:200, :], own_ref.at[0:8]))
    moves.append((extra.at[56:200, :], own_ref.at[8]))
    sent = [pltpu.make_async_copy(src, dst, sems.at[13 + i]) for i, (src, dst) in enumerate(moves)]
    for item in sent:
        item.start()
    for t in range(TILES):
        frame[t, :, 56:200, :] = frame[t, :, 56:200, :] + accum[t, :, 56:200, :]
        item = pltpu.make_async_copy(frame.at[t, :, 56:200, :], u_ref.at[t], sems.at[27 + t])
        item.start()
        sent.append(item)
    for item in sent:
        item.wait()


def sides_kernel(own_any, ev_any, odc_any, ce_ref, co_ref, own_ref, evc_ref, odc_ref, sems):
    started = [
        pltpu.make_async_copy(own_any, own_ref, sems.at[0]),
        pltpu.make_async_copy(ev_any.at[0:9], evc_ref, sems.at[1]),
        pltpu.make_async_copy(odc_any, odc_ref, sems.at[2]),
    ]
    for item in started:
        item.start()
    for item in started:
        item.wait()
    row_odd = lax.axis_index("row") % 2
    col_odd = lax.axis_index("col") % 2
    first = lanes_of((STRIP, LANE)) < HALF
    for c in range(9):
        ev = evc_ref[c]
        od = odc_ref[c]
        top = own_ref[c, :STRIP] + jnp.where(row_odd == 1, ev, od)
        bottom = halves_swapped(own_ref[c, STRIP:] + jnp.where(row_odd == 1, od, ev))
        to_right = jnp.where(first, top, bottom)
        to_left = jnp.where(first, bottom, top)
        ce_ref[c] = jnp.where(col_odd == 1, to_left, to_right)
        co_ref[c] = jnp.where(col_odd == 1, to_right, to_left)


def weights_kernel(taps_ref, bias_ref, map_ref, map_bias_ref, conv_out, map_out, bias_out):
    def hot(rows, cols, test):
        a = lax.broadcasted_iota(jnp.int32, (rows, cols), 0)
        b = lax.broadcasted_iota(jnp.int32, (rows, cols), 1)
        return jnp.where(test(a, b), 1.0, 0.0).astype(f32)

    def exact(a, b):
        return jnp.dot(a, b, precision=lax.Precision.HIGHEST, preferred_element_type=f32)

    def column(b):
        half = ((b >= 96) & (b < 144)) | ((b >= 192) & (b < 224))
        line = jnp.where(half, b % 8, b % 16)
        dx = jnp.where(half, (b - jnp.where(b < 144, 96, 192)) // 8 % 3, b // 16 % 3)
        k = line // 4 + jnp.where(half, 4, 0)
        return dx * 4 + line % 4, k, b < 216

    def placed(a, b):
        source, _, valid = column(b)
        return valid & (a == source)

    place = hot(12, KTOT, placed)
    row = lax.broadcasted_iota(jnp.int32, (LANE, KTOT), 0)
    col = lax.broadcasted_iota(jnp.int32, (LANE, KTOT), 1)
    _, window_row, is_tap = column(col)
    shift = window_row - row // 32
    is_bias = (col == 224) | (col == 225)
    use_low = ((col >= 144) & (col < 216)) | (col == 225)
    hidden_hot = hot(LANE, 32, lambda a, b: a % 32 == b)
    channel_hot = hot(32, 4, lambda a, b: a % 4 == b)
    spread = hot(32, 256, lambda a, b: a == b % 32)
    same_row = hot(32, 256, lambda a, b: a // 4 == b // 32)
    for layer in range(3):
        bias = jnp.sum(hidden_hot * bias_ref[layer : layer + 1, :], axis=1, keepdims=True)
        total = jnp.where(is_bias, bias, 0.0)
        for dy in range(3):
            part = exact(taps_ref[layer, dy], place)
            whole = jnp.concatenate([part] * 4, axis=0)
            total = total + jnp.where((shift == dy) & is_tap, whole, 0.0)
        high, low = split(total * 0.5)
        conv_out[layer] = jnp.where(use_low, low.astype(f32), high.astype(f32)).astype(bf16)
        wide = exact(exact(channel_hot, map_ref[layer]), spread) * same_row
        high, low = split(wide)
        map_out[layer, 0:32] = high
        map_out[layer, 32:64] = low
        out_bias = jnp.sum(channel_hot * map_bias_ref[layer : layer + 1, :], axis=1, keepdims=True)
        bias_out[layer] = jnp.broadcast_to(out_bias, (32, LANE))


def merge_kernel(u_any, ev_any, odc_any, odm_any, low_st, up_st, u_ref, ev_ref, od_ref, sems):
    pairs = (
        (u_any, u_ref),
        (ev_any, ev_ref),
        (odc_any, od_ref.at[0:9]),
        (odm_any, od_ref.at[9:41]),
    )
    started = [pltpu.make_async_copy(a, b, sems.at[i]) for i, (a, b) in enumerate(pairs)]
    for item in started:
        item.start()
    for item in started:
        item.wait()
    row_odd = lax.axis_index("row") % 2

    def combine(t, c):
        plane = c if t == 4 else 9 + 8 * t + c
        ev = ev_ref[plane]
        od = od_ref[plane]
        top = u_ref[t, c, :STRIP] + jnp.where(row_odd == 1, ev, od)
        bottom = u_ref[t, c, STRIP:] + jnp.where(row_odd == 1, od, ev)
        return jnp.concatenate([top, bottom], axis=0)

    for t in range(TILES):
        for c in range(4):
            low_st[t, pl.ds(c, ROWS_SET, stride=4), :] = combine(t, c)[5:143]
            up_st[t, pl.ds(c, ROWS_SET, stride=4), :] = combine(t, 4 + c)[6:144]


def denoise_kernel(
    low_any,
    up_any,
    ce_any,
    co_any,
    conv_sc,
    map_sc,
    bias_ref,
    out_any,
    low_st,
    up_st,
    cond_a,
    cond_b,
    half_sc,
    ce_ref,
    co_ref,
    out_ref,
    sems,
):
    row_id = lax.axis_index("row")
    col_id = lax.axis_index("col")
    col_odd = col_id % 2
    lane = lanes_of((STRIP, LANE))
    first = lane < HALF
    low_copy = pltpu.make_async_copy(low_any, low_st, sems.at[0])
    up_copy = pltpu.make_async_copy(up_any, up_st, sems.at[1])
    side_copies = [
        pltpu.make_async_copy(ce_any, ce_ref, sems.at[2]),
        pltpu.make_async_copy(co_any, co_ref, sems.at[3]),
    ]
    side_copies[0].start()
    side_copies[1].start()
    low_copy.start()
    up_copy.start()

    def add_sides(c):
        store = low_st if c < 4 else up_st
        skip = 5 if c < 4 else 6
        ce = ce_ref[c]
        co = co_ref[c]
        from_left = jnp.where(col_odd == 1, ce, co)
        from_right = jnp.where(col_odd == 1, co, ce)
        swapped_left = halves_swapped(from_left)
        swapped_right = halves_swapped(from_right)
        ce = ce_ref[8]
        co = co_ref[8]
        tail = jnp.where(col_odd == 1, ce, co)
        head = jnp.where(col_odd == 1, co, ce)
        tail_top = pltpu.roll(tail, (120 - 8 * c) % LANE, 1)
        tail_bottom = pltpu.roll(tail, (HALF + 120 - 8 * c) % LANE, 1)
        head_top = pltpu.roll(head, (HALF - 8 * c) % LANE, 1)
        head_bottom = pltpu.roll(head, (LANE - 8 * c) % LANE, 1)
        at_tail = lane >= 120
        at_head = lane < 8
        pieces = {
            0: (jnp.where(first, from_left, 0.0), jnp.where(first, swapped_left, 0.0)),
            3: (jnp.where(first, 0.0, from_right), jnp.where(first, 0.0, swapped_right)),
            4: (
                jnp.where(at_tail, tail_top, jnp.where(at_head, head_top, 0.0)),
                jnp.where(at_tail, tail_bottom, jnp.where(at_head, head_bottom, 0.0)),
            ),
        }
        for t, both in pieces.items():
            at = pl.ds(c % 4, ROWS_SET, stride=4)
            whole = jnp.concatenate(both, axis=0)[skip : skip + ROWS_SET]
            store[t, at, :] = store[t, at, :] + whole

    side_copies[0].wait()
    side_copies[1].wait()
    low_copy.wait()
    for c in range(4):
        add_sides(c)
    up_copy.wait()
    for c in range(4, 8):
        add_sides(c)

    last_row = lax.axis_size("row") - 1
    last_col = lax.axis_size("col") - 1
    right_off = jnp.where(col_id == last_col, 512, 576)
    left_off = jnp.where(col_id == 0, 640, 576)

    def prepare(store, first_row, cond_st):
        row_low = jnp.where(row_id == 0, -first_row * 4, 0)
        row_high = (jnp.where(row_id == last_row, 128, 131) - first_row) * 4

        def body(i, carry):
            at = pl.multiple_of(i * 16, 16)
            x = jnp.concatenate([store[t, pl.ds(at, 16), :] for t in range(TILES)], axis=1)
            column = lax.broadcasted_iota(jnp.int32, x.shape, 1)
            index = lax.broadcasted_iota(jnp.int32, x.shape, 0) + at
            inside = (index >= row_low) & (index < row_high)
            inside = inside & ((column < right_off) | (column >= left_off))
            x = jnp.where(inside, x, 0.0)
            heads = []
            rests = []
            for dx in range(3):
                y = x if dx == 1 else pltpu.roll(x, 1 if dx == 0 else 639, 1)
                high = y.astype(bf16)
                rest = y - high.astype(f32)
                cond_st[0, dx, pl.ds(at, 16), :] = high
                cond_st[1, dx, pl.ds(at, 16), :] = rest.astype(bf16)
                heads.append(y[:8])
                rests.append(rest[:8])
            for i in range(3):
                both = jnp.concatenate((heads + rests)[2 * i : 2 * i + 2], axis=0)
                cond_st[2, i, pl.ds(at, 16), :] = both.astype(bf16)
            return carry

        return body

    ones = jnp.ones((16, 640), bf16)

    def layer_pass(layer, cond_st, store, write_at, width, coming=None):
        groups = 17
        bias = bias_ref[layer]

        def first_map(g, slot):
            for h in range(2):
                here = pl.ds(pl.multiple_of(g * 32 + 16 * h, 16), 16)
                below = pl.ds(pl.multiple_of(g * 32 + 16 * h + 16, 16), 16)
                main = [cond_st[part, dx, here, :width] for part in (0, 1) for dx in range(3)]
                half = [cond_st[2, i, below, :width] for i in range(3)]
                pieces = main + half + main[:3] + half[:2] + [ones[:, :width]]
                half_sc[slot, h * LANE : (h + 1) * LANE, :width] = jnp.dot(
                    conv_sc[layer], jnp.concatenate(pieces, axis=0), preferred_element_type=f32
                )

        def second_map(g, slot):
            dst = pl.multiple_of(write_at + g * 32, 8)
            half = half_sc[slot, :, :width]
            hidden = half + half * jnp.tanh(half)
            high, low = split(hidden)
            out = jnp.dot(map_sc[layer], high, preferred_element_type=f32)
            low_out = jnp.dot(map_sc[layer, 0:32], low, preferred_element_type=f32)
            term = out[:32] + out[32:] + low_out
            for t in range(width // LANE):
                bit = term[:, t * LANE : (t + 1) * LANE]
                store[t, pl.ds(dst, 32), :] = store[t, pl.ds(dst, 32), :] + (bit + bias)

        first_map(0, 0)
        pairs_whole = (groups - 1) // 2

        def body(i, carry):
            if coming is not None:
                for j in range(4):
                    coming(jnp.maximum(4 * i - 4, 0) + j, 0)
            first_map(2 * i + 1, 1)
            second_map(2 * i, 0)
            first_map(2 * i + 2, 0)
            second_map(2 * i + 1, 1)
            return carry

        lax.fori_loop(0, pairs_whole, body, 0)
        second_map(2 * pairs_whole, 0)
        if coming is not None:
            for j in range(28, 35):
                coming(j, 0)

    def finish(store, skip, at, sem):
        for t in range(4):
            for c in range(4):
                lines = store[t, pl.ds(skip + c, 128, stride=4), :]
                out_ref[at + c, :, t * LANE : (t + 1) * LANE] = lines
        copy = pltpu.make_async_copy(out_ref.at[at : at + 4], out_any.at[at : at + 4], sem)
        copy.start()
        return copy

    lax.fori_loop(0, 35, prepare(low_st, -3, cond_a), 0, unroll=7)
    layer_pass(0, cond_a, up_st, 0, 640, prepare(up_st, -2, cond_b))
    layer_pass(1, cond_b, low_st, 8, 640, prepare(low_st, -3, cond_a))
    low_out = finish(low_st, 12, 0, sems.at[4])
    layer_pass(2, cond_a, up_st, 0, 512)
    up_out = finish(up_st, 8, 4, sems.at[5])
    low_out.wait()
    up_out.wait()


def dft_matrices():
    index = np.arange(LANE)
    angle = 2.0 * np.pi / LANE * (np.outer(index, index) % LANE)
    c = np.cos(angle) / np.sqrt(LANE)
    s = np.sin(angle) / np.sqrt(LANE)
    a = np.block([[c, s], [-s, c]]).astype(np.float32)
    b = np.block([[c, -s], [s, c]]).astype(np.float32)

    def parts(m):
        high = m.astype(jnp.bfloat16)
        low = (m - high.astype(np.float32)).astype(jnp.bfloat16)
        return high, low

    (ah, al), (bh, bl) = parts(a), parts(b)
    left_f = np.concatenate([ah, ah, al], axis=1)
    left_b = np.concatenate([bh, bh, bl], axis=1)
    right_f = np.concatenate([bh, bh, bl], axis=0)
    right_b = np.concatenate([ah, ah, al], axis=0)
    return left_f, left_b, right_f, right_b


def sds(*shape):
    return jax.ShapeDtypeStruct(shape, f32)


def slots_call(*operands):
    anywhere = pl.BlockSpec(memory_space=pl.ANY)
    return pl.pallas_call(
        slots_kernel,
        out_shape=[
            sds(TILES, 8, BAND, LANE),
            sds(41, STRIP, LANE),
            sds(9, STRIP, LANE),
            sds(32, STRIP, LANE),
            sds(9, BAND, LANE),
        ],
        in_specs=[smem()] * 3 + [anywhere] * 6 + [vmem()] * 3 + [anywhere] * 4,
        out_specs=[anywhere] * 5,
        scratch_shapes=[
            pltpu.VMEM((TILES, 8, 256, LANE), f32),
            pltpu.VMEM((TILES, 8, 256, LANE), f32),
            pltpu.VMEM((4, 4, 2, LANE, LANE), f32),
            pltpu.VMEM((5, 4, 2, LANE, LANE), f32),
            pltpu.VMEM((256, LANE), f32),
            pltpu.VMEM((256, 768), bf16),
            pltpu.VMEM((256, 768), bf16),
            pltpu.VMEM((768, 256), bf16),
            pltpu.VMEM((768, 256), bf16),
            pltpu.VMEM((4, LANE, LANE), f32),
            pltpu.SemaphoreType.DMA((32,)),
        ],
        compiler_params=params(62),
        name="slots",
    )(*operands)


def denoise_call(u, ev, odc, odm, ce, co, taps, conv_bias, output_weight, output_bias):
    anywhere = pl.BlockSpec(memory_space=pl.ANY)
    lines = sds(TILES, 4 * ROWS_KEPT, LANE)
    conv_parts, map_parts, out_bias = pl.pallas_call(
        weights_kernel,
        out_shape=[
            jax.ShapeDtypeStruct((3, LANE, KTOT), bf16),
            jax.ShapeDtypeStruct((3, 64, 256), bf16),
            sds(3, 32, LANE),
        ],
        in_specs=[vmem()] * 4,
        out_specs=[vmem()] * 3,
        compiler_params=params(62),
        cost_estimate=pl.CostEstimate(flops=1 << 20, bytes_accessed=3 << 20, transcendentals=0),
        name="weights",
    )(taps, conv_bias, output_weight, output_bias)
    low, up = pl.pallas_call(
        merge_kernel,
        out_shape=[lines] * 2,
        in_specs=[anywhere] * 4,
        out_specs=[vmem()] * 2,
        scratch_shapes=[
            pltpu.VMEM((TILES, 8, BAND, LANE), f32),
            pltpu.VMEM((41, STRIP, LANE), f32),
            pltpu.VMEM((41, STRIP, LANE), f32),
            pltpu.SemaphoreType.DMA((4,)),
        ],
        compiler_params=params(62),
        cost_estimate=pl.CostEstimate(flops=1 << 20, bytes_accessed=9 << 20, transcendentals=0),
        name="merge",
    )(u, ev, odc, odm)
    return pl.pallas_call(
        denoise_kernel,
        out_shape=sds(8, 128, 512),
        in_specs=[anywhere] * 4 + [vmem()] * 3,
        out_specs=anywhere,
        scratch_shapes=[
            pltpu.VMEM((TILES, 4 * ROWS_KEPT, LANE), f32),
            pltpu.VMEM((TILES, 4 * ROWS_KEPT, LANE), f32),
            pltpu.VMEM((3, 3, 4 * ROWS_KEPT, 640), bf16),
            pltpu.VMEM((3, 3, 4 * ROWS_KEPT, 640), bf16),
            pltpu.VMEM((2, 256, 640), f32),
            pltpu.VMEM((9, STRIP, LANE), f32),
            pltpu.VMEM((9, STRIP, LANE), f32),
            pltpu.VMEM((8, 128, 512), f32),
            pltpu.SemaphoreType.DMA((6,)),
        ],
        compiler_params=params(62),
        name="denoise",
    )(low, up, ce, co, conv_parts, map_parts, out_bias)


def per_device(
    object_field,
    probe_field,
    propagator_phase,
    position_rows,
    position_cols,
    tile_counts,
    intensities,
    conv_weight,
    conv_bias,
    output_weight,
    output_bias,
):
    rows = lax.axis_size("row")
    cols = lax.axis_size("col")

    def pairs(count, start):
        found = []
        for i in range(start, count - 1, 2):
            found += [(i, i + 1), (i + 1, i)]
        return found

    def row_ev(x):
        return lax.ppermute(x, "row", pairs(rows, 0))

    def row_od(x):
        return lax.ppermute(x, "row", pairs(rows, 1))

    def col_ev(x):
        return lax.ppermute(x, "col", pairs(cols, 0))

    def col_od(x):
        return lax.ppermute(x, "col", pairs(cols, 1))

    obj = object_field.reshape(8, 128, 512)
    def edge(index):
        return pl.BlockSpec((8, 128, LANE), lambda i: (0, 0, index))

    def whole(*shape):
        return pl.BlockSpec(shape, lambda i: (0,) * len(shape))

    ce, co = pl.pallas_call(
        pack_kernel,
        out_shape=[sds(8, HALF, LANE)] * 2,
        grid=(1,),
        in_specs=[edge(0), edge(3)],
        out_specs=[whole(8, HALF, LANE)] * 2,
        compiler_params=params(62),
        name="pack",
    )(obj, obj)
    ce = col_ev(ce)
    co = col_od(co)
    anywhere = pl.BlockSpec(memory_space=pl.ANY)
    strip = sds(TILES, 8, HALF, LANE)
    ev, odm = pl.pallas_call(
        strips_kernel,
        out_shape=[strip, sds(4, 8, HALF, LANE)],
        in_specs=[vmem()],
        out_specs=[vmem()] * 2,
        compiler_params=params(62),
        cost_estimate=pl.CostEstimate(flops=0, bytes_accessed=4 << 20, transcendentals=0),
        name="strips",
    )(obj)
    odm = row_od(odm)
    ce, co, odm = lax.optimization_barrier((ce, co, odm))
    comb, ev, odc = pl.pallas_call(
        comb_kernel,
        out_shape=[sds(8, 128, LANE), strip, sds(8, HALF, LANE)],
        in_specs=[anywhere] * 3,
        out_specs=[anywhere] * 3,
        scratch_shapes=[
            pltpu.VMEM((8, 128, LANE), f32),
            pltpu.VMEM((8, HALF, LANE), f32),
            pltpu.VMEM((8, HALF, LANE), f32),
            pltpu.SemaphoreType.DMA((5,)),
        ],
        input_output_aliases={2: 1},
        compiler_params=params(62),
        name="comb",
    )(ce, co, ev)
    odc = row_od(odc)
    ev = row_ev(ev)
    phase_re = jnp.cos(propagator_phase)
    phase_im = jnp.sin(propagator_phase)
    tables = [jnp.asarray(m) for m in dft_matrices()]
    u, ev, odc, odm, own = slots_call(
        position_rows.reshape(-1),
        position_cols.reshape(-1),
        tile_counts.reshape(-1),
        obj,
        comb,
        ev,
        odc,
        odm,
        intensities.reshape(4, LANE, LANE),
        probe_field,
        phase_re,
        phase_im,
        *tables,
    )
    odc = row_od(odc)
    odm, odc = lax.optimization_barrier((odm, odc))
    odm = row_od(odm)
    ev = row_ev(ev)
    ce, co = pl.pallas_call(
        sides_kernel,
        out_shape=[sds(9, STRIP, LANE)] * 2,
        in_specs=[anywhere] * 3,
        out_specs=[vmem()] * 2,
        scratch_shapes=[
            pltpu.VMEM((9, BAND, LANE), f32),
            pltpu.VMEM((9, STRIP, LANE), f32),
            pltpu.VMEM((9, STRIP, LANE), f32),
            pltpu.SemaphoreType.DMA((3,)),
        ],
        compiler_params=params(62),
        name="sides",
    )(own, ev, odc)
    ce = col_ev(ce)
    co = col_od(co)
    taps = conv_weight.reshape(3, 3, 3, 32, 4).transpose(0, 1, 3, 2, 4).reshape(3, 3, 32, 12)
    out = denoise_call(u, ev, odc, odm, ce, co, taps, conv_bias, output_weight, output_bias)
    return out.reshape(4, 2, 128, 512)


def solution(mesh):
    placed = (
        P(None, None, "row", "col"),
        P(),
        P(),
        P("row", "col", None),
        P("row", "col", None),
        P("row", "col"),
        P("row", "col", None, None, None),
        P(),
        P(),
        P(),
        P(),
    )
    return jax.shard_map(
        per_device,
        mesh=mesh,
        in_specs=placed,
        out_specs=P(None, None, "row", "col"),
        check_vma=False,
    )
```

```python
import functools

import jax
import jax.numpy as jnp
import numpy as np
from jax import lax
from jax.experimental import pallas as pl
from jax.experimental.pallas import tpu as pltpu
from jax.sharding import PartitionSpec as P

step_size = 0.02
LANE = 128
HALF = 64
STRIP = 72
BAND = 144
TILES = 5
ROWS_KEPT = 140
ROWS_SET = 138
KTOT = 240

f32 = jnp.float32
bf16 = jnp.bfloat16


def params(mib):
    return pltpu.CompilerParams(vmem_limit_bytes=mib << 20)


def vmem():
    return pl.BlockSpec(memory_space=pltpu.VMEM)


def smem():
    return pl.BlockSpec(memory_space=pltpu.SMEM)


def lanes_of(shape):
    return lax.broadcasted_iota(jnp.int32, shape, len(shape) - 1)


def split(value):
    high = value.astype(bf16)
    low = (value - high.astype(f32)).astype(bf16)
    return high, low


def halves_swapped(value):
    return pltpu.roll(value, HALF, value.ndim - 1)


def pack_kernel(first_ref, last_ref, ce_ref, co_ref):
    col_odd = lax.axis_index("col") % 2
    first = lanes_of((HALF, LANE)) < HALF
    for c in range(8):
        left = first_ref[c]
        right = last_ref[c]
        to_left = jnp.where(first, left[:HALF], halves_swapped(left[HALF:]))
        to_right = jnp.where(first, halves_swapped(right[HALF:]), right[:HALF])
        ce_ref[c] = jnp.where(col_odd == 1, to_left, to_right)
        co_ref[c] = jnp.where(col_odd == 1, to_right, to_left)


def strips_kernel(obj_ref, ev_ref, od_ref):
    row_odd = lax.axis_index("row") % 2
    ev_start = pl.multiple_of((1 - row_odd) * HALF, HALF)
    od_start = pl.multiple_of(row_odd * HALF, HALF)
    for c in range(8):
        for t in range(4):
            ev_ref[t, c] = obj_ref[c, pl.ds(ev_start, HALF), t * LANE : (t + 1) * LANE]
            od_ref[t, c] = obj_ref[c, pl.ds(od_start, HALF), t * LANE : (t + 1) * LANE]


def comb_kernel(ce_any, co_any, ev_in, od_in, comb_ref, ev_ref, od_ref, comb_sc, ce_ref, co_ref, sems):
    del ev_in, od_in
    fetched = [
        pltpu.make_async_copy(ce_any, ce_ref, sems.at[3]),
        pltpu.make_async_copy(co_any, co_ref, sems.at[4]),
    ]
    for item in fetched:
        item.start()
    for item in fetched:
        item.wait()
    row_odd = lax.axis_index("row") % 2
    col_odd = lax.axis_index("col") % 2
    first = lanes_of((HALF, LANE)) < HALF
    for c in range(8):
        ce = ce_ref[c]
        co = co_ref[c]
        from_right = jnp.where(col_odd == 1, co, ce)
        from_left = jnp.where(col_odd == 1, ce, co)
        comb_sc[c, :HALF] = jnp.where(first, from_right, from_left)
        comb_sc[c, HALF:] = halves_swapped(jnp.where(first, from_left, from_right))
    ev_start = pl.multiple_of((1 - row_odd) * HALF, HALF)
    od_start = pl.multiple_of(row_odd * HALF, HALF)
    started = [
        pltpu.make_async_copy(comb_sc.at[:, pl.ds(od_start, HALF), :], od_ref.at[4], sems.at[0]),
        pltpu.make_async_copy(comb_sc.at[:, pl.ds(ev_start, HALF), :], ev_ref.at[4], sems.at[1]),
        pltpu.make_async_copy(comb_sc, comb_ref, sems.at[2]),
    ]
    for item in started:
        item.start()
    for item in started:
        item.wait()


def slots_kernel(
    rows_ref,
    cols_ref,
    count_ref,
    obj_ref,
    comb_ref,
    ev_ref,
    od_ref,
    meas_any,
    probe_ref,
    phase_re_ref,
    phase_im_ref,
    left_f_any,
    left_b_any,
    right_f_any,
    right_b_any,
    u_ref,
    out_evc,
    out_evm,
    out_odc,
    out_odm,
    own_ref,
    frame,
    accum,
    win,
    waves,
    extra,
    left_f_ref,
    left_b_ref,
    right_f_ref,
    right_b_ref,
    meas_ref,
    sems,
):
    row_odd = lax.axis_index("row") % 2
    ev_at = pl.multiple_of((1 - row_odd) * 192, HALF)
    od_at = pl.multiple_of(row_odd * 192, HALF)
    copies = []
    for t in range(4):
        copies.append((obj_ref.at[:, :, t * LANE : (t + 1) * LANE], frame.at[t, :, HALF:192, :]))
    copies.append((comb_ref, frame.at[4, :, HALF:192, :]))
    copies.append((ev_ref, frame.at[:, :, pl.ds(ev_at, HALF), :]))
    copies.append((od_ref, frame.at[:, :, pl.ds(od_at, HALF), :]))
    started = [pltpu.make_async_copy(src, dst, sems.at[i]) for i, (src, dst) in enumerate(copies)]
    late = [
        (left_f_any, left_f_ref),
        (right_f_any, right_f_ref),
        (right_b_any, right_b_ref),
        (left_b_any, left_b_ref),
        (meas_any, meas_ref),
    ]
    later = [pltpu.make_async_copy(src, dst, sems.at[7 + i]) for i, (src, dst) in enumerate(late)]
    for item in started + later:
        item.start()
    accum[...] = jnp.zeros(accum.shape, f32)
    for item in started:
        item.wait()

    lane = lanes_of((LANE, LANE))
    spots = []
    for k in range(4):
        row = rows_ref[k]
        at = lax.rem(cols_ref[k] + (640 - HALF), 640)
        q = at // LANE
        s = at - q * LANE
        nxt = jnp.where(q == 4, 0, q + 1)
        spots.append((row, q, nxt, s))

    for k in range(4):
        row, q, nxt, s = spots[k]
        keep = lane >= s
        turn = jnp.where(s == 0, 0, LANE - s)

        def take(c, carry, k=k, row=row, q=q, nxt=nxt, keep=keep, turn=turn):
            here = frame[q, c, pl.ds(row, LANE), :]
            beyond = frame[nxt, c, pl.ds(row, LANE), :]
            win[c // 2, k, c % 2] = pltpu.roll(jnp.where(keep, here, beyond), turn, 1)
            return carry

        lax.fori_loop(0, 8, take, 0, unroll=8)

    h_re = phase_re_ref[...]
    h_im = phase_im_ref[...]

    def left(xs, mat_ref):
        outs = []
        for g in range(0, 4, 2):
            stack = jnp.concatenate([jnp.concatenate(xs[k], axis=0) for k in (g, g + 1)], axis=1)
            high, low = split(stack)
            out = jnp.dot(
                mat_ref[...], jnp.concatenate([high, low, high], axis=0), preferred_element_type=f32
            )
            outs += [(out[:LANE, at : at + LANE], out[LANE:, at : at + LANE]) for at in (0, LANE)]
        return outs

    def right(xs, mat_ref):
        outs = []
        for g in range(0, 4, 2):
            stack = jnp.concatenate([jnp.concatenate(xs[k], axis=1) for k in (g, g + 1)], axis=0)
            high, low = split(stack)
            out = jnp.dot(
                jnp.concatenate([high, low, high], axis=1), mat_ref[...], preferred_element_type=f32
            )
            outs += [(out[at : at + LANE, :LANE], out[at : at + LANE, LANE:]) for at in (0, LANE)]
        return outs

    def forth(xs):
        return right(left(xs, left_f_ref), right_f_ref)

    def back(xs):
        return left(right(xs, right_b_ref), left_b_ref)

    def times(xs, re, im):
        return [(a * re - b * im, a * im + b * re) for a, b in xs]

    for k in range(4):
        waves[0, k, 0] = probe_ref[0]
        waves[0, k, 1] = probe_ref[1]

    def exit_wave(s):
        xs = []
        for k in range(4):
            p_re, p_im = waves[s, k, 0], waves[s, k, 1]
            o_re, o_im = win[s, k, 0], win[s, k, 1]
            xs.append((p_re * o_re - p_im * o_im, p_re * o_im + p_im * o_re))
        return xs

    def forward(s, carry):
        xs = back(times(forth(exit_wave(s)), h_re, h_im))
        for k in range(4):
            waves[s + 1, k, 0] = xs[k][0]
            waves[s + 1, k, 1] = xs[k][1]
        return carry

    for item in later:
        item.wait()
    lax.fori_loop(0, 3, forward, 0)
    far = forth(exit_wave(3))
    count = count_ref[0]
    seeds = []
    for k in range(4):
        re, im = far[k]
        factor = (re * re + im * im - meas_ref[k]) * (-2.0 * step_size)
        factor = jnp.where(k < count, factor, 0.0)
        seeds.append((factor * re, factor * im))
    gs = back(seeds)
    grad = waves
    for k in range(4):
        grad[4, k, 0] = gs[k][0]
        grad[4, k, 1] = gs[k][1]

    def through(s):
        xs = []
        for k in range(4):
            g_re, g_im = waves[4, k, 0], waves[4, k, 1]
            p_re, p_im = waves[s, k, 0], waves[s, k, 1]
            o_re, o_im = win[s, k, 0], win[s, k, 1]
            win[s, k, 0] = p_re * g_re + p_im * g_im
            win[s, k, 1] = p_re * g_im - p_im * g_re
            xs.append((o_re * g_re + o_im * g_im, o_re * g_im - o_im * g_re))
        return xs

    def backward(i, carry):
        xs = back(times(forth(through(3 - i)), h_re, -h_im))
        for k in range(4):
            waves[4, k, 0] = xs[k][0]
            waves[4, k, 1] = xs[k][1]
        return carry

    lax.fori_loop(0, 3, backward, 0)
    for k in range(4):
        g_re, g_im = waves[4, k, 0], waves[4, k, 1]
        p_re, p_im = probe_ref[0], probe_ref[1]
        win[0, k, 0] = p_re * g_re + p_im * g_im
        win[0, k, 1] = p_re * g_im - p_im * g_re

    for k in range(4):
        row, q, nxt, s = spots[k]
        keep = lane >= s

        def give(c, carry, k=k, row=row, q=q, nxt=nxt, keep=keep, s=s):
            turned = pltpu.roll(win[c // 2, k, c % 2], s, 1)
            here = accum[q, c, pl.ds(row, LANE), :]
            accum[q, c, pl.ds(row, LANE), :] = here + jnp.where(keep, turned, 0.0)
            beyond = accum[nxt, c, pl.ds(row, LANE), :]
            accum[nxt, c, pl.ds(row, LANE), :] = beyond + jnp.where(keep, 0.0, turned)
            return carry

        lax.fori_loop(0, 8, give, 0, unroll=8)

    wide = lanes_of((256, LANE)) // 8
    gathered = jnp.zeros((256, LANE), f32)
    for c in range(8):
        tail = pltpu.roll(accum[3, c], (8 * c + 8) % LANE, 1)
        head = pltpu.roll(accum[0, c], HALF + 8 * c, 1)
        gathered = jnp.where(wide == c, tail, gathered)
        gathered = jnp.where(wide == 8 + c, head, gathered)
    extra[...] = gathered

    ev_from = pl.multiple_of((1 - row_odd) * 184, 8)
    od_from = pl.multiple_of(row_odd * 184, 8)
    moves = [
        (accum.at[4, :, pl.ds(od_from, STRIP), :], out_odc.at[0:8]),
        (extra.at[pl.ds(od_from, STRIP), :], out_odc.at[8]),
    ]
    for t in range(4):
        moves.append((accum.at[t, :, pl.ds(od_from, STRIP), :], out_odm.at[8 * t : 8 * t + 8]))
    moves.append((accum.at[4, :, pl.ds(ev_from, STRIP), :], out_evc.at[0:8]))
    moves.append((extra.at[pl.ds(ev_from, STRIP), :], out_evc.at[8]))
    for t in range(4):
        moves.append((accum.at[t, :, pl.ds(ev_from, STRIP), :], out_evm.at[8 * t : 8 * t + 8]))
    moves.append((accum.at[4, :, 56:200, :], own_ref.at[0:8]))
    moves.append((extra.at[56:200, :], own_ref.at[8]))
    sent = [pltpu.make_async_copy(src, dst, sems.at[12 + i]) for i, (src, dst) in enumerate(moves)]
    for item in sent:
        item.start()
    for t in range(TILES):
        frame[t, :, 56:200, :] = frame[t, :, 56:200, :] + accum[t, :, 56:200, :]
        item = pltpu.make_async_copy(frame.at[t, :, 56:200, :], u_ref.at[t], sems.at[26 + t])
        item.start()
        sent.append(item)
    for item in sent:
        item.wait()


def sides_kernel(own_any, evc_any, odc_any, ce_ref, co_ref, own_ref, evc_ref, odc_ref, sems):
    started = [
        pltpu.make_async_copy(own_any, own_ref, sems.at[0]),
        pltpu.make_async_copy(evc_any, evc_ref, sems.at[1]),
        pltpu.make_async_copy(odc_any, odc_ref, sems.at[2]),
    ]
    for item in started:
        item.start()
    for item in started:
        item.wait()
    row_odd = lax.axis_index("row") % 2
    col_odd = lax.axis_index("col") % 2
    first = lanes_of((STRIP, LANE)) < HALF
    for c in range(9):
        ev = evc_ref[c]
        od = odc_ref[c]
        top = own_ref[c, :STRIP] + jnp.where(row_odd == 1, ev, od)
        bottom = halves_swapped(own_ref[c, STRIP:] + jnp.where(row_odd == 1, od, ev))
        to_right = jnp.where(first, top, bottom)
        to_left = jnp.where(first, bottom, top)
        ce_ref[c] = jnp.where(col_odd == 1, to_left, to_right)
        co_ref[c] = jnp.where(col_odd == 1, to_right, to_left)


def weights_kernel(taps_ref, bias_ref, map_ref, map_bias_ref, conv_out, map_out, bias_out):
    def hot(rows, cols, test):
        a = lax.broadcasted_iota(jnp.int32, (rows, cols), 0)
        b = lax.broadcasted_iota(jnp.int32, (rows, cols), 1)
        return jnp.where(test(a, b), 1.0, 0.0).astype(f32)

    def exact(a, b):
        return jnp.dot(a, b, precision=lax.Precision.HIGHEST, preferred_element_type=f32)

    def column(b):
        half = ((b >= 96) & (b < 144)) | ((b >= 192) & (b < 224))
        line = jnp.where(half, b % 8, b % 16)
        dx = jnp.where(half, (b - jnp.where(b < 144, 96, 192)) // 8 % 3, b // 16 % 3)
        k = line // 4 + jnp.where(half, 4, 0)
        return dx * 4 + line % 4, k, b < 216

    def placed(a, b):
        source, _, valid = column(b)
        return valid & (a == source)

    place = hot(12, KTOT, placed)
    row = lax.broadcasted_iota(jnp.int32, (LANE, KTOT), 0)
    col = lax.broadcasted_iota(jnp.int32, (LANE, KTOT), 1)
    _, window_row, is_tap = column(col)
    shift = window_row - row // 32
    is_bias = (col == 224) | (col == 225)
    use_low = ((col >= 144) & (col < 216)) | (col == 225)
    hidden_hot = hot(LANE, 32, lambda a, b: a % 32 == b)
    channel_hot = hot(32, 4, lambda a, b: a % 4 == b)
    spread = hot(32, 256, lambda a, b: a == b % 32)
    same_row = hot(32, 256, lambda a, b: a // 4 == b // 32)
    for layer in range(3):
        bias = jnp.sum(hidden_hot * bias_ref[layer : layer + 1, :], axis=1, keepdims=True)
        total = jnp.where(is_bias, bias, 0.0)
        for dy in range(3):
            part = exact(taps_ref[layer, dy], place)
            whole = jnp.concatenate([part] * 4, axis=0)
            total = total + jnp.where((shift == dy) & is_tap, whole, 0.0)
        high, low = split(total * 0.5)
        conv_out[layer] = jnp.where(use_low, low.astype(f32), high.astype(f32)).astype(bf16)
        wide = exact(exact(channel_hot, map_ref[layer]), spread) * same_row
        high, low = split(wide)
        map_out[layer, 0:32] = high
        map_out[layer, 32:64] = low
        out_bias = jnp.sum(channel_hot * map_bias_ref[layer : layer + 1, :], axis=1, keepdims=True)
        bias_out[layer] = jnp.broadcast_to(out_bias, (32, LANE))


def merge_kernel(u_any, evc_any, evm_any, odc_any, odm_any, low_st, up_st, u_ref, ev_ref, od_ref, sems):
    pairs = (
        (u_any, u_ref),
        (evc_any, ev_ref.at[0:9]),
        (evm_any, ev_ref.at[9:41]),
        (odc_any, od_ref.at[0:9]),
        (odm_any, od_ref.at[9:41]),
    )
    started = [pltpu.make_async_copy(a, b, sems.at[i]) for i, (a, b) in enumerate(pairs)]
    for item in started:
        item.start()
    for item in started:
        item.wait()
    row_odd = lax.axis_index("row") % 2

    def combine(t, c):
        plane = c if t == 4 else 9 + 8 * t + c
        ev = ev_ref[plane]
        od = od_ref[plane]
        top = u_ref[t, c, :STRIP] + jnp.where(row_odd == 1, ev, od)
        bottom = u_ref[t, c, STRIP:] + jnp.where(row_odd == 1, od, ev)
        return jnp.concatenate([top, bottom], axis=0)

    for t in range(TILES):
        for c in range(4):
            low_st[t, pl.ds(c, ROWS_SET, stride=4), :] = combine(t, c)[5:143]
            up_st[t, pl.ds(c, ROWS_SET, stride=4), :] = combine(t, 4 + c)[6:144]


def denoise_kernel(
    low_any,
    up_any,
    ce_any,
    co_any,
    conv_sc,
    map_sc,
    bias_ref,
    out_any,
    low_st,
    up_st,
    cond_a,
    cond_b,
    half_sc,
    ce_ref,
    co_ref,
    out_ref,
    sems,
):
    row_id = lax.axis_index("row")
    col_id = lax.axis_index("col")
    col_odd = col_id % 2
    lane = lanes_of((STRIP, LANE))
    first = lane < HALF
    low_copy = pltpu.make_async_copy(low_any, low_st, sems.at[0])
    up_copy = pltpu.make_async_copy(up_any, up_st, sems.at[1])
    side_copies = [
        pltpu.make_async_copy(ce_any, ce_ref, sems.at[2]),
        pltpu.make_async_copy(co_any, co_ref, sems.at[3]),
    ]
    side_copies[0].start()
    side_copies[1].start()
    low_copy.start()
    up_copy.start()

    def add_sides(c):
        store = low_st if c < 4 else up_st
        skip = 5 if c < 4 else 6
        ce = ce_ref[c]
        co = co_ref[c]
        from_left = jnp.where(col_odd == 1, ce, co)
        from_right = jnp.where(col_odd == 1, co, ce)
        swapped_left = halves_swapped(from_left)
        swapped_right = halves_swapped(from_right)
        ce = ce_ref[8]
        co = co_ref[8]
        tail = jnp.where(col_odd == 1, ce, co)
        head = jnp.where(col_odd == 1, co, ce)
        tail_top = pltpu.roll(tail, (120 - 8 * c) % LANE, 1)
        tail_bottom = pltpu.roll(tail, (HALF + 120 - 8 * c) % LANE, 1)
        head_top = pltpu.roll(head, (HALF - 8 * c) % LANE, 1)
        head_bottom = pltpu.roll(head, (LANE - 8 * c) % LANE, 1)
        at_tail = lane >= 120
        at_head = lane < 8
        pieces = {
            0: (jnp.where(first, from_left, 0.0), jnp.where(first, swapped_left, 0.0)),
            3: (jnp.where(first, 0.0, from_right), jnp.where(first, 0.0, swapped_right)),
            4: (
                jnp.where(at_tail, tail_top, jnp.where(at_head, head_top, 0.0)),
                jnp.where(at_tail, tail_bottom, jnp.where(at_head, head_bottom, 0.0)),
            ),
        }
        for t, both in pieces.items():
            at = pl.ds(c % 4, ROWS_SET, stride=4)
            whole = jnp.concatenate(both, axis=0)[skip : skip + ROWS_SET]
            store[t, at, :] = store[t, at, :] + whole

    side_copies[0].wait()
    side_copies[1].wait()
    low_copy.wait()
    for c in range(4):
        add_sides(c)
    up_copy.wait()
    for c in range(4, 8):
        add_sides(c)

    last_row = lax.axis_size("row") - 1
    last_col = lax.axis_size("col") - 1
    right_off = jnp.where(col_id == last_col, 512, 576)
    left_off = jnp.where(col_id == 0, 640, 576)

    def prepare(store, first_row, cond_st):
        row_low = jnp.where(row_id == 0, -first_row * 4, 0)
        row_high = (jnp.where(row_id == last_row, 128, 131) - first_row) * 4

        def body(i, carry):
            at = pl.multiple_of(i * 16, 16)
            x = jnp.concatenate([store[t, pl.ds(at, 16), :] for t in range(TILES)], axis=1)
            column = lax.broadcasted_iota(jnp.int32, x.shape, 1)
            index = lax.broadcasted_iota(jnp.int32, x.shape, 0) + at
            inside = (index >= row_low) & (index < row_high)
            inside = inside & ((column < right_off) | (column >= left_off))
            x = jnp.where(inside, x, 0.0)
            heads = []
            rests = []
            for dx in range(3):
                y = x if dx == 1 else pltpu.roll(x, 1 if dx == 0 else 639, 1)
                high = y.astype(bf16)
                rest = y - high.astype(f32)
                cond_st[0, dx, pl.ds(at, 16), :] = high
                cond_st[1, dx, pl.ds(at, 16), :] = rest.astype(bf16)
                heads.append(y[:8])
                rests.append(rest[:8])
            for i in range(3):
                both = jnp.concatenate((heads + rests)[2 * i : 2 * i + 2], axis=0)
                cond_st[2, i, pl.ds(at, 16), :] = both.astype(bf16)
            return carry

        return body

    ones = jnp.ones((16, 640), bf16)

    def layer_pass(layer, cond_st, store, write_at, width, coming=None):
        groups = 17
        bias = bias_ref[layer]

        def first_map(g, slot):
            for h in range(2):
                here = pl.ds(pl.multiple_of(g * 32 + 16 * h, 16), 16)
                below = pl.ds(pl.multiple_of(g * 32 + 16 * h + 16, 16), 16)
                main = [cond_st[part, dx, here, :width] for part in (0, 1) for dx in range(3)]
                half = [cond_st[2, i, below, :width] for i in range(3)]
                pieces = main + half + main[:3] + half[:2] + [ones[:, :width]]
                half_sc[slot, h * LANE : (h + 1) * LANE, :width] = jnp.dot(
                    conv_sc[layer], jnp.concatenate(pieces, axis=0), preferred_element_type=f32
                )

        def second_map(g, slot):
            dst = pl.multiple_of(write_at + g * 32, 8)
            half = half_sc[slot, :, :width]
            hidden = half + half * jnp.tanh(half)
            high, low = split(hidden)
            out = jnp.dot(map_sc[layer], high, preferred_element_type=f32)
            low_out = jnp.dot(map_sc[layer, 0:32], low, preferred_element_type=f32)
            term = out[:32] + out[32:] + low_out
            for t in range(width // LANE):
                bit = term[:, t * LANE : (t + 1) * LANE]
                store[t, pl.ds(dst, 32), :] = store[t, pl.ds(dst, 32), :] + (bit + bias)

        first_map(0, 0)
        pairs_whole = (groups - 1) // 2

        def body(i, carry):
            if coming is not None:
                for j in range(4):
                    coming(jnp.maximum(4 * i - 4, 0) + j, 0)
            first_map(2 * i + 1, 1)
            second_map(2 * i, 0)
            first_map(2 * i + 2, 0)
            second_map(2 * i + 1, 1)
            return carry

        lax.fori_loop(0, pairs_whole, body, 0)
        second_map(2 * pairs_whole, 0)
        if coming is not None:
            for j in range(28, 35):
                coming(j, 0)

    def finish(store, skip, at, sem):
        for t in range(4):
            for c in range(4):
                lines = store[t, pl.ds(skip + c, 128, stride=4), :]
                out_ref[at + c, :, t * LANE : (t + 1) * LANE] = lines
        copy = pltpu.make_async_copy(out_ref.at[at : at + 4], out_any.at[at : at + 4], sem)
        copy.start()
        return copy

    lax.fori_loop(0, 35, prepare(low_st, -3, cond_a), 0, unroll=7)
    layer_pass(0, cond_a, up_st, 0, 640, prepare(up_st, -2, cond_b))
    layer_pass(1, cond_b, low_st, 8, 640, prepare(low_st, -3, cond_a))
    low_out = finish(low_st, 12, 0, sems.at[4])
    layer_pass(2, cond_a, up_st, 0, 512)
    up_out = finish(up_st, 8, 4, sems.at[5])
    low_out.wait()
    up_out.wait()


def dft_matrices():
    index = np.arange(LANE)
    angle = 2.0 * np.pi / LANE * (np.outer(index, index) % LANE)
    c = np.cos(angle) / np.sqrt(LANE)
    s = np.sin(angle) / np.sqrt(LANE)
    a = np.block([[c, s], [-s, c]]).astype(np.float32)
    b = np.block([[c, -s], [s, c]]).astype(np.float32)

    def parts(m):
        high = m.astype(jnp.bfloat16)
        low = (m - high.astype(np.float32)).astype(jnp.bfloat16)
        return high, low

    (ah, al), (bh, bl) = parts(a), parts(b)
    left_f = np.concatenate([ah, ah, al], axis=1)
    left_b = np.concatenate([bh, bh, bl], axis=1)
    right_f = np.concatenate([bh, bh, bl], axis=0)
    right_b = np.concatenate([ah, ah, al], axis=0)
    return left_f, left_b, right_f, right_b


def sds(*shape):
    return jax.ShapeDtypeStruct(shape, f32)


def slots_call(*operands):
    anywhere = pl.BlockSpec(memory_space=pl.ANY)
    return pl.pallas_call(
        slots_kernel,
        out_shape=[
            sds(TILES, 8, BAND, LANE),
            sds(9, STRIP, LANE),
            sds(32, STRIP, LANE),
            sds(9, STRIP, LANE),
            sds(32, STRIP, LANE),
            sds(9, BAND, LANE),
        ],
        in_specs=[smem()] * 3 + [anywhere] * 5 + [vmem()] * 3 + [anywhere] * 4,
        out_specs=[anywhere] * 6,
        scratch_shapes=[
            pltpu.VMEM((TILES, 8, 256, LANE), f32),
            pltpu.VMEM((TILES, 8, 256, LANE), f32),
            pltpu.VMEM((4, 4, 2, LANE, LANE), f32),
            pltpu.VMEM((5, 4, 2, LANE, LANE), f32),
            pltpu.VMEM((256, LANE), f32),
            pltpu.VMEM((256, 768), bf16),
            pltpu.VMEM((256, 768), bf16),
            pltpu.VMEM((768, 256), bf16),
            pltpu.VMEM((768, 256), bf16),
            pltpu.VMEM((4, LANE, LANE), f32),
            pltpu.SemaphoreType.DMA((31,)),
        ],
        compiler_params=params(62),
        name="slots",
    )(*operands)


def denoise_call(u, evc, evm, odc, odm, ce, co, taps, conv_bias, output_weight, output_bias):
    anywhere = pl.BlockSpec(memory_space=pl.ANY)
    lines = sds(TILES, 4 * ROWS_KEPT, LANE)
    conv_parts, map_parts, out_bias = pl.pallas_call(
        weights_kernel,
        out_shape=[
            jax.ShapeDtypeStruct((3, LANE, KTOT), bf16),
            jax.ShapeDtypeStruct((3, 64, 256), bf16),
            sds(3, 32, LANE),
        ],
        in_specs=[vmem()] * 4,
        out_specs=[vmem()] * 3,
        compiler_params=params(62),
        cost_estimate=pl.CostEstimate(flops=1 << 20, bytes_accessed=3 << 20, transcendentals=0),
        name="weights",
    )(taps, conv_bias, output_weight, output_bias)
    low, up = pl.pallas_call(
        merge_kernel,
        out_shape=[lines] * 2,
        in_specs=[anywhere] * 5,
        out_specs=[vmem()] * 2,
        scratch_shapes=[
            pltpu.VMEM((TILES, 8, BAND, LANE), f32),
            pltpu.VMEM((41, STRIP, LANE), f32),
            pltpu.VMEM((41, STRIP, LANE), f32),
            pltpu.SemaphoreType.DMA((5,)),
        ],
        compiler_params=params(62),
        cost_estimate=pl.CostEstimate(flops=1 << 20, bytes_accessed=9 << 20, transcendentals=0),
        name="merge",
    )(u, evc, evm, odc, odm)
    return pl.pallas_call(
        denoise_kernel,
        out_shape=sds(8, 128, 512),
        in_specs=[anywhere] * 4 + [vmem()] * 3,
        out_specs=anywhere,
        scratch_shapes=[
            pltpu.VMEM((TILES, 4 * ROWS_KEPT, LANE), f32),
            pltpu.VMEM((TILES, 4 * ROWS_KEPT, LANE), f32),
            pltpu.VMEM((3, 3, 4 * ROWS_KEPT, 640), bf16),
            pltpu.VMEM((3, 3, 4 * ROWS_KEPT, 640), bf16),
            pltpu.VMEM((2, 256, 640), f32),
            pltpu.VMEM((9, STRIP, LANE), f32),
            pltpu.VMEM((9, STRIP, LANE), f32),
            pltpu.VMEM((8, 128, 512), f32),
            pltpu.SemaphoreType.DMA((6,)),
        ],
        compiler_params=params(62),
        name="denoise",
    )(low, up, ce, co, conv_parts, map_parts, out_bias)


def per_device(
    object_field,
    probe_field,
    propagator_phase,
    position_rows,
    position_cols,
    tile_counts,
    intensities,
    conv_weight,
    conv_bias,
    output_weight,
    output_bias,
):
    rows = lax.axis_size("row")
    cols = lax.axis_size("col")

    def pairs(count, start):
        found = []
        for i in range(start, count - 1, 2):
            found += [(i, i + 1), (i + 1, i)]
        return found

    def row_ev(x):
        return lax.ppermute(x, "row", pairs(rows, 0))

    def row_od(x):
        return lax.ppermute(x, "row", pairs(rows, 1))

    def col_ev(x):
        return lax.ppermute(x, "col", pairs(cols, 0))

    def col_od(x):
        return lax.ppermute(x, "col", pairs(cols, 1))

    obj = object_field.reshape(8, 128, 512)
    def edge(index):
        return pl.BlockSpec((8, 128, LANE), lambda i: (0, 0, index))

    def whole(*shape):
        return pl.BlockSpec(shape, lambda i: (0,) * len(shape))

    ce, co = pl.pallas_call(
        pack_kernel,
        out_shape=[sds(8, HALF, LANE)] * 2,
        grid=(1,),
        in_specs=[edge(0), edge(3)],
        out_specs=[whole(8, HALF, LANE)] * 2,
        compiler_params=params(62),
        name="pack",
    )(obj, obj)
    ce = col_ev(ce)
    co = col_od(co)
    anywhere = pl.BlockSpec(memory_space=pl.ANY)
    strip = sds(TILES, 8, HALF, LANE)
    ev, od = pl.pallas_call(
        strips_kernel,
        out_shape=[strip] * 2,
        in_specs=[vmem()],
        out_specs=[vmem()] * 2,
        compiler_params=params(62),
        cost_estimate=pl.CostEstimate(flops=0, bytes_accessed=4 << 20, transcendentals=0),
        name="strips",
    )(obj)
    comb, ev, od = pl.pallas_call(
        comb_kernel,
        out_shape=[sds(8, 128, LANE), strip, strip],
        in_specs=[anywhere] * 4,
        out_specs=[anywhere] * 3,
        scratch_shapes=[
            pltpu.VMEM((8, 128, LANE), f32),
            pltpu.VMEM((8, HALF, LANE), f32),
            pltpu.VMEM((8, HALF, LANE), f32),
            pltpu.SemaphoreType.DMA((5,)),
        ],
        input_output_aliases={2: 1, 3: 2},
        compiler_params=params(62),
        name="comb",
    )(ce, co, ev, od)
    od = row_od(od)
    ev = row_ev(ev)
    phase_re = jnp.cos(propagator_phase)
    phase_im = jnp.sin(propagator_phase)
    tables = [jnp.asarray(m) for m in dft_matrices()]
    u, evc, evm, odc, odm, own = slots_call(
        position_rows.reshape(-1),
        position_cols.reshape(-1),
        tile_counts.reshape(-1),
        obj,
        comb,
        ev,
        od,
        intensities.reshape(4, LANE, LANE),
        probe_field,
        phase_re,
        phase_im,
        *tables,
    )
    odc = row_od(odc)
    odm, odc = lax.optimization_barrier((odm, odc))
    odm = row_od(odm)
    evc = row_ev(evc)
    evm = row_ev(evm)
    ce, co = pl.pallas_call(
        sides_kernel,
        out_shape=[sds(9, STRIP, LANE)] * 2,
        in_specs=[anywhere] * 3,
        out_specs=[vmem()] * 2,
        scratch_shapes=[
            pltpu.VMEM((9, BAND, LANE), f32),
            pltpu.VMEM((9, STRIP, LANE), f32),
            pltpu.VMEM((9, STRIP, LANE), f32),
            pltpu.SemaphoreType.DMA((3,)),
        ],
        compiler_params=params(62),
        name="sides",
    )(own, evc, odc)
    ce = col_ev(ce)
    co = col_od(co)
    taps = conv_weight.reshape(3, 3, 3, 32, 4).transpose(0, 1, 3, 2, 4).reshape(3, 3, 32, 12)
    out = denoise_call(u, evc, evm, odc, odm, ce, co, taps, conv_bias, output_weight, output_bias)
    return out.reshape(4, 2, 128, 512)


def solution(mesh):
    placed = (
        P(None, None, "row", "col"),
        P(),
        P(),
        P("row", "col", None),
        P("row", "col", None),
        P("row", "col"),
        P("row", "col", None, None, None),
        P(),
        P(),
        P(),
        P(),
    )
    return jax.shard_map(
        per_device,
        mesh=mesh,
        in_specs=placed,
        out_specs=P(None, None, "row", "col"),
        check_vma=False,
    )
```
